128 devices in a mesh: dp: 32 (over y, z, core), expert: 4 (over x).
Axes of the slice: x: 4, y: 4, z: 4, core: 2. Of those that a mesh axis runs over, the one named last changes fastest.
Arguments:
- tokens: bfloat16 [16384, 768], P(('dp', 'expert')), may hold values from -6 to 6
- norm_attn: bfloat16 [768], P('dp'), may hold values from 0.5 to 1.5
- w_qkv: bfloat16 [768, 2304], P('dp'), may hold values from -0.09375 to 0.09375
- w_attn_out: bfloat16 [768, 768], P('dp'), may hold values from -1.75 to 1.75
- bias_table: bfloat16 [32, 12], P('dp'), may hold values from -4 to 4
- norm_moe: bfloat16 [768], P('dp'), may hold values from 0.5 to 1.5
- router: bfloat16 [768, 4], P('dp'), may hold values from -0.15625 to 0.15625
- w_in: bfloat16 [768, 4, 3072], P('dp', 'expert'), may hold values from -0.21875 to 0.21875
- w_out: bfloat16 [3072, 4, 768], P('dp', 'expert'), may hold values from -0.4375 to 0.4375
- routes: int32 [16384, 1], P(('dp', 'expert')), may hold values from 0 to 3; in each aligned block of 128 rows (0 to 127, 128 to 255, ...) at most 40 rows name the same one
- buckets: int32 [1023], replicated, may hold values from 0 to 31, as said below
- cotangent: bfloat16 [16384, 768], P(('dp', 'expert')), may hold values from -6 to 6
Outputs:
- mixed: bfloat16 [16384, 768], P(('dp', 'expert'))
- d_tokens: bfloat16 [16384, 768], P(('dp', 'expert'))
- g_norm_attn: float32 [768], P('dp')
- g_w_qkv: float32 [768, 2304], P('dp')
- g_w_attn_out: float32 [768, 768], P('dp')
- g_bias_table: float32 [32, 12], P('dp')
- g_norm_moe: float32 [768], P('dp')
- g_router: float32 [768, 4], P('dp')
- g_w_in: float32 [768, 4, 3072], P('dp', 'expert')
- g_w_out: float32 [3072, 4, 768], P('dp', 'expert')
The draws below stay inside these ranges and needn't reach their ends.
Inputs may be any that keep to these rules, and one draw needn't show every extreme that they name: `routes`: in each device's rows (aligned blocks of 128 tokens) no expert is named by more than 40 tokens; some expert is named by exactly 40 in some block. Entry r is the bucket of the key-minus-query distance r - 511: 0 at distance 0, buckets below 16 for keys before the query and the others for keys after it, never falling with the distance's size on either side.
All inputs are finite; a program needn't handle non-finite values.
Results may differ from the reference program's by a relative error of at most 0.028.
Values may be sent and summed in bfloat16 or wider, within the bound.
A program may use at most 128 MiB of HBM per device.

```python
import math
import jax
import jax.numpy as jnp
import numpy as np
from jax import lax

D = 768
HEADS = 12
HD = 64
FF = 3072
BUCKETS = 32
TOK_DEV = 128
EXPERTS = 4
LEN = 512
TOKENS = 16384
CAP = 40


def draw_buckets(key, part):
    key = jax.random.fold_in(key, 11)
    half_count = BUCKETS // 2
    exact_count = half_count // 2
    distance = jnp.arange(1, LEN, dtype=jnp.int32)
    raw_bits = jax.random.randint(key, (2, LEN - 1), 0, 1 << 20, dtype=jnp.int32)
    rises = jnp.where(distance[None, :] < exact_count, 1, (raw_bits % distance[None, :] < exact_count).astype(jnp.int32))
    levels = jnp.minimum(jnp.cumsum(rises, axis=1), half_count - 1)
    levels = levels.at[:, LEN - 2].set(half_count - 1)
    before = levels[0, ::-1]
    after = levels[1] + half_count
    return jnp.concatenate([before, jnp.zeros((1,), jnp.int32), after]).astype(jnp.int32)


def block_levels(rng, dims, pieces, least, largest):
    level, own = 1.0, jax.random.fold_in(rng, 6)
    for dim, blocks in pieces:
        draws = jnp.exp(jax.random.uniform(jax.random.fold_in(own, dim), (blocks,), jnp.float32, least / len(pieces), largest / len(pieces)))
        level = level * jnp.repeat(draws, dims[dim] // blocks).reshape([-1 if axis == dim else 1 for axis in range(len(dims))])
    return level


def shared_out(stream_key, own, number, rows, count, top, most, skew):
    order = jax.random.permutation(stream_key, count)
    heavy_load, ordinary = load_shares(count, rows * top, most, skew, True), load_shares(count, rows * top, most, skew, False)
    places = jnp.arange(count)

    def named(tallies, rotation):
        used = int((tallies > 0).sum())
        fixed = max(1, used // 4)
        passed = fixed + (places - fixed + rotation * (used - fixed)) % max(1, count - fixed)
        return jnp.zeros((count,), jnp.int32).at[order[jnp.where(places < fixed, places, passed)]].set(jnp.asarray(tallies, jnp.int32))

    tallies = jnp.where(number % 4 == 0, named(heavy_load, number // 4), named(ordinary, number - number // 4 - 1))
    mixed = jax.random.permutation(jax.random.fold_in(own, 3), count)
    source_of, taker = mixed[0:count // 2 * 2:2], mixed[1:count // 2 * 2:2]
    room = jnp.minimum(tallies[source_of] - 1, most - tallies[taker]) // 2
    room = jnp.where((source_of == order[0]) | (taker == order[0]) | (tallies[taker] == 0), 0, jnp.maximum(room, 0))
    passed = jax.random.randint(jax.random.fold_in(own, 4), (count // 2,), 0, 1 << 20) % (room + 1)
    tallies = tallies.at[source_of].add(-passed).at[taker].add(passed)
    members = jnp.searchsorted(jnp.cumsum(tallies), jnp.arange(rows * top), side="right").astype(jnp.int32)
    grid = members.reshape(top, rows).T
    grid = grid[jax.random.permutation(jax.random.fold_in(own, 1), rows)]
    rotation = jax.random.randint(jax.random.fold_in(own, 2), (rows, 1), 0, top)
    return jnp.take_along_axis(grid, (jnp.arange(top)[None, :] + rotation) % top, axis=1)


def load_shares(number_of, total, reach, lean, full):
    weights = [(1 << 20) // math.isqrt(grade ** lean) + 1 for grade in range(1, number_of + 1)]
    largest = reach if full else min(reach, max(-(-total // number_of), total * weights[0] // sum(weights)))
    least = 1 if total - largest >= number_of - 1 else 0
    counts, spare = [largest] + [least] * (number_of - 1), total - largest - least * (number_of - 1)
    while spare > 0:
        movable = [i for i in range(1, number_of) if counts[i] < largest] or [i for i in range(1, number_of) if counts[i] < reach]
        mass, budget = sum([weights[i] for i in movable]), spare
        for i in movable:
            extra = min(reach - counts[i], max(1, budget * weights[i] // mass), spare)
            counts[i] = counts[i] + extra
            spare = spare - extra
    return np.array(counts)


def noise(rng, extent, width, bound, cuts=(), held_as=jnp.bfloat16):
    result = jax.random.normal(rng, extent, jnp.float32) * width
    if len(cuts) > 0:
        result = block_levels(rng, extent, cuts, -0.22, 0.18) * result
    return jnp.clip(result, min=-bound, max=bound).astype(held_as)


def setup_inputs(seed: int = 0) -> dict:
    streams_of = jax.random.split(jax.random.key(seed), 13)
    tokens = noise(streams_of[0], (TOKENS, D), 1.0, 6.0, ((0, 128),))
    norm_attn = jnp.clip(1.0 + 0.1 * jax.random.normal(streams_of[1], (D,), jnp.float32), 0.5, 1.5).astype(jnp.bfloat16)
    w_qkv = noise(streams_of[2], (D, 3 * D), (5 * D) ** -0.5, 0.09375, ((0, 32),))
    w_attn_out = noise(streams_of[3], (D, D), (D // 64) ** -0.5, 1.75, ((0, 32),))
    bias_table = noise(streams_of[4], (BUCKETS, HEADS), 1.0, 4.0, ((0, 32),))
    norm_moe = jnp.clip(1.0 + 0.1 * jax.random.normal(streams_of[5], (D,), jnp.float32), 0.5, 1.5).astype(jnp.bfloat16)
    router = noise(streams_of[6], (D, EXPERTS), (2 * D) ** -0.5, 0.15625, ((0, 32),))
    w_in = noise(streams_of[7], (D, EXPERTS, FF), D ** -0.5, 0.21875, ((0, 32), (1, 4)))
    w_out = noise(streams_of[8], (FF, EXPERTS, D), (FF // 16) ** -0.5, 0.4375, ((0, 32), (1, 4)))
    routes_keys = jax.random.split(jax.random.fold_in(streams_of[9], 1), TOKENS // TOK_DEV)
    routes_turns = jax.random.permutation(jax.random.fold_in(streams_of[9], 3), TOKENS // TOK_DEV)
    routes = jax.vmap(lambda own, number: shared_out(jax.random.fold_in(streams_of[9], 2), own, number, TOK_DEV, EXPERTS, 1, CAP, 2))(routes_keys, routes_turns).reshape((TOKENS, 1))
    buckets = draw_buckets(jax.random.fold_in(streams_of[12], 71), 0)
    cotangent = noise(streams_of[11], (TOKENS, D), 1.0, 6.0, ((0, 128),))
    return dict(tokens=tokens, norm_attn=norm_attn, w_qkv=w_qkv, w_attn_out=w_attn_out, bias_table=bias_table, norm_moe=norm_moe, router=router, w_in=w_in, w_out=w_out, routes=routes, buckets=buckets, cotangent=cotangent)


@jax.custom_vjp
def low(v):
    return lax.optimization_barrier(v.astype(jnp.bfloat16)).astype(jnp.float32)

@jax.custom_vjp
def low_back(v):
    return v

def low_keep(v):
    return (low(v), None)

def low_pass(kept, grad):
    return (grad,)

def back_keep(v):
    return (v, None)

def back_low(kept, grad):
    return (low(grad),)
low.defvjp(low_keep, low_pass)
low_back.defvjp(back_keep, back_low)

def rms_norm(values, gain_vec):
    return values * lax.rsqrt(lax.optimization_barrier(jnp.mean(values * values, -1, keepdims=True)) + 1e-06) * gain_vec

def attend(sequence, bias_full):
    highest = lax.Precision.HIGHEST
    queries = sequence[:, 0]
    key_rows = sequence[:, 1]
    value_rows = sequence[:, 2]
    scores = low_back(jnp.einsum('qhd,khd->hqk', queries, key_rows, precision=highest)) + bias_full
    probability = jax.nn.softmax(scores, axis=-1)
    return jnp.einsum('hqk,khd->qhd', low(probability), value_rows, precision=highest).reshape(LEN, D)

def expert_apply(inputs, first, second):
    highest = lax.Precision.HIGHEST
    hidden = low_back(jnp.dot(inputs, first, precision=highest))
    activated = low(jax.nn.gelu(hidden))
    return low(low_back(jnp.dot(activated, second, precision=highest)))

def reference(tokens, norm_attn, w_qkv, w_attn_out, bias_table, norm_moe, router, w_in, w_out, routes, buckets, cotangent):
    highest = lax.Precision.HIGHEST
    rows_all = tokens.shape[0]
    blocks = rows_all // TOK_DEV
    routed = routes[:, 0].astype(jnp.int32)
    chosen_int = (routed[:, None] == jnp.arange(EXPERTS, dtype=jnp.int32)[None, :]).astype(jnp.int32)
    per_block = chosen_int.reshape(blocks, TOK_DEV, EXPERTS)
    slot_id = lax.optimization_barrier(jnp.sum((jnp.cumsum(per_block, 1) - 1) * per_block, -1)).reshape(-1)
    block_id = jnp.arange(rows_all, dtype=jnp.int32) // TOK_DEV
    places = ((block_id * EXPERTS + routed) * CAP + slot_id).astype(jnp.int32)
    chosen = chosen_int.astype(jnp.float32)
    position = jnp.arange(LEN, dtype=jnp.int32)
    relative = position[None, :] - position[:, None] + LEN - 1
    bucket = buckets[relative]

    def forward(resid_in, gain_one, qkv_weight, out_weight, table, gain_two, router_weight, in_weight, out_expert):
        normed_low = low(rms_norm(resid_in, gain_one))
        projected = low(low_back(jnp.dot(normed_low, qkv_weight, precision=highest)))
        bias_full = jnp.transpose(table[bucket], (2, 0, 1))
        sequences = projected.reshape(rows_all // LEN, LEN, 3, HEADS, HD)
        step = jax.checkpoint(attend)
        heads_out = lax.map(lambda sequence: step(sequence, bias_full), sequences).reshape(rows_all, D)
        mixed_heads = low(low_back(heads_out))
        after_attn = resid_in + low_back(jnp.dot(mixed_heads, out_weight, precision=highest))
        moe_input = low(rms_norm(after_attn, gain_two))
        probability = jax.nn.softmax(jnp.dot(moe_input, router_weight, precision=highest), axis=-1)
        gate_value = lax.optimization_barrier(jnp.sum(probability * chosen, -1))
        sent_input = low_back(moe_input)
        buffer = jnp.zeros((blocks * EXPERTS * CAP, D), jnp.float32).at[places].set(sent_input)
        per_expert = buffer.reshape(blocks, EXPERTS, CAP, D).transpose(1, 0, 2, 3).reshape(EXPERTS, blocks * CAP, D)
        expert_step = jax.checkpoint(expert_apply)
        results = lax.map(lambda triple: expert_step(*triple), (per_expert, in_weight.transpose(1, 0, 2), out_expert.transpose(1, 0, 2)))
        returned = results.reshape(EXPERTS, blocks, CAP, D).transpose(1, 0, 2, 3).reshape(-1, D)
        return after_attn + gate_value[:, None] * returned[places]
    inputs = tuple((value.astype(jnp.float32) for value in (tokens, norm_attn, w_qkv, w_attn_out, bias_table, norm_moe, router, w_in, w_out)))
    mixed, backward = jax.vjp(forward, *inputs)
    grads = backward(cotangent.astype(jnp.float32))
    return (mixed.astype(jnp.bfloat16), grads[0].astype(jnp.bfloat16), grads[1], grads[2], grads[3], grads[4], grads[5], grads[6], grads[7], grads[8])
```

```python
import jax
import jax.numpy as jnp
from jax import lax
from jax.experimental import pallas as pl
from jax.experimental.pallas import tpu as pltpu
from jax.sharding import PartitionSpec as P

epsilon = 1e-06
highest = lax.Precision.HIGHEST
bf16 = jnp.bfloat16
f32 = jnp.float32
NT = (((1,), (1,)), ((), ()))
TN = (((0,), (0,)), ((), ()))


def mm(a, b):
    return jnp.dot(a, b, preferred_element_type=f32)


def mm_nt(a, b):
    return lax.dot_general(a, b, NT, preferred_element_type=f32)


def mm_tn(a, b):
    return lax.dot_general(a, b, TN, preferred_element_type=f32)


def stack_heads(pair):
    left = lax.broadcasted_iota(jnp.int32, pair.shape, 1) < 64
    zero = jnp.zeros_like(pair)
    return jnp.concatenate([jnp.where(left, pair, zero), jnp.where(left, zero, pair)], 0)


def join_pair(stacked):
    rows = stacked.shape[0] // 2
    left = lax.broadcasted_iota(jnp.int32, (rows, 128), 1) < 64
    return jnp.where(left, stacked[:rows], stacked[rows:])


def toeplitz(window_row, rows, keys):
    width = window_row.shape[1]
    wide = jnp.broadcast_to(window_row, (rows, width))
    rolled = pltpu.roll(wide, width - (rows - 1), 1, stride=1, stride_axis=0)
    return rolled[:, :keys]


def diagonal_sums(block, width):
    rows, keys = block.shape
    wide = jnp.concatenate([block, jnp.zeros((rows, width - keys), f32)], 1)
    half = rows // 2
    while half >= 8:
        wide = wide[:half] + pltpu.roll(wide[half:], width - half, 1)
        half //= 2
    row = lax.broadcasted_iota(jnp.int32, wide.shape, 0)
    for bit in (1, 2, 4):
        wide = jnp.where((row & bit) != 0, pltpu.roll(wide, width - bit, 1), wide)
    total = jnp.sum(wide, 0, keepdims=True)
    return pltpu.roll(total, rows - 1, 1)


def attention_forward(query, key, value, window, out, weights):
    pair = pl.program_id(0)
    rows = query.shape[0]
    keys = key.shape[0]
    bias = jnp.concatenate(
        [toeplitz(window[pl.ds(2 * pair + j, 1), :], rows, keys) for j in (0, 1)], 0
    )
    scores = mm_nt(stack_heads(query[...]), key[...]) + bias
    top = jnp.max(scores, -1, keepdims=True)
    raised = jnp.exp(scores - top)
    probability = raised / jnp.sum(raised, -1, keepdims=True)
    weights[...] = probability.reshape(2, rows, keys)
    out[...] = join_pair(mm(probability.astype(bf16), value[...])).astype(bf16)


def attention_backward(query, key, value, weights, d_out, d_query, d_key, d_value, d_window):
    rows = query.shape[0]
    keys = key.shape[0]
    probability = weights[...].reshape(2 * rows, keys)
    d_stack = stack_heads(d_out[...])
    d_weights = mm_nt(d_stack, value[...])
    d_value[...] = mm_tn(probability.astype(bf16), d_stack).astype(bf16)
    d_scores = probability * (
        d_weights - jnp.sum(probability * d_weights, -1, keepdims=True)
    )
    for j in (0, 1):
        d_window[0, j : j + 1, :] = diagonal_sums(
            d_scores[j * rows : (j + 1) * rows], d_window.shape[2]
        )
    low = d_scores.astype(bf16)
    d_query[...] = join_pair(mm(low, key[...])).astype(bf16)
    d_key[...] = mm_tn(low, stack_heads(query[...])).astype(bf16)


def rms_forward(values, gain):
    r = lax.rsqrt(jnp.mean(values * values, -1, keepdims=True) + epsilon)
    return r, values * r * gain


def rms_backward(values, r, gain, grad):
    u = grad * gain
    d_values = r * u - values * (r * r * r) * jnp.mean(u * values, -1, keepdims=True)
    return d_values, jnp.sum(grad * values * r, 0)


MESH = pl.DeviceIdType.MESH


class Place:
    def __init__(self):
        d = lax.axis_index("dp")
        self.d = d
        self.x = lax.axis_index("expert")
        self.c = lax.rem(d, 2)
        self.z = lax.rem(lax.div(d, 2), 4)
        self.y = lax.div(d, 8)
        self.p = self.z * (1 - self.c) + self.y * self.c
        self.q = self.y * (1 - self.c) + self.z * self.c

    def at(self, p, q):
        y = q * (1 - self.c) + p * self.c
        z = p * (1 - self.c) + q * self.c
        return ((y * 4 + z) * 2 + self.c, self.x)

    def along_p(self, by):
        return self.at(lax.rem(self.p + by, 4), self.q)

    def along_q(self, by):
        return self.at(self.p, lax.rem(self.q + by, 4))

    def along_x(self, by):
        return (self.d, lax.rem(self.x + by, 4))

    def sibling(self):
        return (self.d + 1 - 2 * self.c, self.x)

    def each_core(self, body):
        pl.when(self.c == 0)(lambda: body(0))
        pl.when(self.c == 1)(lambda: body(1))

    def barrier(self, with_x):
        peers = [self.sibling()] + [self.along_p(i) for i in (1, 2, 3)]
        peers += [self.along_q(i) for i in (1, 2, 3)]
        if with_x:
            peers += [self.along_x(i) for i in (1, 2, 3)]
        sem = pltpu.get_barrier_semaphore()
        for peer in peers:
            pl.semaphore_signal(sem, inc=1, device_id=peer, device_id_type=MESH)
        pl.semaphore_wait(sem, len(peers))


def remote(src, dst, send, recv, to):
    return pltpu.make_async_remote_copy(
        src_ref=src, dst_ref=dst, send_sem=send, recv_sem=recv, device_id=to, device_id_type=MESH
    )


def block_of(ref, tall, k, p, q):
    y, z = (q, p) if k == 0 else (p, q)
    return ref.at[y, z, k] if tall else ref.at[k, y, z]


def slab_of(ref, tall, k, q, low=0, count=4):
    y, z = (q, pl.ds(low, count)) if k == 0 else (pl.ds(low, count), q)
    return ref.at[y, z, k] if tall else ref.at[k, y, z]


class Gather:
    sends = 11
    recvs = 11

    def __init__(self, place, ref, tall, send, recv, number):
        self.o, self.ref, self.tall, self.send, self.recv = place, ref, tall, send, recv
        self.number = number

    def block(self, k, by):
        return block_of(self.ref, self.tall, k, lax.rem(self.o.p + by, 4), self.o.q)

    def slab(self, k, by, low=0, count=4):
        return slab_of(self.ref, self.tall, k, lax.rem(self.o.q + by, 4), low, count)

    def go(self, part, s, r, to):
        def body(k):
            src = part(k)
            remote(src, src, self.send.at[s], self.recv.at[r], to).start()

        self.o.each_core(body)

    def arrived(self, r, count):
        if count == 1:
            view = block_of(self.ref, self.tall, 0, 0, 0)
        else:
            view = slab_of(self.ref, self.tall, 0, 0, 0, count)
        remote(view, view, self.send.at[0], self.recv.at[r], self.o.sibling()).wait_recv()

    def sent(self, s, count):
        if count == 1:
            view = block_of(self.ref, self.tall, 0, 0, 0)
        else:
            view = slab_of(self.ref, self.tall, 0, 0, 0, count)
        remote(view, view, self.send.at[s], self.recv.at[0], self.o.sibling()).wait_send()

    def ring_one(self):
        self.go(lambda k: self.block(k, 0), 0, 0, self.o.along_p(1))
        self.go(lambda k: self.block(k, 0), 1, 1, self.o.along_p(3))

    def ring_one_far(self):
        self.arrived(0, 1)
        self.arrived(1, 1)
        if self.number % 2 == 0:
            self.go(lambda k: self.block(k, 3), 2, 2, self.o.along_p(1))
        else:
            self.go(lambda k: self.block(k, 1), 2, 2, self.o.along_p(3))

    def ring_two(self):
        self.arrived(2, 1)
        self.go(lambda k: self.slab(k, 0), 3, 3, self.o.along_q(1))
        self.go(lambda k: self.slab(k, 0), 4, 4, self.o.along_q(3))
        self.go(lambda k: self.slab(k, 0), 7, 7, self.o.sibling())

    def ring_two_far(self):
        self.arrived(3, 4)
        self.go(lambda k: self.slab(k, 3, 0, 2), 5, 5, self.o.along_q(1))
        self.arrived(4, 4)
        self.go(lambda k: self.slab(k, 1, 2, 2), 6, 6, self.o.along_q(3))
        self.go(lambda k: self.slab(k, 3), 8, 8, self.o.sibling())
        self.go(lambda k: self.slab(k, 1), 9, 9, self.o.sibling())

    def last(self):
        self.arrived(5, 2)
        self.arrived(6, 2)
        self.go(lambda k: self.slab(k, 2), 10, 10, self.o.sibling())

    def finish(self):
        for r in (7, 8, 9, 10):
            self.arrived(r, 4)

    def drain(self):
        for s, count in ((0, 1), (1, 1), (2, 1), (3, 4), (4, 4), (5, 2), (6, 2), (7, 4), (8, 4), (9, 4), (10, 4)):
            self.sent(s, count)


class SmallSum:
    def __init__(self, place, value, arrivals, send, recv, with_x):
        self.o, self.value, self.arrivals, self.send, self.recv = place, value, arrivals, send, recv
        o = place
        self.steps = [[o.sibling()], [o.along_p(i) for i in (1, 2, 3)], [o.along_q(i) for i in (1, 2, 3)]]
        if with_x:
            self.steps.append([o.along_x(i) for i in (1, 2, 3)])
        self.copies = []
        n = 0
        for s, peers in enumerate(self.steps):
            row = []
            for peer in peers:
                row.append(
                    remote(value.at[s], arrivals.at[n], send.at[n], recv.at[n], peer)
                )
                n += 1
            self.copies.append(row)

    def start(self, s):
        for copy in self.copies[s]:
            copy.start()

    def add(self, s):
        first = sum(len(row) for row in self.copies[:s])
        total = self.value[s]
        for i, copy in enumerate(self.copies[s]):
            copy.wait_recv()
            total = total + self.arrivals[first + i]
        self.value[s + 1] = total

    def drain(self):
        for row in self.copies:
            for copy in row:
                copy.wait_send()


def place_small(o, pack):
    row = lax.broadcasted_iota(jnp.int32, (32, 1024), 0)
    lane = lax.broadcasted_iota(jnp.int32, (32, 1024), 1)
    target = jnp.where(row < 24, 24 * o.d + row, jnp.where(row == 24, 768 + o.d, -1))
    hit = jnp.where(lane == target, 1.0, 0.0)
    spread = mm_tn(pack[...].astype(bf16), hit.astype(bf16))
    return jnp.concatenate(
        [spread[0:8, :768], spread[8:16, 768:896], spread[16:24, 768:896]], 1
    )


def meet(o, halves, stage, other, sem):
    at = 0
    for ref in halves:
        n = ref.shape[1] // 2
        own = pl.ds(pl.multiple_of(o.c * n, 128), n)
        theirs = pl.ds(pl.multiple_of((1 - o.c) * n, 128), n)
        stage[pl.ds(pl.multiple_of(24 * o.c, 8), 24), at : at + n] = ref[:, own].astype(f32)
        other[:, at : at + n] = ref[:, theirs].astype(f32)
        at += n
    return remote(
        other, stage.at[pl.ds(pl.multiple_of(24 * o.c, 8), 24)], sem.at[0], sem.at[1], o.sibling()
    )


def gather_kernel(
    w_qkv, w_ao, w_in, w_out, pack, g_qkv, g_ao, g_in, g_out, small,
    stage, other, pair_sem, sends, recvs, arrivals, small_send, small_recv,
):
    o = Place()
    o.barrier(False)
    flows = [
        Gather(o, ref, tall, sends.at[i], recvs.at[i], i)
        for i, (ref, tall) in enumerate(((g_qkv, 0), (g_ao, 0), (g_in, 0), (g_out, 1)))
    ]
    qkv, ao, win, wout = flows
    pair = meet(o, (w_qkv, w_ao, w_in), stage, other, pair_sem)
    pair.start()
    tot = SmallSum(o, small, arrivals, small_send, small_recv, False)
    small[0] = place_small(o, pack)
    tot.start(0)
    g_out[o.y, o.z, o.c] = w_out[...]
    pair.wait_recv()
    at = 0
    for ref in (g_qkv, g_ao, g_in):
        n = ref.shape[-1]
        ref[o.c, o.y, o.z] = stage[:, at : at + n].astype(bf16)
        at += n
    qkv.ring_one()
    tot.add(0)
    tot.start(1)
    qkv.ring_one_far()
    qkv.ring_two()
    for f in (ao, win, wout):
        f.ring_one()
    tot.add(1)
    tot.start(2)
    for f in (ao, win, wout):
        f.ring_one_far()
    qkv.ring_two_far()
    for f in (ao, win, wout):
        f.ring_two()
    tot.add(2)
    qkv.last()
    ao.ring_two_far()
    qkv.finish()
    ao.last()
    win.ring_two_far()
    ao.finish()
    win.last()
    wout.ring_two_far()
    win.finish()
    wout.last()
    wout.finish()
    pair.wait_send()
    tot.drain()
    for f in flows:
        f.drain()


def gather_all(w_qkv, w_ao, w_in, w_out, pack):
    vm = pl.BlockSpec(memory_space=pltpu.VMEM)
    return pl.pallas_call(
        gather_kernel,
        in_specs=[vm] * 5,
        out_specs=[vm] * 5,
        out_shape=[
            jax.ShapeDtypeStruct((2, 4, 4, 48, 1152), bf16),
            jax.ShapeDtypeStruct((2, 4, 4, 48, 384), bf16),
            jax.ShapeDtypeStruct((2, 4, 4, 48, 1536), bf16),
            jax.ShapeDtypeStruct((4, 4, 2, 96, 768), bf16),
            jax.ShapeDtypeStruct((4, 8, 1024), f32),
        ],
        scratch_shapes=[
            pltpu.VMEM((48, 3072), f32),
            pltpu.VMEM((24, 3072), f32),
            pltpu.SemaphoreType.DMA((2,)),
            pltpu.SemaphoreType.DMA((4, 11)),
            pltpu.SemaphoreType.DMA((4, 11)),
            pltpu.VMEM((7, 8, 1024), f32),
            pltpu.SemaphoreType.DMA((7,)),
            pltpu.SemaphoreType.DMA((7,)),
        ],
        compiler_params=pltpu.CompilerParams(
            collective_id=0, has_side_effects=True, vmem_limit_bytes=48 * 2**20
        ),
    )(w_qkv, w_ao, w_in, w_out, pack)


def per_device(
    tokens, norm_attn, w_qkv, w_attn_out, bias_table, norm_moe, router, w_in, w_out, routes, buckets, cotangent
):
    rows, width = tokens.shape
    dp = lax.axis_index("dp")
    ex = lax.axis_index("expert")
    groups = 4
    keys = rows * groups
    heads = 12
    window_width = keys + rows

    own = norm_attn.shape[0]
    pack = jnp.concatenate([norm_attn[:, None], norm_moe[:, None], router, jnp.zeros((own, 122), bf16)], 1)
    last = jnp.concatenate([jnp.zeros((1, 8), bf16), bias_table, jnp.zeros((1, 108), bf16)], 1)
    pack = jnp.concatenate([pack, last, jnp.zeros((7, 128), bf16)], 0).astype(f32)
    g_qkv, g_ao, g_in, g_out, small = gather_all(w_qkv, w_attn_out, w_in[:, 0], w_out[:, 0], pack)
    small = small[3]
    full_qkv = jnp.concatenate([g_qkv[0].reshape(768, -1), g_qkv[1].reshape(768, -1)], 1)
    full_out = jnp.concatenate([g_ao[0].reshape(768, -1), g_ao[1].reshape(768, -1)], 1)
    full_in = jnp.concatenate([g_in[0].reshape(768, -1), g_in[1].reshape(768, -1)], 1)
    full_outw = g_out.reshape(3072, 768)
    gain_one, gain_two, router_t = small[0:1, :768], small[1:2, :768], small[2:6, :768]
    table_full = jnp.concatenate([small[:8, 768:800], small[:4, 896:928]], 0)

    x = tokens.astype(f32)
    r_one, normed = rms_forward(x, gain_one)
    normed = normed.astype(bf16)
    projected = mm(normed, full_qkv).astype(bf16)
    query = projected[:, :768]
    kv = lax.all_gather(projected[:, 768:], "expert", axis=0, tiled=True)
    key, value = kv[:, :768], kv[:, 768:]
    padded = jnp.concatenate([buckets, jnp.zeros((1,), jnp.int32)])
    bucket_window = lax.dynamic_slice_in_dim(padded, (groups - 1 - ex) * rows, window_width, 0)
    picks = (bucket_window[None, :] == jnp.arange(32, dtype=jnp.int32)[:, None]).astype(f32)
    window = jnp.concatenate(
        [jnp.dot(table_full, picks, precision=highest), jnp.zeros((4, window_width), f32)], 0
    )

    pairs = heads // 2
    heads_out, weights = pl.pallas_call(
        attention_forward,
        grid=(pairs,),
        in_specs=[
            pl.BlockSpec((rows, 128), lambda p: (0, p)),
            pl.BlockSpec((keys, 128), lambda p: (0, p)),
            pl.BlockSpec((keys, 128), lambda p: (0, p)),
            pl.BlockSpec((16, window_width), lambda p: (0, 0)),
        ],
        out_specs=[
            pl.BlockSpec((rows, 128), lambda p: (0, p)),
            pl.BlockSpec((2, rows, keys), lambda p: (p, 0, 0)),
        ],
        out_shape=[
            jax.ShapeDtypeStruct((rows, width), bf16),
            jax.ShapeDtypeStruct((heads, rows, keys), f32),
        ],
        compiler_params=pltpu.CompilerParams(vmem_limit_bytes=32 * 2**20),
    )(query, key, value, window)

    after_attn = x + mm(heads_out, full_out)
    r_two, moe_input = rms_forward(after_attn, gain_two)
    moe_input = moe_input.astype(bf16)
    logits = jnp.dot(moe_input.astype(f32), router_t.T, precision=highest)
    probs = jax.nn.softmax(logits, -1)
    chosen_int = (routes == jnp.arange(4, dtype=jnp.int32)[None, :]).astype(jnp.int32)
    chosen = chosen_int.astype(f32)
    gate = jnp.sum(probs * chosen, -1, keepdims=True)
    slots = 48
    slot = jnp.sum((jnp.cumsum(chosen_int, 0) - 1) * chosen_int, -1)
    column = routes[:, 0] * slots + slot
    placing = (column[:, None] == jnp.arange(4 * slots, dtype=jnp.int32)[None, :]).astype(bf16)
    upstream = cotangent.astype(f32)
    d_combined = (gate * upstream).astype(bf16)
    outgoing = mm_tn(placing, jnp.concatenate([moe_input, d_combined], 1)).astype(bf16)
    incoming = lax.all_to_all(outgoing, "expert", split_axis=0, concat_axis=0, tiled=True)
    sent, d_result = incoming[:, :768], incoming[:, 768:]
    hidden = mm(sent, full_in)
    activated, gelu_back = jax.vjp(jax.nn.gelu, hidden)
    act_low = activated.astype(bf16)
    result = mm(act_low, full_outw).astype(bf16)
    d_act = mm_nt(d_result, full_outw)
    d_hidden = gelu_back(d_act)[0].astype(bf16)
    grad_w_out = mm_tn(act_low, d_result).astype(bf16)
    grad_w_in = mm_tn(sent, d_hidden).astype(bf16)
    out_in = lax.psum_scatter(grad_w_in, "dp", scatter_dimension=0, tiled=True)
    out_outw = lax.psum_scatter(grad_w_out, "dp", scatter_dimension=0, tiled=True)
    d_incoming = mm_nt(d_hidden, full_in).astype(bf16)
    back = lax.all_to_all(
        jnp.concatenate([result, d_incoming], 1), "expert", split_axis=0, concat_axis=0, tiled=True
    )
    returned = mm(placing, back)
    combined, d_moe = returned[:, :768], returned[:, 768:]
    mixed = (after_attn + gate * combined).astype(bf16)
    d_gate = jnp.sum(upstream * combined, -1, keepdims=True)
    d_logits = probs * (d_gate * chosen - d_gate * gate)
    grad_router = jnp.dot(d_logits.T, moe_input.astype(f32), precision=highest)
    d_moe = d_moe + jnp.dot(d_logits, router_t, precision=highest)
    d_after, grad_norm_two = rms_backward(after_attn, r_two, gain_two, d_moe)
    d_after = d_after + upstream
    d_attn = d_after.astype(bf16)
    grad_attn_out = mm_tn(heads_out, d_attn).astype(bf16)
    d_heads = mm_nt(d_attn, full_out).astype(bf16)

    d_query, d_key, d_value, d_window = pl.pallas_call(
        attention_backward,
        grid=(pairs,),
        in_specs=[
            pl.BlockSpec((rows, 128), lambda p: (0, p)),
            pl.BlockSpec((keys, 128), lambda p: (0, p)),
            pl.BlockSpec((keys, 128), lambda p: (0, p)),
            pl.BlockSpec((2, rows, keys), lambda p: (p, 0, 0)),
            pl.BlockSpec((rows, 128), lambda p: (0, p)),
        ],
        out_specs=[
            pl.BlockSpec((rows, 128), lambda p: (0, p)),
            pl.BlockSpec((keys, 128), lambda p: (0, p)),
            pl.BlockSpec((keys, 128), lambda p: (0, p)),
            pl.BlockSpec((1, 8, window_width), lambda p: (p, 0, 0)),
        ],
        out_shape=[
            jax.ShapeDtypeStruct((rows, width), bf16),
            jax.ShapeDtypeStruct((keys, width), bf16),
            jax.ShapeDtypeStruct((keys, width), bf16),
            jax.ShapeDtypeStruct((pairs, 8, window_width), f32),
        ],
        compiler_params=pltpu.CompilerParams(vmem_limit_bytes=32 * 2**20),
    )(query, key, value, weights, d_heads)
    d_window = d_window[:, :2].reshape(heads, window_width)
    grad_table_t = lax.dot_general(d_window, picks, NT, precision=highest)
    d_kv = jnp.concatenate([d_key, d_value], 1).reshape(groups, rows, 2 * width)
    d_kv = lax.all_to_all(d_kv, "expert", split_axis=0, concat_axis=0, tiled=True)
    d_kv = jnp.sum(d_kv.astype(f32), 0).astype(bf16)
    d_projected = jnp.concatenate([d_query, d_kv], 1)
    grad_qkv = mm_tn(normed, d_projected).astype(bf16)
    d_normed = mm_nt(d_projected, full_qkv)
    d_resid, grad_norm_one = rms_backward(x, r_one, gain_one, d_normed)
    d_tokens = (d_after + d_resid).astype(bf16)

    dense = lax.psum_scatter(
        jnp.concatenate([grad_qkv, grad_attn_out], 1), "dp", scatter_dimension=0, tiled=True
    )
    dense = lax.psum(dense.astype(bf16), "expert").astype(f32)
    small_grads = jnp.concatenate(
        [
            jnp.concatenate(
                [grad_norm_one[None], grad_norm_two[None], grad_router, jnp.zeros((2, 768), f32)], 0
            ),
            jnp.pad(grad_table_t[:8], ((0, 0), (0, 96))),
            jnp.pad(grad_table_t[8:], ((0, 4), (0, 96))),
        ],
        1,
    )
    small_grads = lax.psum(small_grads, ("dp", "expert"))
    mine = lax.dynamic_slice(small_grads, (0, dp * own), (8, own))
    table_col = jnp.concatenate(
        [
            lax.dynamic_slice(small_grads, (0, 768 + dp), (8, 1)),
            lax.dynamic_slice(small_grads, (0, 896 + dp), (4, 1)),
        ],
        0,
    )
    return (
        mixed,
        d_tokens,
        mine[0],
        dense[:, :2304],
        dense[:, 2304:],
        table_col.T,
        mine[1],
        mine[2:6].T,
        out_in.astype(f32)[:, None],
        out_outw.astype(f32)[:, None],
    )


def solution(mesh):
    both = ("dp", "expert")
    in_specs = (
        P(both, None), P("dp"), P("dp", None), P("dp", None), P("dp", None), P("dp"), P("dp", None),
        P("dp", "expert", None), P("dp", "expert", None), P(both, None), P(), P(both, None),
    )
    out_specs = (
        P(both, None), P(both, None), P("dp"), P("dp", None), P("dp", None), P("dp", None), P("dp"),
        P("dp", None), P("dp", "expert", None), P("dp", "expert", None),
    )
    return jax.shard_map(
        per_device, mesh=mesh, in_specs=in_specs, out_specs=out_specs, check_vma=False
    )
```

```python
import jax
import jax.numpy as jnp
from jax import lax
from jax.experimental import pallas as pl
from jax.experimental.pallas import tpu as pltpu
from jax.sharding import PartitionSpec as P

epsilon = 1e-06
highest = lax.Precision.HIGHEST
bf16 = jnp.bfloat16
f32 = jnp.float32
NT = (((1,), (1,)), ((), ()))
TN = (((0,), (0,)), ((), ()))


def mm(a, b):
    return jnp.dot(a, b, preferred_element_type=f32)


def mm_nt(a, b):
    return lax.dot_general(a, b, NT, preferred_element_type=f32)


def mm_tn(a, b):
    return lax.dot_general(a, b, TN, preferred_element_type=f32)


def stack_heads(pair):
    left = lax.broadcasted_iota(jnp.int32, pair.shape, 1) < 64
    zero = jnp.zeros_like(pair)
    return jnp.concatenate([jnp.where(left, pair, zero), jnp.where(left, zero, pair)], 0)


def join_pair(stacked):
    rows = stacked.shape[0] // 2
    left = lax.broadcasted_iota(jnp.int32, (rows, 128), 1) < 64
    return jnp.where(left, stacked[:rows], stacked[rows:])


def toeplitz(window_row, rows, keys):
    width = window_row.shape[1]
    wide = jnp.broadcast_to(window_row, (rows, width))
    rolled = pltpu.roll(wide, width - (rows - 1), 1, stride=1, stride_axis=0)
    return rolled[:, :keys]


def diagonal_sums(block, width):
    rows, keys = block.shape
    wide = jnp.concatenate([block, jnp.zeros((rows, width - keys), f32)], 1)
    half = rows // 2
    while half >= 8:
        wide = wide[:half] + pltpu.roll(wide[half:], width - half, 1)
        half //= 2
    row = lax.broadcasted_iota(jnp.int32, wide.shape, 0)
    for bit in (1, 2, 4):
        wide = jnp.where((row & bit) != 0, pltpu.roll(wide, width - bit, 1), wide)
    total = jnp.sum(wide, 0, keepdims=True)
    return pltpu.roll(total, rows - 1, 1)


def attention_forward(query, key, value, window, out, weights):
    pair = pl.program_id(0)
    rows = query.shape[0]
    keys = key.shape[0]
    bias = jnp.concatenate(
        [toeplitz(window[pl.ds(2 * pair + j, 1), :], rows, keys) for j in (0, 1)], 0
    )
    scores = mm_nt(stack_heads(query[...]), key[...]) + bias
    top = jnp.max(scores, -1, keepdims=True)
    raised = jnp.exp(scores - top)
    probability = raised / jnp.sum(raised, -1, keepdims=True)
    weights[...] = probability.reshape(2, rows, keys)
    out[...] = join_pair(mm(probability.astype(bf16), value[...])).astype(bf16)


def attention_backward(query, key, value, weights, d_out, d_query, d_key, d_value, d_window):
    rows = query.shape[0]
    keys = key.shape[0]
    probability = weights[...].reshape(2 * rows, keys)
    d_stack = stack_heads(d_out[...])
    d_weights = mm_nt(d_stack, value[...])
    d_value[...] = mm_tn(probability.astype(bf16), d_stack).astype(bf16)
    d_scores = probability * (
        d_weights - jnp.sum(probability * d_weights, -1, keepdims=True)
    )
    for j in (0, 1):
        d_window[0, j : j + 1, :] = diagonal_sums(
            d_scores[j * rows : (j + 1) * rows], d_window.shape[2]
        )
    low = d_scores.astype(bf16)
    d_query[...] = join_pair(mm(low, key[...])).astype(bf16)
    d_key[...] = mm_tn(low, stack_heads(query[...])).astype(bf16)


def rms_forward(values, gain):
    r = lax.rsqrt(jnp.mean(values * values, -1, keepdims=True) + epsilon)
    return r, values * r * gain


def rms_backward(values, r, gain, grad):
    u = grad * gain
    d_values = r * u - values * (r * r * r) * jnp.mean(u * values, -1, keepdims=True)
    return d_values, jnp.sum(grad * values * r, 0)


MESH = pl.DeviceIdType.MESH


class Place:
    def __init__(self):
        d = lax.axis_index("dp")
        self.d = d
        self.x = lax.axis_index("expert")
        self.c = lax.rem(d, 2)
        self.z = lax.rem(lax.div(d, 2), 4)
        self.y = lax.div(d, 8)
        self.p = self.z * (1 - self.c) + self.y * self.c
        self.q = self.y * (1 - self.c) + self.z * self.c

    def at(self, p, q):
        y = q * (1 - self.c) + p * self.c
        z = p * (1 - self.c) + q * self.c
        return ((y * 4 + z) * 2 + self.c, self.x)

    def along_p(self, by):
        return self.at(lax.rem(self.p + by, 4), self.q)

    def along_q(self, by):
        return self.at(self.p, lax.rem(self.q + by, 4))

    def along_x(self, by):
        return (self.d, lax.rem(self.x + by, 4))

    def sibling(self):
        return (self.d + 1 - 2 * self.c, self.x)

    def each_core(self, body):
        pl.when(self.c == 0)(lambda: body(0))
        pl.when(self.c == 1)(lambda: body(1))

    def barrier(self, with_x):
        peers = [self.sibling()] + [self.along_p(i) for i in (1, 2, 3)]
        peers += [self.along_q(i) for i in (1, 2, 3)]
        if with_x:
            peers += [self.along_x(i) for i in (1, 2, 3)]
        sem = pltpu.get_barrier_semaphore()
        for peer in peers:
            pl.semaphore_signal(sem, inc=1, device_id=peer, device_id_type=MESH)
        pl.semaphore_wait(sem, len(peers))


def remote(src, dst, send, recv, to):
    return pltpu.make_async_remote_copy(
        src_ref=src, dst_ref=dst, send_sem=send, recv_sem=recv, device_id=to, device_id_type=MESH
    )


def block_of(ref, tall, k, p, q):
    y, z = (q, p) if k == 0 else (p, q)
    return ref.at[y, z, k] if tall else ref.at[k, y, z]


def slab_of(ref, tall, k, q, low=0, count=4):
    y, z = (q, pl.ds(low, count)) if k == 0 else (pl.ds(low, count), q)
    return ref.at[y, z, k] if tall else ref.at[k, y, z]


class Gather:
    sends = 11
    recvs = 11

    def __init__(self, place, ref, tall, send, recv, number):
        self.o, self.ref, self.tall, self.send, self.recv = place, ref, tall, send, recv
        self.number = number

    def block(self, k, by):
        return block_of(self.ref, self.tall, k, lax.rem(self.o.p + by, 4), self.o.q)

    def slab(self, k, by, low=0, count=4):
        return slab_of(self.ref, self.tall, k, lax.rem(self.o.q + by, 4), low, count)

    def go(self, part, s, r, to):
        def body(k):
            src = part(k)
            remote(src, src, self.send.at[s], self.recv.at[r], to).start()

        self.o.each_core(body)

    def arrived(self, r, count):
        if count == 1:
            view = block_of(self.ref, self.tall, 0, 0, 0)
        else:
            view = slab_of(self.ref, self.tall, 0, 0, 0, count)
        remote(view, view, self.send.at[0], self.recv.at[r], self.o.sibling()).wait_recv()

    def sent(self, s, count):
        if count == 1:
            view = block_of(self.ref, self.tall, 0, 0, 0)
        else:
            view = slab_of(self.ref, self.tall, 0, 0, 0, count)
        remote(view, view, self.send.at[s], self.recv.at[0], self.o.sibling()).wait_send()

    def ring_one(self):
        self.go(lambda k: self.block(k, 0), 0, 0, self.o.along_p(1))
        self.go(lambda k: self.block(k, 0), 1, 1, self.o.along_p(3))

    def ring_one_far(self):
        self.arrived(0, 1)
        self.arrived(1, 1)
        if self.number % 2 == 0:
            self.go(lambda k: self.block(k, 3), 2, 2, self.o.along_p(1))
        else:
            self.go(lambda k: self.block(k, 1), 2, 2, self.o.along_p(3))

    def ring_two(self):
        self.arrived(2, 1)
        self.go(lambda k: self.slab(k, 0), 3, 3, self.o.along_q(1))
        self.go(lambda k: self.slab(k, 0), 4, 4, self.o.along_q(3))
        self.go(lambda k: self.slab(k, 0), 7, 7, self.o.sibling())

    def ring_two_far(self):
        self.arrived(3, 4)
        self.go(lambda k: self.slab(k, 3, 0, 2), 5, 5, self.o.along_q(1))
        self.arrived(4, 4)
        self.go(lambda k: self.slab(k, 1, 2, 2), 6, 6, self.o.along_q(3))
        self.go(lambda k: self.slab(k, 3), 8, 8, self.o.sibling())
        self.go(lambda k: self.slab(k, 1), 9, 9, self.o.sibling())

    def last(self):
        self.arrived(5, 2)
        self.arrived(6, 2)
        self.go(lambda k: self.slab(k, 2), 10, 10, self.o.sibling())

    def finish(self):
        for r in (7, 8, 9, 10):
            self.arrived(r, 4)

    def drain(self):
        for s, count in ((0, 1), (1, 1), (2, 1), (3, 4), (4, 4), (5, 2), (6, 2), (7, 4), (8, 4), (9, 4), (10, 4)):
            self.sent(s, count)


class SmallSum:
    def __init__(self, place, value, arrivals, send, recv, with_x):
        self.o, self.value, self.arrivals, self.send, self.recv = place, value, arrivals, send, recv
        o = place
        self.steps = [[o.sibling()], [o.along_p(i) for i in (1, 2, 3)], [o.along_q(i) for i in (1, 2, 3)]]
        if with_x:
            self.steps.append([o.along_x(i) for i in (1, 2, 3)])
        self.copies = []
        n = 0
        for s, peers in enumerate(self.steps):
            row = []
            for peer in peers:
                row.append(
                    remote(value.at[s], arrivals.at[n], send.at[n], recv.at[n], peer)
                )
                n += 1
            self.copies.append(row)

    def start(self, s):
        for copy in self.copies[s]:
            copy.start()

    def add(self, s):
        first = sum(len(row) for row in self.copies[:s])
        total = self.value[s]
        for i, copy in enumerate(self.copies[s]):
            copy.wait_recv()
            total = total + self.arrivals[first + i]
        self.value[s + 1] = total

    def drain(self):
        for row in self.copies:
            for copy in row:
                copy.wait_send()


def place_small(o, pack):
    row = lax.broadcasted_iota(jnp.int32, (32, 1024), 0)
    lane = lax.broadcasted_iota(jnp.int32, (32, 1024), 1)
    target = jnp.where(row < 24, 24 * o.d + row, jnp.where(row == 24, 768 + o.d, -1))
    hit = jnp.where(lane == target, 1.0, 0.0)
    spread = mm_tn(pack[...].astype(bf16), hit.astype(bf16))
    return jnp.concatenate(
        [spread[0:8, :768], spread[8:16, 768:896], spread[16:24, 768:896]], 1
    )


def meet(o, halves, stage, other, sem):
    at = 0
    for ref in halves:
        n = ref.shape[1] // 2
        own = pl.ds(pl.multiple_of(o.c * n, 128), n)
        theirs = pl.ds(pl.multiple_of((1 - o.c) * n, 128), n)
        stage[pl.ds(pl.multiple_of(24 * o.c, 8), 24), at : at + n] = ref[:, own].astype(f32)
        other[:, at : at + n] = ref[:, theirs].astype(f32)
        at += n
    return remote(
        other, stage.at[pl.ds(pl.multiple_of(24 * o.c, 8), 24)], sem.at[0], sem.at[1], o.sibling()
    )


def gather_kernel(
    w_qkv, w_ao, w_in, w_out, pack, g_qkv, g_ao, g_in, g_out, small,
    stage, other, pair_sem, sends, recvs, arrivals, small_send, small_recv,
):
    o = Place()
    o.barrier(False)
    flows = [
        Gather(o, ref, tall, sends.at[i], recvs.at[i], i)
        for i, (ref, tall) in enumerate(((g_qkv, 0), (g_ao, 0), (g_in, 0), (g_out, 1)))
    ]
    qkv, ao, win, wout = flows
    pair = meet(o, (w_qkv, w_ao, w_in), stage, other, pair_sem)
    pair.start()
    tot = SmallSum(o, small, arrivals, small_send, small_recv, False)
    small[0] = place_small(o, pack)
    tot.start(0)
    g_out[o.y, o.z, o.c] = w_out[...]
    pair.wait_recv()
    at = 0
    for ref in (g_qkv, g_ao, g_in):
        n = ref.shape[-1]
        ref[o.c, o.y, o.z] = stage[:, at : at + n].astype(bf16)
        at += n
    qkv.ring_one()
    tot.add(0)
    tot.start(1)
    qkv.ring_one_far()
    qkv.ring_two()
    for f in (ao, win, wout):
        f.ring_one()
    tot.add(1)
    tot.start(2)
    for f in (ao, win, wout):
        f.ring_one_far()
    qkv.ring_two_far()
    for f in (ao, win, wout):
        f.ring_two()
    tot.add(2)
    qkv.last()
    ao.ring_two_far()
    qkv.finish()
    ao.last()
    win.ring_two_far()
    ao.finish()
    win.last()
    wout.ring_two_far()
    win.finish()
    wout.last()
    wout.finish()
    pair.wait_send()
    tot.drain()
    for f in flows:
        f.drain()


def gather_all(w_qkv, w_ao, w_in, w_out, pack):
    vm = pl.BlockSpec(memory_space=pltpu.VMEM)
    return pl.pallas_call(
        gather_kernel,
        in_specs=[vm] * 5,
        out_specs=[vm] * 5,
        out_shape=[
            jax.ShapeDtypeStruct((2, 4, 4, 48, 1152), bf16),
            jax.ShapeDtypeStruct((2, 4, 4, 48, 384), bf16),
            jax.ShapeDtypeStruct((2, 4, 4, 48, 1536), bf16),
            jax.ShapeDtypeStruct((4, 4, 2, 96, 768), bf16),
            jax.ShapeDtypeStruct((4, 8, 1024), f32),
        ],
        scratch_shapes=[
            pltpu.VMEM((48, 3072), f32),
            pltpu.VMEM((24, 3072), f32),
            pltpu.SemaphoreType.DMA((2,)),
            pltpu.SemaphoreType.DMA((4, 11)),
            pltpu.SemaphoreType.DMA((4, 11)),
            pltpu.VMEM((7, 8, 1024), f32),
            pltpu.SemaphoreType.DMA((7,)),
            pltpu.SemaphoreType.DMA((7,)),
        ],
        compiler_params=pltpu.CompilerParams(
            collective_id=0, has_side_effects=True, vmem_limit_bytes=48 * 2**20
        ),
    )(w_qkv, w_ao, w_in, w_out, pack)


class Scatter:
    def __init__(self, place, ref, tall, pair, far, near, side, send, recv):
        self.o, self.ref, self.tall = place, ref, tall
        self.pair, self.far, self.near, self.side = pair, far, near, side
        self.send, self.recv = send, recv

    def where(self, p, q):
        o = self.o
        return q * (1 - o.c) + p * o.c, p * (1 - o.c) + q * o.c

    def q_at(self, by):
        return lax.rem(self.o.q + by, 4)

    def own(self, p, q):
        y, z = self.where(p, q)
        return (y, z, self.o.c) if self.tall else (self.o.c, y, z)

    def to_pair(self, s, low, count):
        rows = pl.ds(low, count)
        theirs = 1 - self.o.c
        src = self.ref.at[rows, :, theirs] if self.tall else self.ref.at[theirs, rows]
        remote(src, self.pair.at[rows], self.send.at[s], self.recv.at[s], self.o.sibling()).start()

    def from_pair(self, s, count):
        view = self.pair.at[pl.ds(0, count)]
        remote(view, view, self.send.at[s], self.recv.at[s], self.o.sibling()).wait_recv()

    def add_pair(self, by):
        q = self.q_at(by)

        def body(p, carry):
            y, z = self.where(p, q)
            at = self.own(p, q)
            self.ref[at] = (self.ref[at].astype(f32) + self.pair[y, z].astype(f32)).astype(bf16)
            return carry

        lax.fori_loop(0, 4, body, 0)

    def go(self, s, by, low, dst, to):
        def body(k):
            src = slab_of(self.ref, self.tall, k, self.q_at(by), low, 2)
            remote(src, dst, self.send.at[s], self.recv.at[s], to).start()

        self.o.each_core(body)

    def ring(self):
        o = self.o
        self.add_pair(2)
        self.go(2, 2, 0, self.far.at[0], o.along_q(1))
        self.go(3, 2, 2, self.far.at[1], o.along_q(3))
        self.add_pair(1)
        self.go(4, 1, 2, self.near.at[0, pl.ds(2, 2)], o.along_q(1))
        self.add_pair(3)
        self.go(5, 3, 0, self.near.at[1, pl.ds(0, 2)], o.along_q(3))
        self.add_pair(0)

    def landed(self, s, view):
        remote(view, view, self.send.at[s], self.recv.at[s], self.o.sibling()).wait_recv()

    def add_far(self, i, by, low):
        q = self.q_at(by)

        def body(j, carry):
            at = self.own(low + j, q)
            self.ref[at] = (self.ref[at].astype(f32) + self.far[i, j].astype(f32)).astype(bf16)
            return carry

        lax.fori_loop(0, 2, body, 0)

    def ring_far(self):
        o = self.o
        self.landed(2, self.far.at[0])
        self.add_far(0, 1, 0)
        self.go(6, 1, 0, self.near.at[0, pl.ds(0, 2)], o.along_q(1))
        self.landed(3, self.far.at[1])
        self.add_far(1, 3, 2)
        self.go(7, 3, 2, self.near.at[1, pl.ds(2, 2)], o.along_q(3))

    def across(self):
        o = self.o
        half = self.near.at[0, pl.ds(0, 2)]
        for s in (4, 5, 6, 7):
            self.landed(s, half)

        def body(p, carry):
            at = self.own(p, o.q)
            total = self.ref[at].astype(f32) + self.near[0, p].astype(f32)
            self.ref[at] = (total + self.near[1, p].astype(f32)).astype(bf16)
            return carry

        lax.fori_loop(0, 4, body, 0)
        for i in (1, 2, 3):
            src = self.ref.at[self.own(lax.rem(o.p + i, 4), o.q)]
            remote(
                src, self.side.at[i - 1], self.send.at[7 + i], self.recv.at[7 + i], o.along_p(i)
            ).start()

    def total(self):
        o = self.o
        for i in (0, 1, 2):
            self.landed(8 + i, self.side.at[i])
        total = self.ref[self.own(o.p, o.q)].astype(f32)
        for i in (0, 1, 2):
            total = total + self.side[i].astype(f32)
        return total

    def sent(self, s, view):
        remote(view, view, self.send.at[s], self.recv.at[s], self.o.sibling()).wait_send()

    def drain(self, pair_parts):
        for s, count in pair_parts:
            self.sent(s, self.pair.at[pl.ds(0, count)])
        for s in range(2, 8):
            self.sent(s, self.far.at[0])
        for s in range(8, 11):
            self.sent(s, self.side.at[0])


SQ = 0.7978845608028654


def gelu_both(h):
    t = jnp.tanh(SQ * (h + 0.044715 * (h * h * h)))
    value = 0.5 * h * (1.0 + t)
    slope = 0.5 * (1.0 + t) + 0.5 * h * (1.0 - t * t) * (SQ * (1.0 + 3 * 0.044715 * (h * h)))
    return value, slope


def expert_chunk(j, sent, sent_t, d_result, g_in, g_out, h_in, h_out, result, d_incoming):
    half, at = lax.div(j, 4), pl.ds(pl.multiple_of(lax.rem(j, 4) * 384, 128), 384)
    y, z = lax.div(j, 2), pl.ds(lax.rem(j, 2) * 2, 2)
    first = g_in[half, :, :, :, at].reshape(768, 384)
    second = g_out[y, z].reshape(384, 768)
    hidden = mm(sent[...], first)
    value, slope = gelu_both(hidden)
    act = value.astype(bf16)
    result[...] += mm(act, second)
    d_act = mm_nt(d_result[...], second)
    d_hidden = (d_act * slope).astype(bf16)
    h_out[y, z] = mm_tn(act, d_result[...]).astype(bf16).reshape(2, 2, 96, 768)
    h_in[half, :, :, :, at] = mm(sent_t[...], d_hidden).astype(bf16).reshape(4, 4, 48, 384)
    d_incoming[...] += mm_nt(d_hidden, first)


def pair_backward(o, i, query, key, value, weights, d_heads, d_query, d_kv, d_kr, d_window, send, recv):
    lanes = pl.ds(pl.multiple_of(i * 128, 128), 128)
    probability = weights[pl.ds(2 * i, 2)].reshape(256, 512)
    d_stack = stack_heads(d_heads[:, lanes])
    d_weights = mm_nt(d_stack, value[:, lanes])
    d_kv[:, 1, :, lanes] = (
        mm_tn(probability.astype(bf16), d_stack).astype(bf16).reshape(4, 128, 128)
    )
    d_scores = probability * (d_weights - jnp.sum(probability * d_weights, -1, keepdims=True))
    low = d_scores.astype(bf16)
    d_kv[:, 0, :, lanes] = (
        mm_tn(low, stack_heads(query[:, lanes])).astype(bf16).reshape(4, 128, 128)
    )
    for by in (1, 2, 3):
        there = lax.rem(o.x + by, 4)
        remote(
            d_kv.at[there, :, :, lanes], d_kr.at[by - 1, :, :, lanes],
            send.at[i, by - 1], recv.at[i, by - 1], o.along_x(by),
        ).start()
    d_query[:, lanes] = join_pair(mm(low, key[:, lanes])).astype(bf16)
    for j in (0, 1):
        d_window[pl.ds(2 * i + j, 1), :] = diagonal_sums(d_scores[j * 128 : (j + 1) * 128], 640)


def back_kernel(
    g_qkv, g_ao, g_in, g_out, sent, d_result, placing, after_attn, probs, chosen, cotangent,
    moe_input, heads_out, tokens, query, kv, weights, small_in, buckets,
    mixed, d_tokens, out_qkv, out_ao, out_in, out_out, small,
    h_qkv, h_ao, h_in, h_out, sent_t, result, d_incoming, ret, back, d_query, d_kv, d_kr, d_window,
    d_heads_ref, d_after_ref, total_q, total_a, total_i, xs, xr, xa,
    pair_q, pair_a, pair_i, pair_o, far_q, far_a, far_i, far_o, near_q, near_a, near_i, near_o,
    side_q, side_a, side_i, side_o,
    sends, recvs, ret_send, ret_recv, dk_send, dk_recv, x_send, x_recv, last_send, last_recv,
    arrivals, small_send, small_recv,
):
    o = Place()
    o.barrier(True)
    fq = Scatter(o, h_qkv, 0, pair_q, far_q, near_q, side_q, sends.at[0], recvs.at[0])
    fa = Scatter(o, h_ao, 0, pair_a, far_a, near_a, side_a, sends.at[1], recvs.at[1])
    fi = Scatter(o, h_in, 0, pair_i, far_i, near_i, side_i, sends.at[2], recvs.at[2])
    fo = Scatter(o, h_out, 1, pair_o, far_o, near_o, side_o, sends.at[3], recvs.at[3])
    tot = SmallSum(o, small, arrivals, small_send, small_recv, True)

    sent_t[...] = sent[...].astype(f32).T.astype(bf16)
    result[...] = jnp.zeros_like(result)
    d_incoming[...] = jnp.zeros_like(d_incoming)

    def chunk(j, carry):
        expert_chunk(j, sent, sent_t, d_result, g_in, g_out, h_in, h_out, result, d_incoming)
        return carry

    start = 4 * (1 - o.c)
    lax.fori_loop(start, start + 4, chunk, 0)
    fi.to_pair(0, 0, 4)
    fo.to_pair(0, 2 * (1 - o.c), 2)
    lax.fori_loop(4 - start, 8 - start, chunk, 0)
    fo.to_pair(1, 2 * o.c, 2)
    ret[:, 0] = result[...].astype(bf16).reshape(4, 48, 768)
    ret[:, 1] = d_incoming[...].astype(bf16).reshape(4, 48, 768)
    ret_copies = [
        remote(
            ret.at[lax.rem(o.x + by, 4)], back.at[o.x], ret_send.at[by - 1], ret_recv.at[by - 1],
            o.along_x(by),
        )
        for by in (1, 2, 3)
    ]
    for copy in ret_copies:
        copy.start()
    back[o.x] = ret[o.x]
    fi.from_pair(0, 4)
    fi.ring()
    for copy in ret_copies:
        copy.wait_recv()

    small8 = small_in[:, :768]
    gain_one, gain_two = small8[0:1], small8[1:2]
    returned = mm(placing[...], back[:, 0].reshape(192, 768))
    d_moe = mm(placing[...], back[:, 1].reshape(192, 768))
    attn = after_attn[...]
    upstream = cotangent[...].astype(f32)
    gate = jnp.sum(probs[...] * chosen[...], -1, keepdims=True)
    mixed[...] = (attn + gate * returned).astype(bf16)
    d_gate = jnp.sum(upstream * returned, -1, keepdims=True)
    d_logits = probs[...] * (d_gate * chosen[...] - d_gate * gate)
    d_moe = d_moe + jnp.dot(d_logits, small8, precision=highest, preferred_element_type=f32)
    grad_router = lax.dot_general(
        d_logits, moe_input[...].astype(f32), TN, precision=highest, preferred_element_type=f32
    )
    r_two = lax.rsqrt(jnp.mean(attn * attn, -1, keepdims=True) + epsilon)
    d_after, grad_norm_two = rms_backward(attn, r_two, gain_two, d_moe)
    d_after = d_after + upstream
    d_after_ref[...] = d_after
    d_attn = d_after.astype(bf16)
    d_heads = jnp.zeros((128, 768), f32)
    for h in (0, 1):
        part = d_attn[:, h * 384 : (h + 1) * 384]
        h_ao[h] = mm_tn(heads_out[...], part).astype(bf16).reshape(4, 4, 48, 384)
        d_heads = d_heads + mm_nt(part, g_ao[h].reshape(768, 384))
    fa.to_pair(0, 0, 4)
    d_heads_ref[...] = d_heads.astype(bf16)
    fo.from_pair(0, 2)
    fo.from_pair(1, 2)
    fo.ring()

    d_window[...] = jnp.zeros_like(d_window)
    key, value = kv.at[:, pl.ds(0, 768)], kv.at[:, pl.ds(768, 768)]

    def pair(i, carry):
        pair_backward(
            o, i, query, key, value, weights, d_heads_ref, d_query, d_kv, d_kr, d_window, dk_send, dk_recv
        )
        return carry

    lax.fori_loop(0, 2, pair, 0)
    fi.ring_far()
    fa.from_pair(0, 4)
    fa.ring()
    lax.fori_loop(2, 4, pair, 0)
    fo.ring_far()
    fi.across()
    lax.fori_loop(4, 6, pair, 0)
    fa.ring_far()

    x = tokens[...].astype(f32)
    r_one, normed = rms_forward(x, gain_one)
    normed_t = normed.T.astype(bf16)

    def project(h, d_part):
        h_qkv[h] = mm(normed_t, d_part).astype(bf16).reshape(4, 4, 48, 1152)
        return mm_nt(d_part, g_qkv[h].reshape(768, 1152))

    bucket_row = buckets[:, pl.ds(pl.multiple_of((3 - o.x) * 128, 128), 640)]
    picks = jnp.where(
        jnp.broadcast_to(bucket_row, (128, 640)) == lax.broadcasted_iota(jnp.int32, (128, 640), 0), 1.0, 0.0
    )
    grad_table = lax.dot_general(
        d_window[...], picks, NT, precision=highest, preferred_element_type=f32
    )
    fo.across()
    for i in range(6):
        for by in (1, 2, 3):
            view = d_kr.at[by - 1, :, :, pl.ds(0, 128)]
            remote(view, view, dk_send.at[i, by - 1], dk_recv.at[i, by - 1], o.sibling()).wait_recv()
    d_own = d_kv[o.x].astype(f32)
    for by in (0, 1, 2):
        d_own = d_own + d_kr[by].astype(f32)
    d_own = d_own.astype(bf16)
    d_key, d_value = d_own[0], d_own[1]
    d_normed = project(0, jnp.concatenate([d_query[...], d_key[:, :384]], 1))
    d_normed = d_normed + project(1, jnp.concatenate([d_key[:, 384:], d_value], 1))
    fq.to_pair(0, 0, 4)
    d_resid, grad_norm_one = rms_backward(x, r_one, gain_one, d_normed)
    d_tokens[...] = (d_after_ref[...] + d_resid).astype(bf16)
    row = lax.broadcasted_iota(jnp.int32, (8, 768), 0)
    top = jnp.where(row == 0, grad_norm_one[None, :], jnp.where(row == 1, grad_norm_two[None, :], grad_router))
    small[0] = jnp.concatenate([top, grad_table[0:8], grad_table[8:16]], 1)
    tot.start(0)
    fa.across()
    fq.from_pair(0, 4)
    fq.ring()
    tot.add(0)
    tot.start(1)
    out_out[...] = fo.total()

    def hand(k, total, out, value):
        n = value.shape[1]
        total[...] = value
        mine = pl.ds(pl.multiple_of(o.c * n, 128), n)
        out[:, mine] = total[pl.ds(pl.multiple_of(24 * o.c, 8), 24), :]
        copy = remote(
            total.at[pl.ds(pl.multiple_of(24 * (1 - o.c), 8), 24)], out.at[:, mine],
            last_send.at[k], last_recv.at[k], o.sibling(),
        )
        copy.start()
        return copy

    last = [hand(0, total_i, out_in, fi.total())]
    total_a[...] = fa.total()
    tot.add(1)
    tot.start(2)
    fq.ring_far()
    fq.across()
    tot.add(2)
    tot.start(3)
    dense = jnp.concatenate([fq.total(), total_a[...]], 1).astype(bf16)
    for j in range(4):
        xs[j] = dense[:, j * 384 : (j + 1) * 384]
    first = [
        remote(xs.at[lax.rem(o.x + by, 4)], xr.at[by - 1], x_send.at[by - 1], x_recv.at[by - 1], o.along_x(by))
        for by in (1, 2, 3)
    ]
    for copy in first:
        copy.start()
    for copy in first:
        copy.wait_recv()
    own = xs[o.x].astype(f32)
    for j in range(3):
        own = own + xr[j].astype(f32)
    xa[o.x] = own.astype(bf16)
    second = [
        remote(xa.at[o.x], xa.at[o.x], x_send.at[by + 2], x_recv.at[by + 2], o.along_x(by)) for by in (1, 2, 3)
    ]
    for copy in second:
        copy.start()
    for copy in second:
        copy.wait_recv()
    whole = jnp.concatenate([xa[0], xa[1], xa[2], xa[3]], 1).astype(f32)
    last.append(hand(1, total_q, out_qkv, whole[:, :1152]))
    last.append(hand(2, total_a, out_ao, whole[:, 1152:]))
    tot.add(3)
    for copy in last:
        copy.wait_recv()
    for copy in ret_copies + first + second + last:
        copy.wait_send()
    for i in range(6):
        for by in (1, 2, 3):
            view = d_kr.at[by - 1, :, :, pl.ds(0, 128)]
            remote(view, view, dk_send.at[i, by - 1], dk_recv.at[i, by - 1], o.sibling()).wait_send()
    tot.drain()
    for f in (fq, fa, fi):
        f.drain([(0, 4)])
    fo.drain([(0, 2), (1, 2)])


def backward_all(*operands):
    vm = pl.BlockSpec(memory_space=pltpu.VMEM)
    dma = pltpu.SemaphoreType.DMA

    def low(*shape):
        return pltpu.VMEM(shape, bf16)

    def full(*shape):
        return pltpu.VMEM(shape, f32)

    sizes = ((48, 1152), (48, 384), (48, 1536), (96, 768))
    return pl.pallas_call(
        back_kernel,
        in_specs=[vm] * len(operands),
        out_specs=[vm] * 7,
        out_shape=[
            jax.ShapeDtypeStruct((128, 768), bf16),
            jax.ShapeDtypeStruct((128, 768), bf16),
            jax.ShapeDtypeStruct((24, 2304), f32),
            jax.ShapeDtypeStruct((24, 768), f32),
            jax.ShapeDtypeStruct((24, 3072), f32),
            jax.ShapeDtypeStruct((96, 768), f32),
            jax.ShapeDtypeStruct((5, 8, 1024), f32),
        ],
        scratch_shapes=[
            low(2, 4, 4, 48, 1152), low(2, 4, 4, 48, 384), low(2, 4, 4, 48, 1536), low(4, 4, 2, 96, 768),
            low(768, 192), full(192, 768), full(192, 768), low(4, 2, 48, 768), low(4, 2, 48, 768),
            low(128, 768), low(4, 2, 128, 768), low(3, 2, 128, 768), full(16, 640),
            low(128, 768), full(128, 768), full(48, 1152), full(48, 384), full(48, 1536),
            low(4, 48, 384), low(3, 48, 384), low(4, 48, 384),
            *[low(4, 4, *s) for s in sizes],
            *[low(2, 2, *s) for s in sizes],
            *[low(2, 4, *s) for s in sizes],
            *[low(3, *s) for s in sizes],
            dma((4, 11)), dma((4, 11)), dma((3,)), dma((3,)), dma((6, 3)), dma((6, 3)),
            dma((6,)), dma((6,)), dma((3,)), dma((3,)),
            full(10, 8, 1024), dma((10,)), dma((10,)),
        ],
        compiler_params=pltpu.CompilerParams(
            collective_id=1, has_side_effects=True, vmem_limit_bytes=60 * 2**20
        ),
    )(*operands)


def per_device(
    tokens, norm_attn, w_qkv, w_attn_out, bias_table, norm_moe, router, w_in, w_out, routes, buckets, cotangent
):
    rows, width = tokens.shape
    dp = lax.axis_index("dp")
    ex = lax.axis_index("expert")
    groups = 4
    keys = rows * groups
    heads = 12
    window_width = keys + rows

    own = norm_attn.shape[0]
    pack = jnp.concatenate([norm_attn[:, None], norm_moe[:, None], router, jnp.zeros((own, 122), bf16)], 1)
    last = jnp.concatenate([jnp.zeros((1, 8), bf16), bias_table, jnp.zeros((1, 108), bf16)], 1)
    pack = jnp.concatenate([pack, last, jnp.zeros((7, 128), bf16)], 0).astype(f32)
    g_qkv, g_ao, g_in, g_out, small = gather_all(w_qkv, w_attn_out, w_in[:, 0], w_out[:, 0], pack)
    small = small[3]
    full_qkv = jnp.concatenate([g_qkv[0].reshape(768, -1), g_qkv[1].reshape(768, -1)], 1)
    full_out = jnp.concatenate([g_ao[0].reshape(768, -1), g_ao[1].reshape(768, -1)], 1)
    gain_one, gain_two, router_t = small[0:1, :768], small[1:2, :768], small[2:6, :768]
    table_full = jnp.concatenate([small[:8, 768:800], small[:4, 896:928]], 0)

    x = tokens.astype(f32)
    r_one, normed = rms_forward(x, gain_one)
    normed = normed.astype(bf16)
    projected = mm(normed, full_qkv).astype(bf16)
    query = projected[:, :768]
    kv = lax.all_gather(projected[:, 768:], "expert", axis=0, tiled=True)
    key, value = kv[:, :768], kv[:, 768:]
    padded = jnp.concatenate([buckets, jnp.zeros((1,), jnp.int32)])
    bucket_window = lax.dynamic_slice_in_dim(padded, (groups - 1 - ex) * rows, window_width, 0)
    picks = (bucket_window[None, :] == jnp.arange(32, dtype=jnp.int32)[:, None]).astype(f32)
    window = jnp.concatenate(
        [jnp.dot(table_full, picks, precision=highest), jnp.zeros((4, window_width), f32)], 0
    )

    pairs = heads // 2
    heads_out, weights = pl.pallas_call(
        attention_forward,
        grid=(pairs,),
        in_specs=[
            pl.BlockSpec((rows, 128), lambda p: (0, p)),
            pl.BlockSpec((keys, 128), lambda p: (0, p)),
            pl.BlockSpec((keys, 128), lambda p: (0, p)),
            pl.BlockSpec((16, window_width), lambda p: (0, 0)),
        ],
        out_specs=[
            pl.BlockSpec((rows, 128), lambda p: (0, p)),
            pl.BlockSpec((2, rows, keys), lambda p: (p, 0, 0)),
        ],
        out_shape=[
            jax.ShapeDtypeStruct((rows, width), bf16),
            jax.ShapeDtypeStruct((heads, rows, keys), f32),
        ],
        compiler_params=pltpu.CompilerParams(vmem_limit_bytes=32 * 2**20),
    )(query, key, value, window)

    after_attn = x + mm(heads_out, full_out)
    r_two, moe_input = rms_forward(after_attn, gain_two)
    moe_input = moe_input.astype(bf16)
    logits = jnp.dot(moe_input.astype(f32), router_t.T, precision=highest)
    probs = jax.nn.softmax(logits, -1)
    chosen_int = (routes == jnp.arange(4, dtype=jnp.int32)[None, :]).astype(jnp.int32)
    chosen = chosen_int.astype(f32)
    gate = jnp.sum(probs * chosen, -1, keepdims=True)
    slots = 48
    slot = jnp.sum((jnp.cumsum(chosen_int, 0) - 1) * chosen_int, -1)
    column = routes[:, 0] * slots + slot
    placing = (column[:, None] == jnp.arange(4 * slots, dtype=jnp.int32)[None, :]).astype(bf16)
    upstream = cotangent.astype(f32)
    d_combined = (gate * upstream).astype(bf16)
    outgoing = mm_tn(placing, jnp.concatenate([moe_input, d_combined], 1)).astype(bf16)
    incoming = lax.all_to_all(outgoing, "expert", split_axis=0, concat_axis=0, tiled=True)
    probs8 = jnp.concatenate([jnp.zeros((rows, 2), f32), probs, jnp.zeros((rows, 2), f32)], 1)
    chosen8 = jnp.concatenate([jnp.zeros((rows, 2), f32), chosen, jnp.zeros((rows, 2), f32)], 1)
    mixed, d_tokens, out_qkv, out_ao, out_in, out_outw, small_grads = backward_all(
        g_qkv, g_ao, g_in, g_out, incoming[:, :768], incoming[:, 768:], placing, after_attn, probs8, chosen8,
        cotangent, moe_input, heads_out, tokens, query, kv, weights, small, padded[None, :],
    )
    small_grads = small_grads[4]
    mine = lax.dynamic_slice(small_grads, (0, dp * own), (8, own))
    table_col = jnp.concatenate(
        [
            lax.dynamic_slice(small_grads, (0, 768 + dp), (8, 1)),
            lax.dynamic_slice(small_grads, (0, 896 + dp), (4, 1)),
        ],
        0,
    )
    return (
        mixed,
        d_tokens,
        mine[0],
        out_qkv,
        out_ao,
        table_col.T,
        mine[1],
        mine[2:6].T,
        out_in[:, None],
        out_outw[:, None],
    )


def solution(mesh):
    both = ("dp", "expert")
    in_specs = (
        P(both, None), P("dp"), P("dp", None), P("dp", None), P("dp", None), P("dp"), P("dp", None),
        P("dp", "expert", None), P("dp", "expert", None), P(both, None), P(), P(both, None),
    )
    out_specs = (
        P(both, None), P(both, None), P("dp"), P("dp", None), P("dp", None), P("dp", None), P("dp"),
        P("dp", None), P("dp", "expert", None), P("dp", "expert", None),
    )
    return jax.shard_map(
        per_device, mesh=mesh, in_specs=in_specs, out_specs=out_specs, check_vma=False
    )
```

```python
import jax
import jax.numpy as jnp
from jax import lax
from jax.experimental import pallas as pl
from jax.experimental.pallas import tpu as pltpu
from jax.sharding import PartitionSpec as P

epsilon = 1e-06
highest = lax.Precision.HIGHEST
bf16 = jnp.bfloat16
f32 = jnp.float32
NT = (((1,), (1,)), ((), ()))
TN = (((0,), (0,)), ((), ()))


def mm(a, b):
    return jnp.dot(a, b, preferred_element_type=f32)


def mm_nt(a, b):
    return lax.dot_general(a, b, NT, preferred_element_type=f32)


def mm_tn(a, b):
    return lax.dot_general(a, b, TN, preferred_element_type=f32)


def stack_heads(pair):
    left = lax.broadcasted_iota(jnp.int32, pair.shape, 1) < 64
    zero = jnp.zeros_like(pair)
    return jnp.concatenate([jnp.where(left, pair, zero), jnp.where(left, zero, pair)], 0)


def join_pair(stacked):
    rows = stacked.shape[0] // 2
    left = lax.broadcasted_iota(jnp.int32, (rows, 128), 1) < 64
    return jnp.where(left, stacked[:rows], stacked[rows:])


def toeplitz(window_row, rows, keys):
    width = window_row.shape[1]
    wide = jnp.broadcast_to(window_row, (rows, width))
    rolled = pltpu.roll(wide, width - (rows - 1), 1, stride=1, stride_axis=0)
    return rolled[:, :keys]


def diagonal_sums(block, width):
    rows, keys = block.shape
    wide = jnp.concatenate([block, jnp.zeros((rows, width - keys), f32)], 1)
    half = rows // 2
    while half >= 8:
        wide = wide[:half] + pltpu.roll(wide[half:], width - half, 1)
        half //= 2
    row = lax.broadcasted_iota(jnp.int32, wide.shape, 0)
    for bit in (1, 2, 4):
        wide = jnp.where((row & bit) != 0, pltpu.roll(wide, width - bit, 1), wide)
    total = jnp.sum(wide, 0, keepdims=True)
    return pltpu.roll(total, rows - 1, 1)


def rms_backward(values, r, gain, grad):
    u = grad * gain
    d_values = r * u - values * (r * r * r) * jnp.mean(u * values, -1, keepdims=True)
    return d_values, jnp.sum(grad * values * r, 0)


MESH = pl.DeviceIdType.MESH


class Place:
    def __init__(self):
        d = lax.axis_index("dp")
        self.d = d
        self.x = lax.axis_index("expert")
        self.c = lax.rem(d, 2)
        self.z = lax.rem(lax.div(d, 2), 4)
        self.y = lax.div(d, 8)
        self.p = self.z * (1 - self.c) + self.y * self.c
        self.q = self.y * (1 - self.c) + self.z * self.c

    def at(self, p, q):
        y = q * (1 - self.c) + p * self.c
        z = p * (1 - self.c) + q * self.c
        return ((y * 4 + z) * 2 + self.c, self.x)

    def along_p(self, by):
        return self.at(lax.rem(self.p + by, 4), self.q)

    def along_q(self, by):
        return self.at(self.p, lax.rem(self.q + by, 4))

    def along_x(self, by):
        return (self.d, lax.rem(self.x + by, 4))

    def sibling(self):
        return (self.d + 1 - 2 * self.c, self.x)

    def each_core(self, body):
        pl.when(self.c == 0)(lambda: body(0))
        pl.when(self.c == 1)(lambda: body(1))

    def barrier(self, with_x):
        peers = [self.sibling()] + [self.along_p(i) for i in (1, 2, 3)]
        peers += [self.along_q(i) for i in (1, 2, 3)]
        if with_x:
            peers += [self.along_x(i) for i in (1, 2, 3)]
        sem = pltpu.get_barrier_semaphore()
        for peer in peers:
            pl.semaphore_signal(sem, inc=1, device_id=peer, device_id_type=MESH)
        pl.semaphore_wait(sem, len(peers))


def remote(src, dst, send, recv, to):
    return pltpu.make_async_remote_copy(
        src_ref=src, dst_ref=dst, send_sem=send, recv_sem=recv, device_id=to, device_id_type=MESH
    )


def block_of(ref, tall, k, p, q):
    y, z = (q, p) if k == 0 else (p, q)
    return ref.at[y, z, k] if tall else ref.at[k, y, z]


def slab_of(ref, tall, k, q, low=0, count=4):
    y, z = (q, pl.ds(low, count)) if k == 0 else (pl.ds(low, count), q)
    return ref.at[y, z, k] if tall else ref.at[k, y, z]


class Gather:
    sends = 11
    recvs = 11

    def __init__(self, place, ref, tall, send, recv, number):
        self.o, self.ref, self.tall, self.send, self.recv = place, ref, tall, send, recv
        self.number = number

    def block(self, k, by):
        return block_of(self.ref, self.tall, k, lax.rem(self.o.p + by, 4), self.o.q)

    def slab(self, k, by, low=0, count=4):
        return slab_of(self.ref, self.tall, k, lax.rem(self.o.q + by, 4), low, count)

    def go(self, part, s, r, to):
        def body(k):
            src = part(k)
            remote(src, src, self.send.at[s], self.recv.at[r], to).start()

        self.o.each_core(body)

    def arrived(self, r, count):
        if count == 1:
            view = block_of(self.ref, self.tall, 0, 0, 0)
        else:
            view = slab_of(self.ref, self.tall, 0, 0, 0, count)
        remote(view, view, self.send.at[0], self.recv.at[r], self.o.sibling()).wait_recv()

    def sent(self, s, count):
        if count == 1:
            view = block_of(self.ref, self.tall, 0, 0, 0)
        else:
            view = slab_of(self.ref, self.tall, 0, 0, 0, count)
        remote(view, view, self.send.at[s], self.recv.at[0], self.o.sibling()).wait_send()

    def ring_one(self):
        self.go(lambda k: self.block(k, 0), 0, 0, self.o.along_p(1))
        self.go(lambda k: self.block(k, 0), 1, 1, self.o.along_p(3))

    def ring_one_far(self):
        self.arrived(0, 1)
        self.arrived(1, 1)
        if self.number % 2 == 0:
            self.go(lambda k: self.block(k, 3), 2, 2, self.o.along_p(1))
        else:
            self.go(lambda k: self.block(k, 1), 2, 2, self.o.along_p(3))

    def ring_two(self):
        self.arrived(2, 1)
        self.go(lambda k: self.slab(k, 0), 3, 3, self.o.along_q(1))
        self.go(lambda k: self.slab(k, 0), 4, 4, self.o.along_q(3))
        self.go(lambda k: self.slab(k, 0), 7, 7, self.o.sibling())

    def ring_two_far(self):
        self.arrived(3, 4)
        self.go(lambda k: self.slab(k, 3, 0, 2), 5, 5, self.o.along_q(1))
        self.arrived(4, 4)
        self.go(lambda k: self.slab(k, 1, 2, 2), 6, 6, self.o.along_q(3))
        self.go(lambda k: self.slab(k, 3), 8, 8, self.o.sibling())
        self.go(lambda k: self.slab(k, 1), 9, 9, self.o.sibling())

    def last(self):
        self.arrived(5, 2)
        self.arrived(6, 2)
        self.go(lambda k: self.slab(k, 2), 10, 10, self.o.sibling())

    def finish(self):
        for r in (7, 8, 9, 10):
            self.arrived(r, 4)

    def drain(self):
        for s, count in ((0, 1), (1, 1), (2, 1), (3, 4), (4, 4), (5, 2), (6, 2), (7, 4), (8, 4), (9, 4), (10, 4)):
            self.sent(s, count)


class SmallSum:
    def __init__(self, place, value, arrivals, send, recv, with_x):
        self.o, self.value, self.arrivals, self.send, self.recv = place, value, arrivals, send, recv
        o = place
        self.steps = [[o.sibling()], [o.along_p(i) for i in (1, 2, 3)], [o.along_q(i) for i in (1, 2, 3)]]
        if with_x:
            self.steps.append([o.along_x(i) for i in (1, 2, 3)])
        self.copies = []
        n = 0
        for s, peers in enumerate(self.steps):
            row = []
            for peer in peers:
                row.append(
                    remote(value.at[s], arrivals.at[n], send.at[n], recv.at[n], peer)
                )
                n += 1
            self.copies.append(row)

    def start(self, s):
        for copy in self.copies[s]:
            copy.start()

    def add(self, s):
        first = sum(len(row) for row in self.copies[:s])
        total = self.value[s]
        for i, copy in enumerate(self.copies[s]):
            copy.wait_recv()
            total = total + self.arrivals[first + i]
        self.value[s + 1] = total

    def drain(self):
        for row in self.copies:
            for copy in row:
                copy.wait_send()


def place_small(o, pack):
    row = lax.broadcasted_iota(jnp.int32, (32, 1024), 0)
    lane = lax.broadcasted_iota(jnp.int32, (32, 1024), 1)
    target = jnp.where(row < 24, 24 * o.d + row, jnp.where(row == 24, 768 + o.d, -1))
    hit = jnp.where(lane == target, 1.0, 0.0)
    spread = mm_tn(pack[...].astype(bf16), hit.astype(bf16))
    return jnp.concatenate(
        [spread[0:8, :768], spread[8:16, 768:896], spread[16:24, 768:896]], 1
    )


def meet(o, halves, stage, other, sem):
    at = 0
    for ref in halves:
        n = ref.shape[1] // 2
        own = pl.ds(pl.multiple_of(o.c * n, 128), n)
        theirs = pl.ds(pl.multiple_of((1 - o.c) * n, 128), n)
        stage[pl.ds(pl.multiple_of(24 * o.c, 8), 24), at : at + n] = ref[:, own].astype(f32)
        other[:, at : at + n] = ref[:, theirs].astype(f32)
        at += n
    return remote(
        other, stage.at[pl.ds(pl.multiple_of(24 * o.c, 8), 24)], sem.at[0], sem.at[1], o.sibling()
    )


class Scatter:
    def __init__(self, place, ref, tall, pair, far, near, side, send, recv):
        self.o, self.ref, self.tall = place, ref, tall
        self.pair, self.far, self.near, self.side = pair, far, near, side
        self.send, self.recv = send, recv

    def where(self, p, q):
        o = self.o
        return q * (1 - o.c) + p * o.c, p * (1 - o.c) + q * o.c

    def q_at(self, by):
        return lax.rem(self.o.q + by, 4)

    def own(self, p, q):
        y, z = self.where(p, q)
        return (y, z, self.o.c) if self.tall else (self.o.c, y, z)

    def to_pair(self, s, low, count):
        rows = pl.ds(low, count)
        theirs = 1 - self.o.c
        src = self.ref.at[rows, :, theirs] if self.tall else self.ref.at[theirs, rows]
        remote(src, self.pair.at[rows], self.send.at[s], self.recv.at[s], self.o.sibling()).start()

    def from_pair(self, s, count):
        view = self.pair.at[pl.ds(0, count)]
        remote(view, view, self.send.at[s], self.recv.at[s], self.o.sibling()).wait_recv()

    def add_pair(self, by):
        q = self.q_at(by)

        def body(p, carry):
            y, z = self.where(p, q)
            at = self.own(p, q)
            self.ref[at] = (self.ref[at].astype(f32) + self.pair[y, z].astype(f32)).astype(bf16)
            return carry

        lax.fori_loop(0, 4, body, 0)

    def go(self, s, by, low, dst, to):
        def body(k):
            src = slab_of(self.ref, self.tall, k, self.q_at(by), low, 2)
            remote(src, dst, self.send.at[s], self.recv.at[s], to).start()

        self.o.each_core(body)

    def ring(self):
        o = self.o
        self.add_pair(2)
        self.go(2, 2, 0, self.far.at[0], o.along_q(1))
        self.go(3, 2, 2, self.far.at[1], o.along_q(3))
        self.add_pair(1)
        self.go(4, 1, 2, self.near.at[0, pl.ds(2, 2)], o.along_q(1))
        self.add_pair(3)
        self.go(5, 3, 0, self.near.at[1, pl.ds(0, 2)], o.along_q(3))
        self.add_pair(0)

    def landed(self, s, view):
        remote(view, view, self.send.at[s], self.recv.at[s], self.o.sibling()).wait_recv()

    def add_far(self, i, by, low):
        q = self.q_at(by)

        def body(j, carry):
            at = self.own(low + j, q)
            self.ref[at] = (self.ref[at].astype(f32) + self.far[i, j].astype(f32)).astype(bf16)
            return carry

        lax.fori_loop(0, 2, body, 0)

    def ring_far(self):
        o = self.o
        self.landed(2, self.far.at[0])
        self.add_far(0, 1, 0)
        self.go(6, 1, 0, self.near.at[0, pl.ds(0, 2)], o.along_q(1))
        self.landed(3, self.far.at[1])
        self.add_far(1, 3, 2)
        self.go(7, 3, 2, self.near.at[1, pl.ds(2, 2)], o.along_q(3))

    def across(self):
        o = self.o
        half = self.near.at[0, pl.ds(0, 2)]
        for s in (4, 5, 6, 7):
            self.landed(s, half)

        def body(p, carry):
            at = self.own(p, o.q)
            total = self.ref[at].astype(f32) + self.near[0, p].astype(f32)
            self.ref[at] = (total + self.near[1, p].astype(f32)).astype(bf16)
            return carry

        lax.fori_loop(0, 4, body, 0)
        for i in (1, 2, 3):
            src = self.ref.at[self.own(lax.rem(o.p + i, 4), o.q)]
            remote(
                src, self.side.at[i - 1], self.send.at[7 + i], self.recv.at[7 + i], o.along_p(i)
            ).start()

    def total(self):
        o = self.o
        for i in (0, 1, 2):
            self.landed(8 + i, self.side.at[i])
        total = self.ref[self.own(o.p, o.q)].astype(f32)
        for i in (0, 1, 2):
            total = total + self.side[i].astype(f32)
        return total

    def sent(self, s, view):
        remote(view, view, self.send.at[s], self.recv.at[s], self.o.sibling()).wait_send()

    def drain(self, pair_parts):
        for s, count in pair_parts:
            self.sent(s, self.pair.at[pl.ds(0, count)])
        for s in range(2, 8):
            self.sent(s, self.far.at[0])
        for s in range(8, 11):
            self.sent(s, self.side.at[0])


SQ = 0.7978845608028654


def gelu_both(h):
    t = jnp.tanh(SQ * (h + 0.044715 * (h * h * h)))
    value = 0.5 * h * (1.0 + t)
    slope = 0.5 * (1.0 + t) + 0.5 * h * (1.0 - t * t) * (SQ * (1.0 + 3 * 0.044715 * (h * h)))
    return value, slope


def expert_chunk(j, sent, sent_t, d_result, g_in, g_out, h_in, h_out, result, d_incoming):
    half, at = lax.div(j, 4), pl.ds(pl.multiple_of(lax.rem(j, 4) * 384, 128), 384)
    y, z = lax.div(j, 2), pl.ds(lax.rem(j, 2) * 2, 2)
    first = g_in[half, :, :, :, at].reshape(768, 384)
    second = g_out[y, z].reshape(384, 768)
    hidden = mm(sent[...], first)
    value, slope = gelu_both(hidden)
    act = value.astype(bf16)
    result[...] += mm(act, second)
    d_act = mm_nt(d_result[...], second)
    d_hidden = (d_act * slope).astype(bf16)
    h_out[y, z] = mm_tn(act, d_result[...]).astype(bf16).reshape(2, 2, 96, 768)
    h_in[half, :, :, :, at] = mm(sent_t[...], d_hidden).astype(bf16).reshape(4, 4, 48, 384)
    d_incoming[...] += mm_nt(d_hidden, first)


def pair_backward(o, i, query, key, value, weights, d_heads, d_query, d_kv, d_kr, d_window, send, recv):
    lanes = pl.ds(pl.multiple_of(i * 128, 128), 128)
    probability = weights[pl.ds(2 * i, 2)].reshape(256, 512)
    d_stack = stack_heads(d_heads[:, lanes])
    d_weights = mm_nt(d_stack, value[:, lanes])
    d_kv[:, 1, :, lanes] = (
        mm_tn(probability.astype(bf16), d_stack).astype(bf16).reshape(4, 128, 128)
    )
    d_scores = probability * (d_weights - jnp.sum(probability * d_weights, -1, keepdims=True))
    low = d_scores.astype(bf16)
    d_kv[:, 0, :, lanes] = (
        mm_tn(low, stack_heads(query[:, lanes])).astype(bf16).reshape(4, 128, 128)
    )
    for by in (1, 2, 3):
        there = lax.rem(o.x + by, 4)
        remote(
            d_kv.at[there, :, :, lanes], d_kr.at[by - 1, :, :, lanes],
            send.at[i, by - 1], recv.at[i, by - 1], o.along_x(by),
        ).start()
    d_query[:, lanes] = join_pair(mm(low, key[:, lanes])).astype(bf16)
    for j in (0, 1):
        d_window[pl.ds(2 * i + j, 1), :] = diagonal_sums(d_scores[j * 128 : (j + 1) * 128], 640)


class Spread:
    def __init__(self, place, ref, send, recv):
        self.o, self.ref, self.send, self.recv = place, ref, send, recv

    def view(self, by, low, count):
        row = pl.multiple_of(lax.rem(self.o.x + by, 4) * 128, 128)
        return self.ref.at[pl.ds(row, 128), pl.ds(low, count)]

    def copy(self, n, by, low, count, to):
        view = self.view(by, low, count)
        return remote(view, view, self.send.at[n], self.recv.at[n], self.o.along_x(to))

    def start(self, part):
        self.copy(2 * part, 0, part * 768, 768, 1).start()
        self.copy(2 * part + 1, 0, part * 768, 768, 3).start()

    def forward(self):
        self.copy(0, 3, 0, 768, 1).wait_recv()
        self.copy(4, 3, 0, 768, 1).start()
        self.copy(3, 1, 768, 768, 3).wait_recv()
        self.copy(5, 1, 768, 768, 3).start()

    def finish(self):
        for n in (1, 2, 4, 5):
            self.copy(n, 0, 0, 768, 1).wait_recv()

    def drain(self):
        for n in range(6):
            self.copy(n, 0, 0, 768, 1).wait_send()


def pair_forward(i, query, kv, window, heads_out, weights):
    lanes = pl.ds(pl.multiple_of(i * 128, 128), 128)
    value_lanes = pl.ds(pl.multiple_of(i * 128 + 768, 128), 128)
    bias = jnp.concatenate([toeplitz(window[pl.ds(2 * i + j, 1), :], 128, 512) for j in (0, 1)], 0)
    scores = mm_nt(stack_heads(query[:, lanes]), kv[:, lanes]) + bias
    top = jnp.max(scores, -1, keepdims=True)
    raised = jnp.exp(scores - top)
    probability = raised / jnp.sum(raised, -1, keepdims=True)
    weights[pl.ds(2 * i, 2)] = probability.reshape(2, 128, 512)
    heads_out[:, lanes] = join_pair(mm(probability.astype(bf16), kv[:, value_lanes])).astype(bf16)


def layer_kernel(
    w_qkv, w_ao, w_in, w_out, pack, tokens, routes, buckets, cotangent,
    mixed, d_tokens, out_qkv, out_ao, out_in, out_out, small,
    stage, other, pair_sem, g_sends, g_recvs, side_in, side_arrivals, side_send, side_recv,
    g_qkv, g_ao, g_in, g_out, normed_ref, query, kv, kv_send, kv_recv, window, weights, heads_out,
    after_attn, moe_input, placing, probs, chosen, disp, inc, disp_send, disp_recv, sent, d_result,
    h_qkv, h_ao, h_in, h_out, sent_t, result, d_incoming, ret, back, d_query, d_kv, d_kr, d_window,
    d_heads_ref, d_after_ref, total_q, total_a, total_i, xs, xr, xa,
    pair_q, pair_a, pair_i, pair_o, far_q, far_a, far_i, far_o, near_q, near_a, near_i, near_o,
    side_q, side_a, side_i, side_o,
    sends, recvs, ret_send, ret_recv, dk_send, dk_recv, x_send, x_recv, last_send, last_recv,
    arrivals, small_send, small_recv,
):
    o = Place()
    o.barrier(True)
    flows = [
        Gather(o, ref, tall, g_sends.at[i], g_recvs.at[i], i)
        for i, (ref, tall) in enumerate(((g_qkv, 0), (g_ao, 0), (g_in, 0), (g_out, 1)))
    ]
    qkv, ao, win, wout = flows
    pair_copy = meet(o, (w_qkv, w_ao, w_in), stage, other, pair_sem)
    pair_copy.start()
    side = SmallSum(o, side_in, side_arrivals, side_send, side_recv, False)
    side_in[0] = place_small(o, pack)
    side.start(0)
    g_out[o.y, o.z, o.c] = w_out[...]
    pair_copy.wait_recv()
    at = 0
    for ref in (g_qkv, g_ao, g_in):
        n = ref.shape[-1]
        ref[o.c, o.y, o.z] = stage[:, at : at + n].astype(bf16)
        at += n
    qkv.ring_one()
    side.add(0)
    side.start(1)
    qkv.ring_one_far()
    qkv.ring_two()
    for f in (ao, win, wout):
        f.ring_one()
    side.add(1)
    side.start(2)
    x = tokens[...].astype(f32)
    r_one = lax.rsqrt(jnp.mean(x * x, -1, keepdims=True) + epsilon)
    bucket_row = buckets[:, pl.ds(pl.multiple_of((3 - o.x) * 128, 128), 640)]
    picks = jnp.where(
        jnp.broadcast_to(bucket_row, (128, 640)) == lax.broadcasted_iota(jnp.int32, (128, 640), 0), 1.0, 0.0
    )
    for f in (ao, win, wout):
        f.ring_one_far()
    qkv.ring_two_far()
    for f in (ao, win, wout):
        f.ring_two()
    side.add(2)
    small_in = side_in.at[3]
    normed_ref[...] = (x * r_one * small_in[0:1, :768]).astype(bf16)
    table_t = jnp.concatenate([small_in[:, 768:896], small_in[:, 896:1024]], 0)
    window[...] = mm(table_t.astype(bf16), picks.astype(bf16))
    qkv.last()
    ao.ring_two_far()
    qkv.finish()

    own_rows = pl.ds(pl.multiple_of(o.x * 128, 128), 128)
    spread = Spread(o, kv, kv_send, kv_recv)
    high = mm(normed_ref[...], g_qkv[1].reshape(768, 1152)).astype(bf16)
    kv[own_rows, 384:1536] = high
    spread.start(1)
    low = mm(normed_ref[...], g_qkv[0].reshape(768, 1152)).astype(bf16)
    kv[own_rows, 0:384] = low[:, 768:]
    spread.start(0)
    query[...] = low[:, :768]
    ao.last()
    win.ring_two_far()
    spread.forward()
    ao.finish()
    spread.finish()

    def ahead(i, carry):
        pair_forward(i, query, kv, window, heads_out, weights)
        return carry

    lax.fori_loop(0, 3, ahead, 0)
    win.last()
    lax.fori_loop(3, 6, ahead, 0)
    wout.ring_two_far()
    mixed_heads = heads_out[...]
    attn = x + jnp.concatenate([mm(mixed_heads, g_ao[h].reshape(768, 384)) for h in (0, 1)], 1)
    after_attn[...] = attn
    small8 = small_in[:, :768]
    r_two = lax.rsqrt(jnp.mean(attn * attn, -1, keepdims=True) + epsilon)
    moe_low = (attn * r_two * small8[1:2]).astype(bf16)
    moe_input[...] = moe_low
    logits = mm_nt(moe_low, small8.astype(bf16))
    lane = lax.broadcasted_iota(jnp.int32, (128, 8), 1)
    logits = jnp.where((lane >= 2) & (lane < 6), logits, -1e30)
    raised = jnp.exp(logits - jnp.max(logits, -1, keepdims=True))
    probability = raised / jnp.sum(raised, -1, keepdims=True)
    probs[...] = probability
    picked = jnp.where(lane == routes[...] + 2, 1.0, 0.0)
    chosen[...] = picked
    gate = jnp.sum(probability * picked, -1, keepdims=True)
    before = jnp.where(
        lax.broadcasted_iota(jnp.int32, (128, 128), 1) < lax.broadcasted_iota(jnp.int32, (128, 128), 0), 1.0, 0.0
    )
    slot = jnp.sum(mm(before.astype(bf16), picked.astype(bf16)) * picked, -1, keepdims=True)
    column = routes[...].astype(f32) * 48.0 + slot
    place = jnp.where(
        lax.broadcasted_iota(jnp.int32, (128, 192), 1).astype(f32) == column, 1.0, 0.0
    ).astype(bf16)
    placing[...] = place
    disp[:, 0] = mm_tn(place, moe_low).astype(bf16).reshape(4, 48, 768)
    d_combined = (gate * cotangent[...].astype(f32)).astype(bf16)
    disp[:, 1] = mm_tn(place, d_combined).astype(bf16).reshape(4, 48, 768)
    disp_copies = [
        remote(
            disp.at[lax.rem(o.x + by, 4)], inc.at[o.x], disp_send.at[by - 1], disp_recv.at[by - 1],
            o.along_x(by),
        )
        for by in (1, 2, 3)
    ]
    for copy in disp_copies:
        copy.start()
    inc[o.x] = disp[o.x]
    win.finish()
    wout.last()
    for copy in disp_copies:
        copy.wait_recv()
    sent[...] = inc[:, 0].reshape(192, 768)
    d_result[...] = inc[:, 1].reshape(192, 768)
    wout.finish()

    fq = Scatter(o, h_qkv, 0, pair_q, far_q, near_q, side_q, sends.at[0], recvs.at[0])
    fa = Scatter(o, h_ao, 0, pair_a, far_a, near_a, side_a, sends.at[1], recvs.at[1])
    fi = Scatter(o, h_in, 0, pair_i, far_i, near_i, side_i, sends.at[2], recvs.at[2])
    fo = Scatter(o, h_out, 1, pair_o, far_o, near_o, side_o, sends.at[3], recvs.at[3])
    tot = SmallSum(o, small, arrivals, small_send, small_recv, True)

    sent_t[...] = sent[...].astype(f32).T.astype(bf16)
    result[...] = jnp.zeros_like(result)
    d_incoming[...] = jnp.zeros_like(d_incoming)

    def chunk(j, carry):
        expert_chunk(j, sent, sent_t, d_result, g_in, g_out, h_in, h_out, result, d_incoming)
        return carry

    start = 4 * (1 - o.c)
    lax.fori_loop(start, start + 4, chunk, 0)
    fi.to_pair(0, 0, 4)
    fo.to_pair(0, 2 * (1 - o.c), 2)
    lax.fori_loop(4 - start, 8 - start, chunk, 0)
    fo.to_pair(1, 2 * o.c, 2)
    ret[:, 0] = result[...].astype(bf16).reshape(4, 48, 768)
    ret[:, 1] = d_incoming[...].astype(bf16).reshape(4, 48, 768)
    ret_copies = [
        remote(
            ret.at[lax.rem(o.x + by, 4)], back.at[o.x], ret_send.at[by - 1], ret_recv.at[by - 1],
            o.along_x(by),
        )
        for by in (1, 2, 3)
    ]
    for copy in ret_copies:
        copy.start()
    back[o.x] = ret[o.x]
    fi.from_pair(0, 4)
    fi.ring()
    for copy in ret_copies:
        copy.wait_recv()

    gain_one, gain_two = small8[0:1], small8[1:2]
    returned = mm(placing[...], back[:, 0].reshape(192, 768))
    d_moe = mm(placing[...], back[:, 1].reshape(192, 768))
    attn = after_attn[...]
    r_two = lax.rsqrt(jnp.mean(attn * attn, -1, keepdims=True) + epsilon)
    upstream = cotangent[...].astype(f32)
    gate = jnp.sum(probs[...] * chosen[...], -1, keepdims=True)
    mixed[...] = (attn + gate * returned).astype(bf16)
    d_gate = jnp.sum(upstream * returned, -1, keepdims=True)
    d_logits = probs[...] * (d_gate * chosen[...] - d_gate * gate)
    d_moe = d_moe + jnp.dot(d_logits, small8, precision=highest, preferred_element_type=f32)
    grad_router = lax.dot_general(
        d_logits, moe_input[...].astype(f32), TN, precision=highest, preferred_element_type=f32
    )
    d_after, grad_norm_two = rms_backward(attn, r_two, gain_two, d_moe)
    d_after = d_after + upstream
    d_after_ref[...] = d_after
    d_attn = d_after.astype(bf16)
    d_heads = jnp.zeros((128, 768), f32)
    for h in (0, 1):
        part = d_attn[:, h * 384 : (h + 1) * 384]
        h_ao[h] = mm_tn(heads_out[...], part).astype(bf16).reshape(4, 4, 48, 384)
        d_heads = d_heads + mm_nt(part, g_ao[h].reshape(768, 384))
    fa.to_pair(0, 0, 4)
    d_heads_ref[...] = d_heads.astype(bf16)
    fo.from_pair(0, 2)
    fo.from_pair(1, 2)
    fo.ring()

    d_window[...] = jnp.zeros_like(d_window)
    key, value = kv.at[:, pl.ds(0, 768)], kv.at[:, pl.ds(768, 768)]

    def pair(i, carry):
        pair_backward(
            o, i, query, key, value, weights, d_heads_ref, d_query, d_kv, d_kr, d_window, dk_send, dk_recv
        )
        return carry

    lax.fori_loop(0, 2, pair, 0)
    fi.ring_far()
    fa.from_pair(0, 4)
    fa.ring()
    lax.fori_loop(2, 4, pair, 0)
    fo.ring_far()
    fi.across()
    lax.fori_loop(4, 6, pair, 0)
    fa.ring_far()

    x = tokens[...].astype(f32)
    normed_t = normed_ref[...].astype(f32).T.astype(bf16)

    def project(h, d_part):
        h_qkv[h] = mm(normed_t, d_part).astype(bf16).reshape(4, 4, 48, 1152)
        return mm_nt(d_part, g_qkv[h].reshape(768, 1152))

    grad_table = lax.dot_general(
        d_window[...], picks, NT, precision=highest, preferred_element_type=f32
    )
    fo.across()
    for i in range(6):
        for by in (1, 2, 3):
            view = d_kr.at[by - 1, :, :, pl.ds(0, 128)]
            remote(view, view, dk_send.at[i, by - 1], dk_recv.at[i, by - 1], o.sibling()).wait_recv()
    d_own = d_kv[o.x].astype(f32)
    for by in (0, 1, 2):
        d_own = d_own + d_kr[by].astype(f32)
    d_own = d_own.astype(bf16)
    d_key, d_value = d_own[0], d_own[1]
    r_one = lax.rsqrt(jnp.mean(x * x, -1, keepdims=True) + epsilon)
    d_normed = project(0, jnp.concatenate([d_query[...], d_key[:, :384]], 1))
    d_normed = d_normed + project(1, jnp.concatenate([d_key[:, 384:], d_value], 1))
    fq.to_pair(0, 0, 4)
    d_resid, grad_norm_one = rms_backward(x, r_one, gain_one, d_normed)
    d_tokens[...] = (d_after_ref[...] + d_resid).astype(bf16)
    row = lax.broadcasted_iota(jnp.int32, (8, 768), 0)
    top = jnp.where(row == 0, grad_norm_one[None, :], jnp.where(row == 1, grad_norm_two[None, :], grad_router))
    small[0] = jnp.concatenate([top, grad_table[0:8], grad_table[8:16]], 1)
    tot.start(0)
    fa.across()
    fq.from_pair(0, 4)
    fq.ring()
    tot.add(0)
    tot.start(1)
    out_out[...] = fo.total()

    def hand(k, total, out, value):
        n = value.shape[1]
        total[...] = value
        mine = pl.ds(pl.multiple_of(o.c * n, 128), n)
        out[:, mine] = total[pl.ds(pl.multiple_of(24 * o.c, 8), 24), :]
        copy = remote(
            total.at[pl.ds(pl.multiple_of(24 * (1 - o.c), 8), 24)], out.at[:, mine],
            last_send.at[k], last_recv.at[k], o.sibling(),
        )
        copy.start()
        return copy

    last = [hand(0, total_i, out_in, fi.total())]
    total_a[...] = fa.total()
    tot.add(1)
    tot.start(2)
    fq.ring_far()
    fq.across()
    tot.add(2)
    tot.start(3)
    dense = jnp.concatenate([fq.total(), total_a[...]], 1).astype(bf16)
    for j in range(4):
        xs[j] = dense[:, j * 384 : (j + 1) * 384]
    first = [
        remote(xs.at[lax.rem(o.x + by, 4)], xr.at[by - 1], x_send.at[by - 1], x_recv.at[by - 1], o.along_x(by))
        for by in (1, 2, 3)
    ]
    for copy in first:
        copy.start()
    for copy in first:
        copy.wait_recv()
    own = xs[o.x].astype(f32)
    for j in range(3):
        own = own + xr[j].astype(f32)
    xa[o.x] = own.astype(bf16)
    second = [
        remote(xa.at[o.x], xa.at[o.x], x_send.at[by + 2], x_recv.at[by + 2], o.along_x(by)) for by in (1, 2, 3)
    ]
    for copy in second:
        copy.start()
    for copy in second:
        copy.wait_recv()
    whole = jnp.concatenate([xa[0], xa[1], xa[2], xa[3]], 1).astype(f32)
    last.append(hand(1, total_q, out_qkv, whole[:, :1152]))
    last.append(hand(2, total_a, out_ao, whole[:, 1152:]))
    tot.add(3)
    for copy in last:
        copy.wait_recv()
    for copy in ret_copies + first + second + last:
        copy.wait_send()
    for i in range(6):
        for by in (1, 2, 3):
            view = d_kr.at[by - 1, :, :, pl.ds(0, 128)]
            remote(view, view, dk_send.at[i, by - 1], dk_recv.at[i, by - 1], o.sibling()).wait_send()
    tot.drain()
    for f in (fq, fa, fi):
        f.drain([(0, 4)])
    fo.drain([(0, 2), (1, 2)])
    pair_copy.wait_send()
    side.drain()
    spread.drain()
    for copy in disp_copies:
        copy.wait_send()
    for f in flows:
        f.drain()


def layer(*operands):
    vm = pl.BlockSpec(memory_space=pltpu.VMEM)
    dma = pltpu.SemaphoreType.DMA

    def low(*shape):
        return pltpu.VMEM(shape, bf16)

    def full(*shape):
        return pltpu.VMEM(shape, f32)

    sizes = ((48, 1152), (48, 384), (48, 1536), (96, 768))
    weights = (low(2, 4, 4, 48, 1152), low(2, 4, 4, 48, 384), low(2, 4, 4, 48, 1536), low(4, 4, 2, 96, 768))
    return pl.pallas_call(
        layer_kernel,
        in_specs=[vm] * len(operands),
        out_specs=[vm] * 7,
        out_shape=[
            jax.ShapeDtypeStruct((128, 768), bf16),
            jax.ShapeDtypeStruct((128, 768), bf16),
            jax.ShapeDtypeStruct((24, 2304), f32),
            jax.ShapeDtypeStruct((24, 768), f32),
            jax.ShapeDtypeStruct((24, 3072), f32),
            jax.ShapeDtypeStruct((96, 768), f32),
            jax.ShapeDtypeStruct((5, 8, 1024), f32),
        ],
        scratch_shapes=[
            full(48, 3072), full(24, 3072), dma((2,)), dma((4, 11)), dma((4, 11)),
            full(4, 8, 1024), full(7, 8, 1024), dma((7,)), dma((7,)),
            *weights, low(128, 768), low(128, 768), low(512, 1536), dma((6,)), dma((6,)), full(16, 640),
            full(12, 128, 512), low(128, 768), full(128, 768), low(128, 768), low(128, 192),
            full(128, 8), full(128, 8), low(4, 2, 48, 768), low(4, 2, 48, 768), dma((3,)), dma((3,)),
            low(192, 768), low(192, 768),
            *weights,
            low(768, 192), full(192, 768), full(192, 768), low(4, 2, 48, 768), low(4, 2, 48, 768),
            low(128, 768), low(4, 2, 128, 768), low(3, 2, 128, 768), full(16, 640),
            low(128, 768), full(128, 768), full(48, 1152), full(48, 384), full(48, 1536),
            low(4, 48, 384), low(3, 48, 384), low(4, 48, 384),
            *[low(4, 4, *s) for s in sizes],
            *[low(2, 2, *s) for s in sizes],
            *[low(2, 4, *s) for s in sizes],
            *[low(3, *s) for s in sizes],
            dma((4, 11)), dma((4, 11)), dma((3,)), dma((3,)), dma((6, 3)), dma((6, 3)),
            dma((6,)), dma((6,)), dma((3,)), dma((3,)),
            full(10, 8, 1024), dma((10,)), dma((10,)),
        ],
        compiler_params=pltpu.CompilerParams(
            collective_id=0, has_side_effects=True, vmem_limit_bytes=62 * 2**20
        ),
    )(*operands)


def per_device(
    tokens, norm_attn, w_qkv, w_attn_out, bias_table, norm_moe, router, w_in, w_out, routes, buckets, cotangent
):
    dp = lax.axis_index("dp")
    own = norm_attn.shape[0]
    pack = jnp.concatenate([norm_attn[:, None], norm_moe[:, None], router, jnp.zeros((own, 122), bf16)], 1)
    last = jnp.concatenate([jnp.zeros((1, 8), bf16), bias_table, jnp.zeros((1, 108), bf16)], 1)
    pack = jnp.concatenate([pack, last, jnp.zeros((7, 128), bf16)], 0)
    padded = jnp.concatenate([buckets, jnp.zeros((1,), jnp.int32)])[None, :]
    mixed, d_tokens, out_qkv, out_ao, out_in, out_out, small = layer(
        w_qkv, w_attn_out, w_in[:, 0], w_out[:, 0], pack, tokens, routes, padded, cotangent
    )
    small = small[4]
    mine = lax.dynamic_slice(small, (0, dp * own), (8, own))
    table_col = jnp.concatenate(
        [
            lax.dynamic_slice(small, (0, 768 + dp), (8, 1)),
            lax.dynamic_slice(small, (0, 896 + dp), (4, 1)),
        ],
        0,
    )
    return (
        mixed, d_tokens, mine[0], out_qkv, out_ao, table_col.T, mine[1], mine[2:6].T,
        out_in[:, None], out_out[:, None],
    )


def solution(mesh):
    both = ("dp", "expert")
    in_specs = (
        P(both, None), P("dp"), P("dp", None), P("dp", None), P("dp", None), P("dp"), P("dp", None),
        P("dp", "expert", None), P("dp", "expert", None), P(both, None), P(), P(both, None),
    )
    out_specs = (
        P(both, None), P(both, None), P("dp"), P("dp", None), P("dp", None), P("dp", None), P("dp"),
        P("dp", None), P("dp", "expert", None), P("dp", "expert", None),
    )
    return jax.shard_map(
        per_device, mesh=mesh, in_specs=in_specs, out_specs=out_specs, check_vma=False
    )
```

```python
import jax
import jax.numpy as jnp
from jax import lax
from jax.experimental import pallas as pl
from jax.experimental.pallas import tpu as pltpu
from jax.sharding import PartitionSpec as P

epsilon = 1e-06
highest = lax.Precision.HIGHEST
bf16 = jnp.bfloat16
f32 = jnp.float32
NT = (((1,), (1,)), ((), ()))
TN = (((0,), (0,)), ((), ()))


def mm(a, b):
    return jnp.dot(a, b, preferred_element_type=f32)


def mm_nt(a, b):
    return lax.dot_general(a, b, NT, preferred_element_type=f32)


def mm_tn(a, b):
    return lax.dot_general(a, b, TN, preferred_element_type=f32)


def stack_heads(pair):
    left = lax.broadcasted_iota(jnp.int32, pair.shape, 1) < 64
    zero = jnp.zeros_like(pair)
    return jnp.concatenate([jnp.where(left, pair, zero), jnp.where(left, zero, pair)], 0)


def join_pair(stacked):
    rows = stacked.shape[0] // 2
    left = lax.broadcasted_iota(jnp.int32, (rows, 128), 1) < 64
    return jnp.where(left, stacked[:rows], stacked[rows:])


def toeplitz(window_row, rows, keys):
    width = window_row.shape[1]
    wide = jnp.broadcast_to(window_row, (rows, width))
    rolled = pltpu.roll(wide, width - (rows - 1), 1, stride=1, stride_axis=0)
    return rolled[:, :keys]


def diagonal_sums(block, width):
    rows, keys = block.shape
    wide = jnp.concatenate([block, jnp.zeros((rows, width - keys), f32)], 1)
    half = rows // 2
    while half >= 8:
        wide = wide[:half] + pltpu.roll(wide[half:], width - half, 1)
        half //= 2
    row = lax.broadcasted_iota(jnp.int32, wide.shape, 0)
    for bit in (1, 2, 4):
        wide = jnp.where((row & bit) != 0, pltpu.roll(wide, width - bit, 1), wide)
    total = jnp.sum(wide, 0, keepdims=True)
    return pltpu.roll(total, rows - 1, 1)


def rms_forward(values, gain):
    r = lax.rsqrt(jnp.mean(values * values, -1, keepdims=True) + epsilon)
    return r, values * r * gain


def rms_backward(values, r, gain, grad):
    u = grad * gain
    d_values = r * u - values * (r * r * r) * jnp.mean(u * values, -1, keepdims=True)
    return d_values, jnp.sum(grad * values * r, 0)


MESH = pl.DeviceIdType.MESH


class Place:
    def __init__(self):
        d = lax.axis_index("dp")
        self.d = d
        self.x = lax.axis_index("expert")
        self.c = lax.rem(d, 2)
        self.z = lax.rem(lax.div(d, 2), 4)
        self.y = lax.div(d, 8)
        self.p = self.z * (1 - self.c) + self.y * self.c
        self.q = self.y * (1 - self.c) + self.z * self.c

    def at(self, p, q):
        y = q * (1 - self.c) + p * self.c
        z = p * (1 - self.c) + q * self.c
        return ((y * 4 + z) * 2 + self.c, self.x)

    def along_p(self, by):
        return self.at(lax.rem(self.p + by, 4), self.q)

    def along_q(self, by):
        return self.at(self.p, lax.rem(self.q + by, 4))

    def along_x(self, by):
        return (self.d, lax.rem(self.x + by, 4))

    def sibling(self):
        return (self.d + 1 - 2 * self.c, self.x)

    def each_core(self, body):
        pl.when(self.c == 0)(lambda: body(0))
        pl.when(self.c == 1)(lambda: body(1))

    def barrier(self, with_x):
        peers = [self.sibling()] + [self.along_p(i) for i in (1, 2, 3)]
        peers += [self.along_q(i) for i in (1, 2, 3)]
        if with_x:
            peers += [self.along_x(i) for i in (1, 2, 3)]
        sem = pltpu.get_barrier_semaphore()
        for peer in peers:
            pl.semaphore_signal(sem, inc=1, device_id=peer, device_id_type=MESH)
        return lambda: pl.semaphore_wait(sem, len(peers))


def remote(src, dst, send, recv, to):
    return pltpu.make_async_remote_copy(
        src_ref=src, dst_ref=dst, send_sem=send, recv_sem=recv, device_id=to, device_id_type=MESH
    )


def block_of(ref, tall, k, p, q):
    y, z = (q, p) if k == 0 else (p, q)
    return ref.at[y, z, k] if tall else ref.at[k, y, z]


def slab_of(ref, tall, k, q, low=0, count=4):
    y, z = (q, pl.ds(low, count)) if k == 0 else (pl.ds(low, count), q)
    return ref.at[y, z, k] if tall else ref.at[k, y, z]


class Gather:
    sends = 11
    recvs = 11

    def __init__(self, place, ref, tall, send, recv, number):
        self.o, self.ref, self.tall, self.send, self.recv = place, ref, tall, send, recv
        self.number = number

    def block(self, k, by):
        return block_of(self.ref, self.tall, k, lax.rem(self.o.p + by, 4), self.o.q)

    def slab(self, k, by, low=0, count=4):
        return slab_of(self.ref, self.tall, k, lax.rem(self.o.q + by, 4), low, count)

    def go(self, part, s, r, to):
        def body(k):
            src = part(k)
            remote(src, src, self.send.at[s], self.recv.at[r], to).start()

        self.o.each_core(body)

    def arrived(self, r, count):
        if count == 1:
            view = block_of(self.ref, self.tall, 0, 0, 0)
        else:
            view = slab_of(self.ref, self.tall, 0, 0, 0, count)
        remote(view, view, self.send.at[0], self.recv.at[r], self.o.sibling()).wait_recv()

    def sent(self, s, count):
        if count == 1:
            view = block_of(self.ref, self.tall, 0, 0, 0)
        else:
            view = slab_of(self.ref, self.tall, 0, 0, 0, count)
        remote(view, view, self.send.at[s], self.recv.at[0], self.o.sibling()).wait_send()

    def ring_one(self):
        self.go(lambda k: self.block(k, 0), 0, 0, self.o.along_p(1))
        self.go(lambda k: self.block(k, 0), 1, 1, self.o.along_p(3))
        if self.number == 0:
            self.go(lambda k: self.block(k, 0), 2, 2, self.o.along_p(2))

    def ring_one_far(self):
        self.arrived(0, 1)
        self.arrived(1, 1)
        if self.number == 0:
            return
        if self.number % 2 == 0:
            self.go(lambda k: self.block(k, 3), 2, 2, self.o.along_p(1))
        else:
            self.go(lambda k: self.block(k, 1), 2, 2, self.o.along_p(3))

    def ring_two(self):
        self.arrived(2, 1)
        self.go(lambda k: self.slab(k, 0), 3, 3, self.o.along_q(1))
        self.go(lambda k: self.slab(k, 0), 4, 4, self.o.along_q(3))
        self.go(lambda k: self.slab(k, 0), 7, 7, self.o.sibling())

    def ring_two_far(self):
        self.arrived(3, 4)
        self.go(lambda k: self.slab(k, 3, 0, 2), 5, 5, self.o.along_q(1))
        self.arrived(4, 4)
        self.go(lambda k: self.slab(k, 1, 2, 2), 6, 6, self.o.along_q(3))
        self.go(lambda k: self.slab(k, 3), 8, 8, self.o.sibling())
        self.go(lambda k: self.slab(k, 1), 9, 9, self.o.sibling())

    def last(self):
        self.arrived(5, 2)
        self.arrived(6, 2)
        self.go(lambda k: self.slab(k, 2), 10, 10, self.o.sibling())

    def finish(self):
        for r in (7, 8, 9, 10):
            self.arrived(r, 4)

    def drain(self):
        for s, count in ((0, 1), (1, 1), (2, 1), (3, 4), (4, 4), (5, 2), (6, 2), (7, 4), (8, 4), (9, 4), (10, 4)):
            self.sent(s, count)


class SmallSum:
    def __init__(self, place, value, arrivals, send, recv, with_x):
        self.o, self.value, self.arrivals, self.send, self.recv = place, value, arrivals, send, recv
        o = place
        self.steps = [[o.sibling()], [o.along_p(i) for i in (1, 2, 3)], [o.along_q(i) for i in (1, 2, 3)]]
        if with_x:
            self.steps.append([o.along_x(i) for i in (1, 2, 3)])
        self.copies = []
        n = 0
        for s, peers in enumerate(self.steps):
            row = []
            for peer in peers:
                row.append(
                    remote(value.at[s], arrivals.at[n], send.at[n], recv.at[n], peer)
                )
                n += 1
            self.copies.append(row)

    def start(self, s):
        for copy in self.copies[s]:
            copy.start()

    def add(self, s):
        first = sum(len(row) for row in self.copies[:s])
        total = self.value[s]
        for i, copy in enumerate(self.copies[s]):
            copy.wait_recv()
            total = total + self.arrivals[first + i]
        self.value[s + 1] = total

    def drain(self):
        for row in self.copies:
            for copy in row:
                copy.wait_send()


def place_small(o, out, na, nm, router_t, table):
    row = lax.broadcasted_iota(jnp.int32, (24, 768), 0)
    lane = lax.broadcasted_iota(jnp.int32, (24, 768), 1)
    hit = jnp.where(lane == 24 * o.d + row, 1.0, 0.0)
    out[...] = jnp.zeros((8, 1024), f32)
    out[0:1, 0:768] = mm(na[...].astype(f32), hit)
    out[1:2, 0:768] = mm(nm[...].astype(f32), hit)
    out[2:6, 0:768] = mm(router_t[...].astype(f32), hit)
    head = lax.broadcasted_iota(jnp.int32, (16, 12), 0) == lax.broadcasted_iota(jnp.int32, (16, 12), 1)
    wide = jnp.broadcast_to(table[...].astype(f32), (16, 12))
    column = jnp.sum(jnp.where(head, wide, 0.0), -1, keepdims=True)
    own = lax.broadcasted_iota(jnp.int32, (16, 128), 1) == o.d
    placed = jnp.where(own, jnp.broadcast_to(column, (16, 128)), 0.0)
    out[:, 768:896] = placed[0:8]
    out[:, 896:1024] = placed[8:16]


def meet(o, halves, stage, other, sem):
    at = 0
    for ref in halves:
        n = ref.shape[1] // 2
        own = pl.ds(pl.multiple_of(o.c * n, 128), n)
        theirs = pl.ds(pl.multiple_of((1 - o.c) * n, 128), n)
        stage[pl.ds(pl.multiple_of(24 * o.c, 8), 24), at : at + n] = ref[:, own].astype(f32)
        other[:, at : at + n] = ref[:, theirs].astype(f32)
        at += n
    return remote(
        other, stage.at[pl.ds(pl.multiple_of(24 * o.c, 8), 24)], sem.at[0], sem.at[1], o.sibling()
    )


class Scatter:
    def __init__(self, place, ref, tall, pair, far, near, side, send, recv):
        self.o, self.ref, self.tall = place, ref, tall
        self.pair, self.far, self.near, self.side = pair, far, near, side
        self.send, self.recv = send, recv

    def where(self, p, q):
        o = self.o
        return q * (1 - o.c) + p * o.c, p * (1 - o.c) + q * o.c

    def q_at(self, by):
        return lax.rem(self.o.q + by, 4)

    def own(self, p, q):
        y, z = self.where(p, q)
        return (y, z, self.o.c) if self.tall else (self.o.c, y, z)

    def to_pair(self, s, low, count):
        rows = pl.ds(low, count)
        theirs = 1 - self.o.c
        src = self.ref.at[rows, :, theirs] if self.tall else self.ref.at[theirs, rows]
        remote(src, self.pair.at[rows], self.send.at[s], self.recv.at[s], self.o.sibling()).start()

    def from_pair(self, s, count):
        view = self.pair.at[pl.ds(0, count)]
        remote(view, view, self.send.at[s], self.recv.at[s], self.o.sibling()).wait_recv()

    def add_pair(self, by):
        q = self.q_at(by)

        def body(p, carry):
            y, z = self.where(p, q)
            at = self.own(p, q)
            self.ref[at] = (self.ref[at].astype(f32) + self.pair[y, z].astype(f32)).astype(bf16)
            return carry

        lax.fori_loop(0, 4, body, 0)

    def go(self, s, by, low, dst, to):
        def body(k):
            src = slab_of(self.ref, self.tall, k, self.q_at(by), low, 2)
            remote(src, dst, self.send.at[s], self.recv.at[s], to).start()

        self.o.each_core(body)

    def ring(self):
        o = self.o
        self.add_pair(2)
        self.go(2, 2, 0, self.far.at[0], o.along_q(1))
        self.go(3, 2, 2, self.far.at[1], o.along_q(3))
        self.add_pair(1)
        self.go(4, 1, 2, self.near.at[0, pl.ds(2, 2)], o.along_q(1))
        self.add_pair(3)
        self.go(5, 3, 0, self.near.at[1, pl.ds(0, 2)], o.along_q(3))
        self.add_pair(0)

    def landed(self, s, view):
        remote(view, view, self.send.at[s], self.recv.at[s], self.o.sibling()).wait_recv()

    def add_far(self, i, by, low):
        q = self.q_at(by)

        def body(j, carry):
            at = self.own(low + j, q)
            self.ref[at] = (self.ref[at].astype(f32) + self.far[i, j].astype(f32)).astype(bf16)
            return carry

        lax.fori_loop(0, 2, body, 0)

    def ring_far(self):
        o = self.o
        self.landed(2, self.far.at[0])
        self.add_far(0, 1, 0)
        self.go(6, 1, 0, self.near.at[0, pl.ds(0, 2)], o.along_q(1))
        self.landed(3, self.far.at[1])
        self.add_far(1, 3, 2)
        self.go(7, 3, 2, self.near.at[1, pl.ds(2, 2)], o.along_q(3))

    def across(self):
        o = self.o
        half = self.near.at[0, pl.ds(0, 2)]
        for s in (4, 5, 6, 7):
            self.landed(s, half)

        def body(p, carry):
            at = self.own(p, o.q)
            total = self.ref[at].astype(f32) + self.near[0, p].astype(f32)
            self.ref[at] = (total + self.near[1, p].astype(f32)).astype(bf16)
            return carry

        lax.fori_loop(0, 4, body, 0)
        for i in (1, 2, 3):
            src = self.ref.at[self.own(lax.rem(o.p + i, 4), o.q)]
            remote(
                src, self.side.at[i - 1], self.send.at[7 + i], self.recv.at[7 + i], o.along_p(i)
            ).start()

    def total(self):
        o = self.o
        for i in (0, 1, 2):
            self.landed(8 + i, self.side.at[i])
        total = self.ref[self.own(o.p, o.q)].astype(f32)
        for i in (0, 1, 2):
            total = total + self.side[i].astype(f32)
        return total

    def sent(self, s, view):
        remote(view, view, self.send.at[s], self.recv.at[s], self.o.sibling()).wait_send()

    def drain(self, pair_parts):
        for s, count in pair_parts:
            self.sent(s, self.pair.at[pl.ds(0, count)])
        for s in range(2, 8):
            self.sent(s, self.far.at[0])
        for s in range(8, 11):
            self.sent(s, self.side.at[0])


SQ = 0.7978845608028654


def gelu_both(h):
    t = jnp.tanh(SQ * (h + 0.044715 * (h * h * h)))
    value = 0.5 * h * (1.0 + t)
    slope = 0.5 * (1.0 + t) + 0.5 * h * (1.0 - t * t) * (SQ * (1.0 + 3 * 0.044715 * (h * h)))
    return value, slope


def hidden_lanes(j):
    return lax.div(j, 2), pl.ds(pl.multiple_of(lax.rem(j, 2) * 768, 128), 768)


def expert_hidden(j, sent, g_in, acts, slopes):
    half, at = hidden_lanes(j)
    value, slope = gelu_both(mm(sent[...], g_in[half, :, :, :, at].reshape(768, 768)))
    acts[j] = value.astype(bf16)
    slopes[j] = slope.astype(bf16)


def expert_second_grad(j, d_result, acts, h_out):
    for r in (0, 1):
        part = acts[j, :, r * 384 : (r + 1) * 384]
        h_out[j, pl.ds(2 * r, 2)] = mm_tn(part, d_result[...]).astype(bf16).reshape(2, 2, 96, 768)


def expert_result(j, acts, g_out, result):
    result[...] += mm(acts[j], g_out[j].reshape(768, 768))


def expert_back(j, sent_t, d_result, slopes, g_in, g_out, h_in, d_incoming):
    half, at = hidden_lanes(j)
    d_act = mm_nt(d_result[...], g_out[j].reshape(768, 768))
    d_hidden = (d_act * slopes[j].astype(f32)).astype(bf16)
    for r in (0, 1):
        part = sent_t[r * 384 : (r + 1) * 384]
        h_in[half, pl.ds(2 * r, 2), :, :, at] = mm(part, d_hidden).astype(bf16).reshape(2, 4, 48, 768)
    d_incoming[...] += mm_nt(d_hidden, g_in[half, :, :, :, at].reshape(768, 768))


def pair_backward(i, query, kv, weights, d_heads, d_query, d_kv, d_window):
    lanes = pl.ds(pl.multiple_of(i * 128, 128), 128)
    value_lanes = pl.ds(pl.multiple_of(i * 128 + 768, 128), 128)
    kept = weights[pl.ds(2 * i, 2)].reshape(256, 512)
    probability = kept.astype(f32)
    d_stack = stack_heads(d_heads[:, lanes])
    d_weights = mm_nt(d_stack, kv[:, value_lanes])
    d_kv[:, value_lanes] = mm_tn(kept, d_stack).astype(bf16)
    d_scores = probability * (d_weights - jnp.sum(probability * d_weights, -1, keepdims=True))
    low = d_scores.astype(bf16)
    d_kv[:, lanes] = mm_tn(low, stack_heads(query[:, lanes])).astype(bf16)
    d_query[:, lanes] = join_pair(mm(low, kv[:, lanes])).astype(bf16)
    for j in (0, 1):
        d_window[pl.ds(2 * i + j, 1), :] = diagonal_sums(d_scores[j * 128 : (j + 1) * 128], 640)


def pair_forward(i, query, kv, window, heads_out, weights):
    lanes = pl.ds(pl.multiple_of(i * 128, 128), 128)
    value_lanes = pl.ds(pl.multiple_of(i * 128 + 768, 128), 128)
    bias = jnp.concatenate([toeplitz(window[pl.ds(2 * i + j, 1), :], 128, 512) for j in (0, 1)], 0)
    scores = mm_nt(stack_heads(query[:, lanes]), kv[:, lanes]) + bias
    top = jnp.max(scores, -1, keepdims=True)
    raised = jnp.exp(scores - top)
    probability = raised / jnp.sum(raised, -1, keepdims=True)
    low = probability.astype(bf16)
    weights[pl.ds(2 * i, 2)] = low.reshape(2, 128, 512)
    heads_out[:, lanes] = join_pair(mm(low, kv[:, value_lanes])).astype(bf16)


def layer_kernel(
    w_qkv, w_ao, w_in, w_out, na, nm, router_t, table, tokens, routes, bucket_list, cotangent,
    mixed, d_tokens, out_qkv, out_ao, out_in, out_out, own_small,
    small, buckets, stage, other, pair_sem, g_sends, g_recvs, side_in, side_arrivals, side_send, side_recv,
    g_qkv, g_ao, g_in, g_out, whole_tokens, tok_send, tok_recv, normed_ref, normed_t, query, kv, window, weights, heads_out,
    after_attn, moe_input, placing, probs, chosen, disp, inc, disp_send, disp_recv, sent, d_result, acts, slopes,
    h_qkv, h_ao, h_in, h_out, sent_t, result, back, d_kv, dn_in, d_window,
    xs, xr, xa,
    pair_a, pair_i, pair_o, far_q, far_a, far_i, far_o, near_q, near_a, near_i, near_o,
    side_q, side_a, side_i, side_o,
    sends, recvs, ret_send, ret_recv, dn_send, dn_recv, x_send, x_recv, last_send, last_recv,
    arrivals, small_send, small_recv,
):
    d_heads_ref, d_after_ref, d_query = heads_out, after_attn, query
    o = Place()
    entered = o.barrier(True)
    flows = [
        Gather(o, ref, tall, g_sends.at[i], g_recvs.at[i], i)
        for i, (ref, tall) in enumerate(((g_qkv, 0), (g_ao, 0), (g_in, 0), (g_out, 1)))
    ]
    qkv, ao, win, wout = flows
    pair_copy = meet(o, (w_qkv, w_ao, w_in), stage, other, pair_sem)
    side = SmallSum(o, side_in, side_arrivals, side_send, side_recv, False)
    place_small(o, side_in.at[0], na, nm, router_t, table)
    buckets[...] = jnp.zeros_like(buckets)
    buckets[:, 0:1023] = bucket_list[...]
    g_out[o.y, o.z, o.c] = w_out[...]
    own_rows = pl.ds(pl.multiple_of(o.x * 128, 128), 128)
    whole_tokens[own_rows] = tokens[...]
    entered()
    pair_copy.start()
    side.start(0)
    wout.ring_one()
    pair_copy.wait_recv()
    at = 0
    for ref in (g_qkv, g_ao, g_in):
        n = ref.shape[-1]
        ref[o.c, o.y, o.z] = stage[:, at : at + n].astype(bf16)
        at += n
    qkv.ring_one()
    side.add(0)
    side.start(1)
    ao.ring_one()
    win.ring_one()
    tok_copies = [
        remote(
            whole_tokens.at[own_rows], whole_tokens.at[own_rows], tok_send.at[by - 1], tok_recv.at[by - 1],
            o.along_x(by),
        )
        for by in (1, 2, 3)
    ]
    for copy in tok_copies:
        copy.start()
    qkv.ring_one_far()
    qkv.ring_two()
    for f in (wout, ao, win):
        f.ring_one_far()
    side.add(1)
    side.start(2)
    x = tokens[...].astype(f32)
    bucket_row = buckets[:, pl.ds(pl.multiple_of((3 - o.x) * 128, 128), 640)]
    picks = jnp.where(
        jnp.broadcast_to(bucket_row, (128, 640)) == lax.broadcasted_iota(jnp.int32, (128, 640), 0), 1.0, 0.0
    )
    qkv.ring_two_far()
    for f in (ao, win, wout):
        f.ring_two()
    for copy in tok_copies:
        copy.wait_recv()
    side.add(2)
    small_in = side_in.at[3]
    gain_row = small_in[0:1, :768]

    def norm_rows(n, carry):
        rows = pl.ds(n * 128, 128)
        _, normed = rms_forward(whole_tokens[rows].astype(f32), gain_row)
        normed_ref[rows] = normed.astype(bf16)
        normed_t[:, rows] = normed.T.astype(bf16)
        return carry

    for n in range(4):
        norm_rows(n, 0)
    table_t = jnp.concatenate([small_in[:, 768:896], small_in[:, 896:1024]], 0)
    window[...] = mm(table_t.astype(bf16), picks.astype(bf16))
    qkv.last()
    ao.ring_two_far()
    qkv.finish()

    query[...] = mm(normed_ref[own_rows], g_qkv[0, :, :, :, 0:768].reshape(768, 768)).astype(bf16)

    def project_rows(n, carry):
        rows = pl.ds(pl.multiple_of(n * 128, 128), 128)
        block = normed_ref[rows]
        kv[rows, 0:384] = mm(block, g_qkv[0, :, :, :, 768:1152].reshape(768, 384)).astype(bf16)
        kv[rows, 384:1536] = mm(block, g_qkv[1].reshape(768, 1152)).astype(bf16)
        return carry

    lax.fori_loop(0, 4, project_rows, 0)
    ao.last()

    def ahead(i, carry):
        pair_forward(i, query, kv, window, heads_out, weights)
        return carry

    lax.fori_loop(0, 3, ahead, 0)
    win.ring_two_far()
    lax.fori_loop(3, 6, ahead, 0)
    ao.finish()
    mixed_heads = heads_out[...]
    attn = x + jnp.concatenate([mm(mixed_heads, g_ao[h].reshape(768, 384)) for h in (0, 1)], 1)
    after_attn[...] = attn
    small8 = small_in[:, :768]
    r_two = lax.rsqrt(jnp.mean(attn * attn, -1, keepdims=True) + epsilon)
    moe_low = (attn * r_two * small8[1:2]).astype(bf16)
    moe_input[...] = moe_low
    logits = mm_nt(moe_low, small8.astype(bf16))
    lane = lax.broadcasted_iota(jnp.int32, (128, 8), 1)
    logits = jnp.where((lane >= 2) & (lane < 6), logits, -1e30)
    raised = jnp.exp(logits - jnp.max(logits, -1, keepdims=True))
    probability = raised / jnp.sum(raised, -1, keepdims=True)
    probs[...] = probability
    named = jnp.broadcast_to(routes[...], (8, 128)) + 2
    picked = jnp.where(lax.broadcasted_iota(jnp.int32, (8, 128), 0) == named, 1.0, 0.0).T
    chosen[...] = picked
    gate = jnp.sum(probability * picked, -1, keepdims=True)
    before = jnp.where(
        lax.broadcasted_iota(jnp.int32, (128, 128), 1) < lax.broadcasted_iota(jnp.int32, (128, 128), 0), 1.0, 0.0
    )
    slot = jnp.sum(mm(before.astype(bf16), picked.astype(bf16)) * picked, -1, keepdims=True)
    column = jnp.sum(picked * ((lane - 2) * 48).astype(f32), -1, keepdims=True) + slot
    place = jnp.where(
        lax.broadcasted_iota(jnp.int32, (128, 192), 1).astype(f32) == column, 1.0, 0.0
    ).astype(bf16)
    placing[...] = place
    def dispatch(part, value):
        disp[part] = mm_tn(place, value).astype(bf16).reshape(4, 48, 768)
        copies = [
            remote(
                disp.at[part, lax.rem(o.x + by, 4)], inc.at[part, o.x],
                disp_send.at[part, by - 1], disp_recv.at[part, by - 1], o.along_x(by),
            )
            for by in (1, 2, 3)
        ]
        for copy in copies:
            copy.start()
        inc[part, o.x] = disp[part, o.x]
        return copies

    tokens_out = dispatch(0, moe_low)
    grads_out = dispatch(1, (gate * cotangent[...].astype(f32)).astype(bf16))
    win.last()
    wout.ring_two_far()
    for copy in tokens_out:
        copy.wait_recv()
    sent[...] = inc[0].reshape(192, 768)
    sent_t[...] = sent[...].astype(f32).T.astype(bf16)
    win.finish()
    pair_q = pair_i.at[:, :, :, pl.ds(0, 1152)]
    fq = Scatter(o, h_qkv, 0, pair_q, far_q, near_q, side_q, sends.at[0], recvs.at[0])
    fa = Scatter(o, h_ao, 0, pair_a, far_a, near_a, side_a, sends.at[1], recvs.at[1])
    fi = Scatter(o, h_in, 0, pair_i, far_i, near_i, side_i, sends.at[2], recvs.at[2])
    fo = Scatter(o, h_out, 1, pair_o, far_o, near_o, side_o, sends.at[3], recvs.at[3])
    tot = SmallSum(o, small, arrivals, small_send, small_recv, True)

    def times(low, high, body):
        def step(j, carry):
            body(j)
            return carry

        lax.fori_loop(low, high, step, 0)

    times(0, 4, lambda j: expert_hidden(j, sent, g_in, acts, slopes))
    wout.last()
    for copy in grads_out:
        copy.wait_recv()
    d_result[...] = inc[1].reshape(192, 768)
    times(0, 4, lambda j: expert_second_grad(j, d_result, acts, h_out))
    fo.to_pair(0, 0, 4)
    wout.finish()
    result[...] = jnp.zeros_like(result)
    times(0, 4, lambda j: expert_result(j, acts, g_out, result))

    def send_back(part, value):
        for copy in (tokens_out, grads_out)[part]:
            copy.wait_send()
        ret = disp
        ret[part] = value.astype(bf16).reshape(4, 48, 768)
        copies = [
            remote(
                ret.at[part, lax.rem(o.x + by, 4)], back.at[part, o.x],
                ret_send.at[part, by - 1], ret_recv.at[part, by - 1], o.along_x(by),
            )
            for by in (1, 2, 3)
        ]
        for copy in copies:
            copy.start()
        back[part, o.x] = ret[part, o.x]
        return copies

    results_back = send_back(0, result[...])
    fo.from_pair(0, 4)
    fo.ring()
    d_incoming = result
    d_incoming[...] = jnp.zeros_like(d_incoming)
    start = 2 * (1 - o.c)

    def back_chunk(j):
        expert_back(j, sent_t, d_result, slopes, g_in, g_out, h_in, d_incoming)

    times(start, start + 2, back_chunk)
    fi.to_pair(0, 0, 4)
    times(2 - start, 4 - start, back_chunk)
    grads_back = send_back(1, d_incoming[...])
    fi.from_pair(0, 4)
    fi.ring()
    for copy in results_back + grads_back:
        copy.wait_recv()

    gain_one, gain_two = small8[0:1], small8[1:2]
    returned = mm(placing[...], back[0].reshape(192, 768))
    d_moe = mm(placing[...], back[1].reshape(192, 768))
    attn = after_attn[...]
    r_two = lax.rsqrt(jnp.mean(attn * attn, -1, keepdims=True) + epsilon)
    upstream = cotangent[...].astype(f32)
    gate = jnp.sum(probs[...] * chosen[...], -1, keepdims=True)
    mixed[...] = (attn + gate * returned).astype(bf16)
    d_gate = jnp.sum(upstream * returned, -1, keepdims=True)
    d_logits = probs[...] * (d_gate * chosen[...] - d_gate * gate)
    d_moe = d_moe + jnp.dot(d_logits, small8, precision=highest, preferred_element_type=f32)
    grad_router = lax.dot_general(
        d_logits, moe_input[...].astype(f32), TN, precision=highest, preferred_element_type=f32
    )
    d_after, grad_norm_two = rms_backward(attn, r_two, gain_two, d_moe)
    d_after = d_after + upstream
    d_after_ref[...] = d_after
    d_attn = d_after.astype(bf16)
    d_heads = jnp.zeros((128, 768), f32)
    for h in (0, 1):
        part = d_attn[:, h * 384 : (h + 1) * 384]
        h_ao[h] = mm_tn(heads_out[...], part).astype(bf16).reshape(4, 4, 48, 384)
        d_heads = d_heads + mm_nt(part, g_ao[h].reshape(768, 384))
    fa.to_pair(0, 0, 4)
    d_heads_ref[...] = d_heads.astype(bf16)
    fo.ring_far()

    d_window[...] = jnp.zeros_like(d_window)

    def pair(i):
        pair_backward(i, query, kv, weights, d_heads_ref, d_query, d_kv, d_window)

    times(0, 2, pair)
    fa.from_pair(0, 4)
    fa.ring()
    times(2, 4, pair)
    fi.ring_far()
    fo.across()
    times(4, 6, pair)
    fa.ring_far()
    def lanes_of(n):
        return pl.ds(pl.multiple_of(n * 384, 128), 384)

    def query_grad(n):
        h_qkv[0, :, :, :, lanes_of(n)] = (
            mm(normed_t[:, own_rows], d_query[:, lanes_of(n)]).astype(bf16).reshape(4, 4, 48, 384)
        )

    def key_value_grad(n):
        h_qkv[1, :, :, :, lanes_of(n)] = (
            mm(normed_t[...], d_kv[:, lanes_of(n + 1)]).astype(bf16).reshape(4, 4, 48, 384)
        )

    times(0, 2, query_grad)
    h_qkv[0, :, :, :, 768:1152] = mm(normed_t[...], d_kv[:, 0:384]).astype(bf16).reshape(4, 4, 48, 384)
    times(0, 3, key_value_grad)
    fq.to_pair(0, 0, 4)
    grad_table = lax.dot_general(
        d_window[...], picks, NT, precision=highest, preferred_element_type=f32
    )
    dn = acts.at[:, pl.ds(0, 128), :]

    result[0:8] = jnp.zeros((8, 768), f32)

    def back_rows(n):
        rows = pl.ds(n * 128, 128)
        part = mm_nt(d_kv[rows, 0:384], g_qkv[0, :, :, :, 768:1152].reshape(768, 384))
        part = part + mm_nt(d_kv[rows, 384:1536], g_qkv[1].reshape(768, 1152))
        dn[n] = part.astype(bf16)
        block = whole_tokens[rows].astype(f32)
        r = lax.rsqrt(jnp.mean(block * block, -1, keepdims=True) + epsilon)
        result[0:1] += jnp.sum(part * block * r, 0, keepdims=True)

    for n in range(4):
        back_rows(n)
    dn_copies = [
        remote(dn.at[lax.rem(o.x + by, 4)], dn_in.at[by - 1], dn_send.at[by - 1], dn_recv.at[by - 1], o.along_x(by))
        for by in (1, 2, 3)
    ]
    for copy in dn_copies:
        copy.start()
    d_own = mm_nt(d_query[...], g_qkv[0, :, :, :, 0:768].reshape(768, 768))
    r_one = lax.rsqrt(jnp.mean(x * x, -1, keepdims=True) + epsilon)
    grad_norm_one = result[0:1] + jnp.sum(d_own * x * r_one, 0, keepdims=True)
    fi.across()
    fa.across()
    row = lax.broadcasted_iota(jnp.int32, (8, 768), 0)
    top = jnp.where(row == 0, grad_norm_one, jnp.where(row == 1, grad_norm_two[None, :], grad_router))
    small[0] = jnp.concatenate([top, grad_table[0:8], grad_table[8:16]], 1)
    tot.start(0)
    fq.from_pair(0, 4)
    fq.ring()
    tot.add(0)
    tot.start(1)
    for copy in dn_copies:
        copy.wait_recv()
    d_normed = d_own + dn[o.x].astype(f32)
    for by in (0, 1, 2):
        d_normed = d_normed + dn_in[by].astype(f32)
    d_resid, _ = rms_backward(x, r_one, gain_one, d_normed)
    d_tokens[...] = (d_after_ref[...] + d_resid).astype(bf16)
    total_q, total_a, total_i = (stage.at[:, pl.ds(a, n)] for a, n in ((0, 1152), (1152, 384), (1536, 1536)))
    out_out[...] = fo.total()

    def hand(k, total, out, value):
        n = value.shape[1]
        total[...] = value
        mine = pl.ds(pl.multiple_of(o.c * n, 128), n)
        out[:, mine] = total[pl.ds(pl.multiple_of(24 * o.c, 8), 24), :]
        copy = remote(
            total.at[pl.ds(pl.multiple_of(24 * (1 - o.c), 8), 24)], out.at[:, mine],
            last_send.at[k], last_recv.at[k], o.sibling(),
        )
        copy.start()
        return copy

    last = [hand(0, total_i, out_in, fi.total())]
    total_a[...] = fa.total()
    tot.add(1)
    tot.start(2)
    fq.ring_far()
    fq.across()
    tot.add(2)
    tot.start(3)
    dense = jnp.concatenate([fq.total(), total_a[...]], 1).astype(bf16)
    for j in range(4):
        xs[j] = dense[:, j * 384 : (j + 1) * 384]
    first = [
        remote(xs.at[lax.rem(o.x + by, 4)], xr.at[by - 1], x_send.at[by - 1], x_recv.at[by - 1], o.along_x(by))
        for by in (1, 2, 3)
    ]
    for copy in first:
        copy.start()
    for copy in first:
        copy.wait_recv()
    own = xs[o.x].astype(f32)
    for j in range(3):
        own = own + xr[j].astype(f32)
    xa[o.x] = own.astype(bf16)
    second = [
        remote(xa.at[o.x], xa.at[o.x], x_send.at[by + 2], x_recv.at[by + 2], o.along_x(by)) for by in (1, 2, 3)
    ]
    for copy in second:
        copy.start()
    for copy in second:
        copy.wait_recv()
    whole = jnp.concatenate([xa[0], xa[1], xa[2], xa[3]], 1).astype(f32)
    last.append(hand(1, total_q, out_qkv, whole[:, :1152]))
    last.append(hand(2, total_a, out_ao, whole[:, 1152:]))
    tot.add(3)
    take = lax.broadcasted_iota(jnp.int32, (768, 128), 0) == lax.broadcasted_iota(jnp.int32, (768, 128), 1) + 24 * o.d
    own_small[:, 0:128] = jnp.dot(
        small[4, :, 0:768], jnp.where(take, 1.0, 0.0), precision=highest, preferred_element_type=f32
    )
    heads_of = jnp.concatenate([small[4, :, 768:896], small[4, :, 896:1024]], 0)
    mine = jnp.where(lax.broadcasted_iota(jnp.int32, (16, 128), 1) == o.d, heads_of, 0.0)
    column = jnp.broadcast_to(jnp.sum(mine, -1, keepdims=True), (16, 128))
    same = lax.broadcasted_iota(jnp.int32, (16, 128), 0) == lax.broadcasted_iota(jnp.int32, (16, 128), 1)
    own_small[0:1, 128:256] = jnp.sum(jnp.where(same, column, 0.0), 0, keepdims=True)
    for copy in last:
        copy.wait_recv()
    for copy in results_back + grads_back + dn_copies + tok_copies + first + second + last:
        copy.wait_send()
    tot.drain()
    for f in (fq, fa, fi, fo):
        f.drain([(0, 4)])
    pair_copy.wait_send()
    side.drain()
    for f in flows:
        f.drain()


def layer(*operands):
    vm = pl.BlockSpec(memory_space=pltpu.VMEM)
    dma = pltpu.SemaphoreType.DMA

    def low(*shape):
        return pltpu.VMEM(shape, bf16)

    def full(*shape):
        return pltpu.VMEM(shape, f32)

    sizes = ((48, 1152), (48, 384), (48, 1536), (96, 768))
    weights = (low(2, 4, 4, 48, 1152), low(2, 4, 4, 48, 384), low(2, 4, 4, 48, 1536), low(4, 4, 2, 96, 768))
    return pl.pallas_call(
        layer_kernel,
        in_specs=[vm] * len(operands),
        out_specs=[vm] * 7,
        out_shape=[
            jax.ShapeDtypeStruct((128, 768), bf16),
            jax.ShapeDtypeStruct((128, 768), bf16),
            jax.ShapeDtypeStruct((24, 2304), f32),
            jax.ShapeDtypeStruct((24, 768), f32),
            jax.ShapeDtypeStruct((24, 3072), f32),
            jax.ShapeDtypeStruct((96, 768), f32),
            jax.ShapeDtypeStruct((8, 256), f32),
        ],
        scratch_shapes=[
            full(5, 8, 1024), pltpu.VMEM((1, 1024), jnp.int32), full(48, 3072), full(24, 3072), dma((2,)), dma((4, 11)), dma((4, 11)),
            full(4, 8, 1024), full(7, 8, 1024), dma((7,)), dma((7,)),
            *weights, low(512, 768), dma((3,)), dma((3,)), low(512, 768), low(768, 512), low(128, 768), low(512, 1536), full(16, 640),
            low(12, 128, 512), low(128, 768), full(128, 768), low(128, 768), low(128, 192),
            full(128, 8), full(128, 8), low(2, 4, 48, 768), low(2, 4, 48, 768), dma((2, 3)), dma((2, 3)),
            low(192, 768), low(192, 768), low(4, 192, 768), low(4, 192, 768),
            *weights,
            low(768, 192), full(192, 768), low(2, 4, 48, 768),
            low(512, 1536), low(3, 128, 768), full(16, 640),
            low(4, 48, 384), low(3, 48, 384), low(4, 48, 384),
            *[low(4, 4, *s) for s in sizes[1:]],
            *[low(2, 2, *s) for s in sizes],
            *[low(2, 4, *s) for s in sizes],
            *[low(3, *s) for s in sizes],
            dma((4, 11)), dma((4, 11)), dma((2, 3)), dma((2, 3)), dma((3,)), dma((3,)),
            dma((6,)), dma((6,)), dma((3,)), dma((3,)),
            full(10, 8, 1024), dma((10,)), dma((10,)),
        ],
        compiler_params=pltpu.CompilerParams(
            collective_id=0, has_side_effects=True, vmem_limit_bytes=63 * 2**20
        ),
    )(*operands)


def emit_kernel(
    mixed, d_tokens, qkv, ao, first, second, own,
    o_mixed, o_tokens, o_na, o_qkv, o_ao, o_table, o_nm, o_router, o_first, o_second,
):
    o_mixed[...] = mixed[...]
    o_tokens[...] = d_tokens[...]
    o_qkv[...] = qkv[...]
    o_ao[...] = ao[...]
    o_first[:, 0, :] = first[...]
    o_second[:, 0, :] = second[...]
    o_na[...] = own[0:1, 0:24]
    o_nm[...] = own[1:2, 0:24]
    o_router[...] = own[2:6, 0:24]
    o_table[...] = own[0:1, 128:140]


def emit(*results):
    vm = pl.BlockSpec(memory_space=pltpu.VMEM)
    kinds = (
        ((128, 768), bf16), ((128, 768), bf16), ((1, 24), f32), ((24, 2304), f32), ((24, 768), f32),
        ((1, 12), f32), ((1, 24), f32), ((4, 24), f32), ((24, 1, 3072), f32), ((96, 1, 768), f32),
    )
    return pl.pallas_call(
        emit_kernel,
        in_specs=[vm] * 7,
        out_specs=[vm] * 10,
        out_shape=[jax.ShapeDtypeStruct(shape, kind) for shape, kind in kinds],
    )(*results)


def per_device(
    tokens, norm_attn, w_qkv, w_attn_out, bias_table, norm_moe, router, w_in, w_out, routes, buckets, cotangent
):
    results = layer(
        w_qkv, w_attn_out, w_in[:, 0], w_out[:, 0], norm_attn[None, :], norm_moe[None, :], router.T, bias_table,
        tokens, routes.T, buckets[None, :], cotangent,
    )
    mixed, d_tokens, g_na, g_qkv, g_ao, g_table, g_nm, g_router, g_in, g_out = emit(*results)
    return mixed, d_tokens, g_na[0], g_qkv, g_ao, g_table, g_nm[0], g_router.T, g_in, g_out


def solution(mesh):
    both = ("dp", "expert")
    in_specs = (
        P(both, None), P("dp"), P("dp", None), P("dp", None), P("dp", None), P("dp"), P("dp", None),
        P("dp", "expert", None), P("dp", "expert", None), P(both, None), P(), P(both, None),
    )
    out_specs = (
        P(both, None), P(both, None), P("dp"), P("dp", None), P("dp", None), P("dp", None), P("dp"),
        P("dp", None), P("dp", "expert", None), P("dp", "expert", None),
    )
    return jax.shard_map(
        per_device, mesh=mesh, in_specs=in_specs, out_specs=out_specs, check_vma=False
    )
```

```python
import jax
import jax.numpy as jnp
from jax import lax
from jax.experimental import pallas as pl
from jax.experimental.pallas import tpu as pltpu
from jax.sharding import PartitionSpec as P

epsilon = 1e-06
highest = lax.Precision.HIGHEST
bf16 = jnp.bfloat16
f32 = jnp.float32
NT = (((1,), (1,)), ((), ()))
TN = (((0,), (0,)), ((), ()))


def mm(a, b):
    return jnp.dot(a, b, preferred_element_type=f32)


def mm_nt(a, b):
    return lax.dot_general(a, b, NT, preferred_element_type=f32)


def mm_tn(a, b):
    return lax.dot_general(a, b, TN, preferred_element_type=f32)


def stack_heads(pair):
    left = lax.broadcasted_iota(jnp.int32, pair.shape, 1) < 64
    zero = jnp.zeros_like(pair)
    return jnp.concatenate([jnp.where(left, pair, zero), jnp.where(left, zero, pair)], 0)


def join_pair(stacked):
    rows = stacked.shape[0] // 2
    left = lax.broadcasted_iota(jnp.int32, (rows, 128), 1) < 64
    return jnp.where(left, stacked[:rows], stacked[rows:])


def toeplitz(window_row, rows, keys):
    width = window_row.shape[1]
    wide = jnp.broadcast_to(window_row, (rows, width))
    rolled = pltpu.roll(wide, width - (rows - 1), 1, stride=1, stride_axis=0)
    return rolled[:, :keys]


def diagonal_sums(block, width):
    rows, keys = block.shape
    wide = jnp.concatenate([block, jnp.zeros((rows, width - keys), f32)], 1)
    half = rows // 2
    while half >= 8:
        wide = wide[:half] + pltpu.roll(wide[half:], width - half, 1)
        half //= 2
    row = lax.broadcasted_iota(jnp.int32, wide.shape, 0)
    for bit in (1, 2, 4):
        wide = jnp.where((row & bit) != 0, pltpu.roll(wide, width - bit, 1), wide)
    total = jnp.sum(wide, 0, keepdims=True)
    return pltpu.roll(total, rows - 1, 1)


def rms_forward(values, gain):
    r = lax.rsqrt(jnp.mean(values * values, -1, keepdims=True) + epsilon)
    return r, values * r * gain


def rms_backward(values, r, gain, grad):
    u = grad * gain
    d_values = r * u - values * (r * r * r) * jnp.mean(u * values, -1, keepdims=True)
    return d_values, jnp.sum(grad * values * r, 0)


MESH = pl.DeviceIdType.MESH


class Place:
    def __init__(self):
        d = lax.axis_index("dp")
        self.d = d
        self.x = lax.axis_index("expert")
        self.c = lax.rem(d, 2)
        self.z = lax.rem(lax.div(d, 2), 4)
        self.y = lax.div(d, 8)
        self.p = self.z * (1 - self.c) + self.y * self.c
        self.q = self.y * (1 - self.c) + self.z * self.c

    def at(self, p, q):
        y = q * (1 - self.c) + p * self.c
        z = p * (1 - self.c) + q * self.c
        return ((y * 4 + z) * 2 + self.c, self.x)

    def along_p(self, by):
        return self.at(lax.rem(self.p + by, 4), self.q)

    def along_q(self, by):
        return self.at(self.p, lax.rem(self.q + by, 4))

    def along_x(self, by):
        return (self.d, lax.rem(self.x + by, 4))

    def sibling(self):
        return (self.d + 1 - 2 * self.c, self.x)

    def each_core(self, body):
        pl.when(self.c == 0)(lambda: body(0))
        pl.when(self.c == 1)(lambda: body(1))

    def barrier(self, with_x):
        peers = [self.sibling()] + [self.along_p(i) for i in (1, 2, 3)]
        peers += [self.along_q(i) for i in (1, 2, 3)]
        if with_x:
            peers += [self.along_x(i) for i in (1, 2, 3)]
        sem = pltpu.get_barrier_semaphore()
        for peer in peers:
            pl.semaphore_signal(sem, inc=1, device_id=peer, device_id_type=MESH)
        return lambda: pl.semaphore_wait(sem, len(peers))


def remote(src, dst, send, recv, to):
    return pltpu.make_async_remote_copy(
        src_ref=src, dst_ref=dst, send_sem=send, recv_sem=recv, device_id=to, device_id_type=MESH
    )


def block_of(ref, tall, k, p, q):
    y, z = (q, p) if k == 0 else (p, q)
    return ref.at[y, z, k] if tall else ref.at[k, y, z]


def slab_of(ref, tall, k, q, low=0, count=4):
    y, z = (q, pl.ds(low, count)) if k == 0 else (pl.ds(low, count), q)
    return ref.at[y, z, k] if tall else ref.at[k, y, z]


class Gather:
    sends = 11
    recvs = 11

    def __init__(self, place, ref, tall, send, recv, number):
        self.o, self.ref, self.tall, self.send, self.recv = place, ref, tall, send, recv
        self.number = number

    def block(self, k, by):
        return block_of(self.ref, self.tall, k, lax.rem(self.o.p + by, 4), self.o.q)

    def slab(self, k, by, low=0, count=4):
        return slab_of(self.ref, self.tall, k, lax.rem(self.o.q + by, 4), low, count)

    def go(self, part, s, r, to):
        def body(k):
            src = part(k)
            remote(src, src, self.send.at[s], self.recv.at[r], to).start()

        self.o.each_core(body)

    def arrived(self, r, count):
        if count == 1:
            view = block_of(self.ref, self.tall, 0, 0, 0)
        else:
            view = slab_of(self.ref, self.tall, 0, 0, 0, count)
        remote(view, view, self.send.at[0], self.recv.at[r], self.o.sibling()).wait_recv()

    def sent(self, s, count):
        if count == 1:
            view = block_of(self.ref, self.tall, 0, 0, 0)
        else:
            view = slab_of(self.ref, self.tall, 0, 0, 0, count)
        remote(view, view, self.send.at[s], self.recv.at[0], self.o.sibling()).wait_send()

    def ring_one(self):
        self.go(lambda k: self.block(k, 0), 0, 0, self.o.along_p(1))
        self.go(lambda k: self.block(k, 0), 1, 1, self.o.along_p(3))
        if self.number == 0:
            self.go(lambda k: self.block(k, 0), 2, 2, self.o.along_p(2))

    def ring_one_far(self):
        self.arrived(0, 1)
        self.arrived(1, 1)
        if self.number == 0:
            return
        if self.number % 2 == 0:
            self.go(lambda k: self.block(k, 3), 2, 2, self.o.along_p(1))
        else:
            self.go(lambda k: self.block(k, 1), 2, 2, self.o.along_p(3))

    def ring_two_block(self, by):
        n = 3 if by == 0 else 9 + 2 * by
        self.go(lambda k: self.block(k, by), n, 3, self.o.along_q(1))
        self.go(lambda k: self.block(k, by), 4 if by == 0 else n + 1, 4, self.o.along_q(3))

    def ring_two(self):
        self.arrived(2, 1)
        for by in (1, 2, 3):
            self.ring_two_block(by)
        self.go(lambda k: self.slab(k, 0), 7, 7, self.o.sibling())

    def ring_two_far(self):
        self.arrived(3, 4)
        self.go(lambda k: self.slab(k, 3, 0, 2), 5, 5, self.o.along_q(1))
        self.arrived(4, 4)
        self.go(lambda k: self.slab(k, 1, 2, 2), 6, 6, self.o.along_q(3))
        self.go(lambda k: self.slab(k, 3), 8, 8, self.o.sibling())
        self.go(lambda k: self.slab(k, 1), 9, 9, self.o.sibling())

    def last(self):
        self.arrived(5, 2)
        self.arrived(6, 2)
        self.go(lambda k: self.slab(k, 2), 10, 10, self.o.sibling())

    def finish(self):
        for r in (7, 8, 9, 10):
            self.arrived(r, 4)

    def drain(self):
        for s, count in ((0, 1), (1, 1), (2, 1), (3, 1), (4, 1), (5, 2), (6, 2), (7, 4), (8, 4), (9, 4), (10, 4),
                         *((n, 1) for n in range(11, 17))):
            self.sent(s, count)


class SmallSum:
    def __init__(self, place, value, arrivals, send, recv, with_x):
        self.o, self.value, self.arrivals, self.send, self.recv = place, value, arrivals, send, recv
        o = place
        self.steps = [[o.sibling()], [o.along_p(i) for i in (1, 2, 3)], [o.along_q(i) for i in (1, 2, 3)]]
        if with_x:
            self.steps.append([o.along_x(i) for i in (1, 2, 3)])
        self.copies = []
        n = 0
        for s, peers in enumerate(self.steps):
            row = []
            for peer in peers:
                row.append(
                    remote(value.at[s], arrivals.at[n], send.at[n], recv.at[n], peer)
                )
                n += 1
            self.copies.append(row)

    def start(self, s):
        for copy in self.copies[s]:
            copy.start()

    def add(self, s):
        first = sum(len(row) for row in self.copies[:s])
        total = self.value[s]
        for i, copy in enumerate(self.copies[s]):
            copy.wait_recv()
            total = total + self.arrivals[first + i]
        self.value[s + 1] = total

    def drain(self):
        for row in self.copies:
            for copy in row:
                copy.wait_send()


def place_small(o, out, na, nm, router_t, table):
    row = lax.broadcasted_iota(jnp.int32, (24, 768), 0)
    lane = lax.broadcasted_iota(jnp.int32, (24, 768), 1)
    hit = jnp.where(lane == 24 * o.d + row, 1.0, 0.0)
    out[...] = jnp.zeros((8, 1024), f32)
    out[0:1, 0:768] = mm(na[...].astype(f32), hit)
    out[1:2, 0:768] = mm(nm[...].astype(f32), hit)
    out[2:6, 0:768] = mm(router_t[...].astype(f32), hit)
    head = lax.broadcasted_iota(jnp.int32, (16, 12), 0) == lax.broadcasted_iota(jnp.int32, (16, 12), 1)
    wide = jnp.broadcast_to(table[...].astype(f32), (16, 12))
    column = jnp.sum(jnp.where(head, wide, 0.0), -1, keepdims=True)
    own = lax.broadcasted_iota(jnp.int32, (16, 128), 1) == o.d
    placed = jnp.where(own, jnp.broadcast_to(column, (16, 128)), 0.0)
    out[:, 768:896] = placed[0:8]
    out[:, 896:1024] = placed[8:16]


def meet(o, halves, stage, other, sem):
    at = 0
    for ref, blocks in halves:
        n = ref.shape[1] // (2 * blocks)
        for t in range(blocks):
            own = pl.ds(pl.multiple_of(o.c * n + 2 * t * n, 128), n)
            theirs = pl.ds(pl.multiple_of((1 - o.c) * n + 2 * t * n, 128), n)
            stage[pl.ds(pl.multiple_of(24 * o.c, 8), 24), at : at + n] = ref[:, own].astype(f32)
            other[:, at : at + n] = ref[:, theirs].astype(f32)
            at += n
    return remote(
        other, stage.at[pl.ds(pl.multiple_of(24 * o.c, 8), 24)], sem.at[0], sem.at[1], o.sibling()
    )


class Scatter:
    def __init__(self, place, ref, tall, pair, far, near, side, send, recv):
        self.o, self.ref, self.tall = place, ref, tall
        self.pair, self.far, self.near, self.side = pair, far, near, side
        self.send, self.recv = send, recv

    def where(self, p, q):
        o = self.o
        return q * (1 - o.c) + p * o.c, p * (1 - o.c) + q * o.c

    def q_at(self, by):
        return lax.rem(self.o.q + by, 4)

    def own(self, p, q):
        y, z = self.where(p, q)
        return (y, z, self.o.c) if self.tall else (self.o.c, y, z)

    def to_pair(self, s, low, count):
        rows = pl.ds(low, count)
        theirs = 1 - self.o.c
        src = self.ref.at[rows, :, theirs] if self.tall else self.ref.at[theirs, rows]
        remote(src, self.pair.at[rows], self.send.at[s], self.recv.at[s], self.o.sibling()).start()

    def from_pair(self, s, count):
        view = self.pair.at[pl.ds(0, count)]
        remote(view, view, self.send.at[s], self.recv.at[s], self.o.sibling()).wait_recv()

    def add_pair(self, by):
        q = self.q_at(by)

        def body(p, carry):
            y, z = self.where(p, q)
            at = self.own(p, q)
            self.ref[at] = (self.ref[at].astype(f32) + self.pair[y, z].astype(f32)).astype(bf16)
            return carry

        lax.fori_loop(0, 4, body, 0)

    def go(self, s, by, low, dst, to):
        def body(k):
            src = slab_of(self.ref, self.tall, k, self.q_at(by), low, 2)
            remote(src, dst, self.send.at[s], self.recv.at[s], to).start()

        self.o.each_core(body)

    def ring(self):
        o = self.o
        self.add_pair(2)
        self.go(2, 2, 0, self.far.at[0], o.along_q(1))
        self.go(3, 2, 2, self.far.at[1], o.along_q(3))
        self.add_pair(1)
        self.go(4, 1, 2, self.near.at[0, pl.ds(2, 2)], o.along_q(1))
        self.add_pair(3)
        self.go(5, 3, 0, self.near.at[1, pl.ds(0, 2)], o.along_q(3))
        self.add_pair(0)

    def landed(self, s, view):
        remote(view, view, self.send.at[s], self.recv.at[s], self.o.sibling()).wait_recv()

    def add_far(self, i, by, low):
        q = self.q_at(by)

        def body(j, carry):
            at = self.own(low + j, q)
            self.ref[at] = (self.ref[at].astype(f32) + self.far[i, j].astype(f32)).astype(bf16)
            return carry

        lax.fori_loop(0, 2, body, 0)

    def ring_far(self):
        o = self.o
        self.landed(2, self.far.at[0])
        self.add_far(0, 1, 0)
        self.go(6, 1, 0, self.near.at[0, pl.ds(0, 2)], o.along_q(1))
        self.landed(3, self.far.at[1])
        self.add_far(1, 3, 2)
        self.go(7, 3, 2, self.near.at[1, pl.ds(2, 2)], o.along_q(3))

    def across(self):
        o = self.o
        half = self.near.at[0, pl.ds(0, 2)]
        for s in (4, 5, 6, 7):
            self.landed(s, half)

        def body(p, carry):
            at = self.own(p, o.q)
            total = self.ref[at].astype(f32) + self.near[0, p].astype(f32)
            self.ref[at] = (total + self.near[1, p].astype(f32)).astype(bf16)
            return carry

        lax.fori_loop(0, 4, body, 0)
        for i in (1, 2, 3):
            src = self.ref.at[self.own(lax.rem(o.p + i, 4), o.q)]
            remote(
                src, self.side.at[i - 1], self.send.at[7 + i], self.recv.at[7 + i], o.along_p(i)
            ).start()

    def total(self):
        o = self.o
        for i in (0, 1, 2):
            self.landed(8 + i, self.side.at[i])
        total = self.ref[self.own(o.p, o.q)].astype(f32)
        for i in (0, 1, 2):
            total = total + self.side[i].astype(f32)
        return total

    def sent(self, s, view):
        remote(view, view, self.send.at[s], self.recv.at[s], self.o.sibling()).wait_send()

    def drain(self, pair_parts):
        for s, count in pair_parts:
            self.sent(s, self.pair.at[pl.ds(0, count)])
        for s in range(2, 8):
            self.sent(s, self.far.at[0])
        for s in range(8, 11):
            self.sent(s, self.side.at[0])


SQ = 0.7978845608028654


def gelu_both(h):
    t = jnp.tanh(SQ * (h + 0.044715 * (h * h * h)))
    value = 0.5 * h * (1.0 + t)
    slope = 0.5 * (1.0 + t) + 0.5 * h * (1.0 - t * t) * (SQ * (1.0 + 3 * 0.044715 * (h * h)))
    return value, slope


def hidden_lanes(j):
    return lax.div(j, 2), pl.ds(pl.multiple_of(lax.rem(j, 2) * 768, 128), 768)


def expert_hidden(j, sent, g_in, acts, slopes):
    half, at = hidden_lanes(j)
    value, slope = gelu_both(mm(sent[...], g_in[half, :, :, :, at].reshape(768, 768)))
    acts[j] = value.astype(bf16)
    slopes[j] = slope.astype(bf16)


def expert_second_grad(j, d_result, acts, h_out):
    for r in (0, 1):
        part = acts[j, :, r * 384 : (r + 1) * 384]
        h_out[j, pl.ds(2 * r, 2)] = mm_tn(part, d_result[...]).astype(bf16).reshape(2, 2, 96, 768)


def expert_result(j, acts, g_out, result):
    result[...] += mm(acts[j], g_out[j].reshape(768, 768))


def expert_back(j, sent_t, d_result, slopes, g_in, g_out, h_in, d_incoming):
    half, at = hidden_lanes(j)
    d_act = mm_nt(d_result[...], g_out[j].reshape(768, 768))
    d_hidden = (d_act * slopes[j].astype(f32)).astype(bf16)
    for r in (0, 1):
        part = sent_t[r * 384 : (r + 1) * 384]
        h_in[half, pl.ds(2 * r, 2), :, :, at] = mm(part, d_hidden).astype(bf16).reshape(2, 4, 48, 768)
    d_incoming[...] += mm_nt(d_hidden, g_in[half, :, :, :, at].reshape(768, 768))


def pair_backward(i, query, kv, weights, d_heads, d_query, d_kv, d_window):
    lanes = pl.ds(pl.multiple_of(i * 128, 128), 128)
    value_lanes = pl.ds(pl.multiple_of(i * 128 + 768, 128), 128)
    kept = weights[pl.ds(2 * i, 2)].reshape(256, 512)
    probability = kept.astype(f32)
    d_stack = stack_heads(d_heads[:, lanes])
    d_weights = mm_nt(d_stack, kv[:, value_lanes])
    d_kv[:, value_lanes] = mm_tn(kept, d_stack).astype(bf16)
    d_scores = probability * (d_weights - jnp.sum(probability * d_weights, -1, keepdims=True))
    low = d_scores.astype(bf16)
    d_kv[:, lanes] = mm_tn(low, stack_heads(query[:, lanes])).astype(bf16)
    d_query[:, lanes] = join_pair(mm(low, kv[:, lanes])).astype(bf16)
    for j in (0, 1):
        d_window[pl.ds(2 * i + j, 1), :] = diagonal_sums(d_scores[j * 128 : (j + 1) * 128], 640)


def pair_forward(i, query, kv, window, heads_out, weights):
    lanes = pl.ds(pl.multiple_of(i * 128, 128), 128)
    value_lanes = pl.ds(pl.multiple_of(i * 128 + 768, 128), 128)
    bias = jnp.concatenate([toeplitz(window[pl.ds(2 * i + j, 1), :], 128, 512) for j in (0, 1)], 0)
    scores = mm_nt(stack_heads(query[:, lanes]), kv[:, lanes]) + bias
    top = jnp.max(scores, -1, keepdims=True)
    raised = jnp.exp(scores - top)
    probability = raised / jnp.sum(raised, -1, keepdims=True)
    low = probability.astype(bf16)
    weights[pl.ds(2 * i, 2)] = low.reshape(2, 128, 512)
    heads_out[:, lanes] = join_pair(mm(low, kv[:, value_lanes])).astype(bf16)


def layer_kernel(
    w_qkv, w_ao, w_in, w_out, na, nm, router_t, table, tokens, routes, bucket_list, cotangent,
    mixed, d_tokens, out_qkv, out_ao, out_in, out_out, own_small,
    small, buckets, stage, other, pair_sem, g_sends, g_recvs, side_in, side_arrivals, side_send, side_recv,
    g_qkv, g_ao, g_in, g_out, whole_tokens, tok_send, tok_recv, normed_ref, normed_t, query, kv, window, weights, heads_out,
    after_attn, moe_input, placing, probs, chosen, disp, inc, disp_send, disp_recv, sent, d_result, acts, slopes,
    h_qkv, h_ao, h_in, h_out, sent_t, result, back, d_kv, dn_in, d_window,
    xs, xr, xa,
    pair_a, pair_i, pair_o, far_q, far_a, far_i, far_o, near_q, near_a, near_i, near_o,
    side_q, side_a, side_i, side_o,
    sends, recvs, ret_send, ret_recv, dn_send, dn_recv, x_send, x_recv, last_send, last_recv,
    arrivals, small_send, small_recv,
):
    d_heads_ref, d_after_ref, d_query = heads_out, after_attn, query
    o = Place()
    entered = o.barrier(True)
    flows = [
        Gather(o, ref, tall, g_sends.at[i], g_recvs.at[i], i)
        for i, (ref, tall) in enumerate(((g_qkv, 0), (g_ao, 0), (g_in, 0), (g_out, 1)))
    ]
    qkv, ao, win, wout = flows
    pair_copy = meet(o, ((w_qkv, 3), (w_ao, 1), (w_in, 1)), stage, other, pair_sem)
    side = SmallSum(o, side_in, side_arrivals, side_send, side_recv, False)
    place_small(o, side_in.at[0], na, nm, router_t, table)
    buckets[...] = jnp.zeros_like(buckets)
    buckets[:, 0:1023] = bucket_list[...]
    g_out[o.y, o.z, o.c] = w_out[...]
    own_rows = pl.ds(pl.multiple_of(o.x * 128, 128), 128)
    whole_tokens[own_rows] = tokens[...]
    entered()
    pair_copy.start()
    side.start(0)
    wout.ring_one()
    wout.ring_two_block(0)
    pair_copy.wait_recv()
    at = 0
    for ref in (g_qkv, g_ao, g_in):
        n = ref.shape[-1]
        ref[o.c, o.y, o.z] = stage[:, at : at + n].astype(bf16)
        at += n
    qkv.ring_one()
    qkv.ring_two_block(0)
    side.add(0)
    side.start(1)
    tok_copies = [
        remote(
            whole_tokens.at[own_rows], whole_tokens.at[own_rows], tok_send.at[by - 1], tok_recv.at[by - 1],
            o.along_x(by),
        )
        for by in (1, 2, 3)
    ]
    for copy in tok_copies:
        copy.start()
    win.ring_one()
    ao.ring_one()
    ao.ring_two_block(0)
    win.ring_two_block(0)
    qkv.ring_one_far()
    qkv.ring_two()
    side.add(1)
    side.start(2)
    x = tokens[...].astype(f32)
    bucket_row = buckets[:, pl.ds(pl.multiple_of((3 - o.x) * 128, 128), 640)]
    picks = jnp.where(
        jnp.broadcast_to(bucket_row, (128, 640)) == lax.broadcasted_iota(jnp.int32, (128, 640), 0), 1.0, 0.0
    )
    for f in (wout, win, ao):
        f.ring_one_far()
    ao.ring_two()
    win.ring_two()
    qkv.ring_two_far()
    wout.ring_two()
    for copy in tok_copies:
        copy.wait_recv()
    side.add(2)
    small_in = side_in.at[3]
    gain_row = small_in[0:1, :768]

    def norm_rows(n, carry):
        rows = pl.ds(n * 128, 128)
        _, normed = rms_forward(whole_tokens[rows].astype(f32), gain_row)
        normed_ref[rows] = normed.astype(bf16)
        normed_t[:, rows] = normed.T.astype(bf16)
        return carry

    for n in range(4):
        norm_rows(n, 0)
    table_t = jnp.concatenate([small_in[:, 768:896], small_in[:, 896:1024]], 0)
    window[...] = mm(table_t.astype(bf16), picks.astype(bf16))
    qkv.last()
    ao.ring_two_far()
    qkv.finish()

    for h in (0, 1):
        query[:, 384 * h : 384 * h + 384] = mm(
            normed_ref[own_rows], g_qkv[h, :, :, :, 0:384].reshape(768, 384)
        ).astype(bf16)

    def project_rows(n, carry):
        rows = pl.ds(pl.multiple_of(n * 128, 128), 128)
        for h in (0, 1):
            both = mm(normed_ref[rows], g_qkv[h, :, :, :, 384:1152].reshape(768, 768)).astype(bf16)
            kv[rows, 384 * h : 384 * h + 384] = both[:, :384]
            kv[rows, 768 + 384 * h : 1152 + 384 * h] = both[:, 384:]
        return carry

    lax.fori_loop(0, 4, project_rows, 0)
    ao.last()

    def ahead(i, carry):
        pair_forward(i, query, kv, window, heads_out, weights)
        return carry

    lax.fori_loop(0, 3, ahead, 0)
    win.ring_two_far()
    lax.fori_loop(3, 6, ahead, 0)
    ao.finish()
    mixed_heads = heads_out[...]
    attn = x + jnp.concatenate([mm(mixed_heads, g_ao[h].reshape(768, 384)) for h in (0, 1)], 1)
    after_attn[...] = attn
    small8 = small_in[:, :768]
    r_two = lax.rsqrt(jnp.mean(attn * attn, -1, keepdims=True) + epsilon)
    moe_low = (attn * r_two * small8[1:2]).astype(bf16)
    moe_input[...] = moe_low
    logits = mm_nt(moe_low, small8.astype(bf16))
    lane = lax.broadcasted_iota(jnp.int32, (128, 8), 1)
    logits = jnp.where((lane >= 2) & (lane < 6), logits, -1e30)
    raised = jnp.exp(logits - jnp.max(logits, -1, keepdims=True))
    probability = raised / jnp.sum(raised, -1, keepdims=True)
    probs[...] = probability
    named = jnp.broadcast_to(routes[...], (8, 128)) + 2
    picked = jnp.where(lax.broadcasted_iota(jnp.int32, (8, 128), 0) == named, 1.0, 0.0).T
    chosen[...] = picked
    gate = jnp.sum(probability * picked, -1, keepdims=True)
    before = jnp.where(
        lax.broadcasted_iota(jnp.int32, (128, 128), 1) < lax.broadcasted_iota(jnp.int32, (128, 128), 0), 1.0, 0.0
    )
    slot = jnp.sum(mm(before.astype(bf16), picked.astype(bf16)) * picked, -1, keepdims=True)
    column = jnp.sum(picked * ((lane - 2) * 48).astype(f32), -1, keepdims=True) + slot
    place = jnp.where(
        lax.broadcasted_iota(jnp.int32, (128, 192), 1).astype(f32) == column, 1.0, 0.0
    ).astype(bf16)
    placing[...] = place
    def dispatch(part, value):
        disp[part] = mm_tn(place, value).astype(bf16).reshape(4, 48, 768)
        copies = [
            remote(
                disp.at[part, lax.rem(o.x + by, 4)], inc.at[part, o.x],
                disp_send.at[part, by - 1], disp_recv.at[part, by - 1], o.along_x(by),
            )
            for by in (1, 2, 3)
        ]
        for copy in copies:
            copy.start()
        inc[part, o.x] = disp[part, o.x]
        return copies

    tokens_out = dispatch(0, moe_low)
    grads_out = dispatch(1, (gate * cotangent[...].astype(f32)).astype(bf16))
    win.last()
    wout.ring_two_far()
    for copy in tokens_out:
        copy.wait_recv()
    sent[...] = inc[0].reshape(192, 768)
    sent_t[...] = sent[...].astype(f32).T.astype(bf16)
    win.finish()
    pair_q = pair_i.at[:, :, :, pl.ds(0, 1152)]
    fq = Scatter(o, h_qkv, 0, pair_q, far_q, near_q, side_q, sends.at[0], recvs.at[0])
    fa = Scatter(o, h_ao, 0, pair_a, far_a, near_a, side_a, sends.at[1], recvs.at[1])
    fi = Scatter(o, h_in, 0, pair_i, far_i, near_i, side_i, sends.at[2], recvs.at[2])
    fo = Scatter(o, h_out, 1, pair_o, far_o, near_o, side_o, sends.at[3], recvs.at[3])
    tot = SmallSum(o, small, arrivals, small_send, small_recv, True)

    def times(low, high, body):
        def step(j, carry):
            body(j)
            return carry

        lax.fori_loop(low, high, step, 0)

    times(0, 4, lambda j: expert_hidden(j, sent, g_in, acts, slopes))
    wout.last()
    for copy in grads_out:
        copy.wait_recv()
    d_result[...] = inc[1].reshape(192, 768)
    times(0, 4, lambda j: expert_second_grad(j, d_result, acts, h_out))
    fo.to_pair(0, 0, 4)
    wout.finish()
    fo.from_pair(0, 4)
    fo.ring()
    result[...] = jnp.zeros_like(result)
    times(0, 4, lambda j: expert_result(j, acts, g_out, result))

    def send_back(part, value):
        for copy in (tokens_out, grads_out)[part]:
            copy.wait_send()
        ret = disp
        ret[part] = value.astype(bf16).reshape(4, 48, 768)
        copies = [
            remote(
                ret.at[part, lax.rem(o.x + by, 4)], back.at[part, o.x],
                ret_send.at[part, by - 1], ret_recv.at[part, by - 1], o.along_x(by),
            )
            for by in (1, 2, 3)
        ]
        for copy in copies:
            copy.start()
        back[part, o.x] = ret[part, o.x]
        return copies

    results_back = send_back(0, result[...])
    d_incoming = result
    d_incoming[...] = jnp.zeros_like(d_incoming)
    start = 2 * (1 - o.c)

    def back_chunk(j):
        expert_back(j, sent_t, d_result, slopes, g_in, g_out, h_in, d_incoming)

    times(start, start + 2, back_chunk)
    fi.to_pair(0, 0, 4)
    times(2 - start, 4 - start, back_chunk)
    grads_back = send_back(1, d_incoming[...])
    fi.from_pair(0, 4)
    fi.ring()
    for copy in results_back + grads_back:
        copy.wait_recv()

    gain_one, gain_two = small8[0:1], small8[1:2]
    returned = mm(placing[...], back[0].reshape(192, 768))
    d_moe = mm(placing[...], back[1].reshape(192, 768))
    attn = after_attn[...]
    r_two = lax.rsqrt(jnp.mean(attn * attn, -1, keepdims=True) + epsilon)
    upstream = cotangent[...].astype(f32)
    gate = jnp.sum(probs[...] * chosen[...], -1, keepdims=True)
    mixed[...] = (attn + gate * returned).astype(bf16)
    d_gate = jnp.sum(upstream * returned, -1, keepdims=True)
    d_logits = probs[...] * (d_gate * chosen[...] - d_gate * gate)
    d_moe = d_moe + jnp.dot(d_logits, small8, precision=highest, preferred_element_type=f32)
    grad_router = lax.dot_general(
        d_logits, moe_input[...].astype(f32), TN, precision=highest, preferred_element_type=f32
    )
    d_after, grad_norm_two = rms_backward(attn, r_two, gain_two, d_moe)
    d_after = d_after + upstream
    d_after_ref[...] = d_after
    d_attn = d_after.astype(bf16)
    d_heads = jnp.zeros((128, 768), f32)
    for h in (0, 1):
        part = d_attn[:, h * 384 : (h + 1) * 384]
        h_ao[h] = mm_tn(heads_out[...], part).astype(bf16).reshape(4, 4, 48, 384)
        d_heads = d_heads + mm_nt(part, g_ao[h].reshape(768, 384))
    fa.to_pair(0, 0, 4)
    d_heads_ref[...] = d_heads.astype(bf16)
    fo.ring_far()

    d_window[...] = jnp.zeros_like(d_window)

    def pair(i):
        pair_backward(i, query, kv, weights, d_heads_ref, d_query, d_kv, d_window)

    def lanes_of(h, base):
        return pl.ds(pl.multiple_of(h * 384 + base, 128), 384)

    def dense_grad(h):
        for t, part in enumerate(
            (
                mm(normed_t[:, own_rows], d_query[:, lanes_of(h, 0)]),
                mm(normed_t[...], d_kv[:, lanes_of(h, 0)]),
                mm(normed_t[...], d_kv[:, lanes_of(h, 768)]),
            )
        ):
            h_qkv[h, :, :, :, t * 384 : t * 384 + 384] = part.astype(bf16).reshape(4, 4, 48, 384)

    theirs = 1 - o.c
    times(3 * theirs, 3 * theirs + 3, pair)
    dense_grad(theirs)
    fa.from_pair(0, 4)
    fq.to_pair(0, 0, 4)
    fa.ring()
    fi.ring_far()
    times(3 * o.c, 3 * o.c + 3, pair)
    dense_grad(o.c)
    fo.across()
    fa.ring_far()
    fq.from_pair(0, 4)
    fq.ring()
    fi.across()
    fa.across()
    grad_table = lax.dot_general(
        d_window[...], picks, NT, precision=highest, preferred_element_type=f32
    )
    result[0:8] = jnp.zeros((8, 768), f32)
    dn = acts.at[:, pl.ds(0, 128), :]

    for n in range(4):
        rows = pl.ds(n * 128, 128)
        part = jnp.zeros((128, 768), f32)
        for h in (0, 1):
            part = part + mm_nt(
                d_kv[rows, 384 * h : 384 * h + 384], g_qkv[h, :, :, :, 384:768].reshape(768, 384)
            )
            part = part + mm_nt(
                d_kv[rows, 768 + 384 * h : 1152 + 384 * h], g_qkv[h, :, :, :, 768:1152].reshape(768, 384)
            )
        dn[n] = part.astype(bf16)
        block = whole_tokens[rows].astype(f32)
        r = lax.rsqrt(jnp.mean(block * block, -1, keepdims=True) + epsilon)
        result[0:1] += jnp.sum(part * block * r, 0, keepdims=True)

    dn_copies = [
        remote(dn.at[lax.rem(o.x + by, 4)], dn_in.at[by - 1], dn_send.at[by - 1], dn_recv.at[by - 1], o.along_x(by))
        for by in (1, 2, 3)
    ]
    for copy in dn_copies:
        copy.start()
    d_own = jnp.zeros((128, 768), f32)
    for h in (0, 1):
        d_own = d_own + mm_nt(
            d_query[:, 384 * h : 384 * h + 384], g_qkv[h, :, :, :, 0:384].reshape(768, 384)
        )
    r_one = lax.rsqrt(jnp.mean(x * x, -1, keepdims=True) + epsilon)
    grad_norm_one = result[0:1] + jnp.sum(d_own * x * r_one, 0, keepdims=True)
    row = lax.broadcasted_iota(jnp.int32, (8, 768), 0)
    top = jnp.where(row == 0, grad_norm_one, jnp.where(row == 1, grad_norm_two[None, :], grad_router))
    small[0] = jnp.concatenate([top, grad_table[0:8], grad_table[8:16]], 1)
    tot.start(0)
    fq.ring_far()
    tot.add(0)
    tot.start(1)
    total_q, total_a, total_i = (stage.at[:, pl.ds(a, n)] for a, n in ((0, 1152), (1152, 384), (1536, 1536)))
    out_out[...] = fo.total()

    def hand(k, total, out, value, blocks):
        total[...] = value
        n = value.shape[1] // blocks
        copies = []
        for t in range(blocks):
            mine = pl.ds(pl.multiple_of(o.c * n + 2 * t * n, 128), n)
            out[:, mine] = total[pl.ds(pl.multiple_of(24 * o.c, 8), 24), t * n : t * n + n]
            copies.append(
                remote(
                    total.at[pl.ds(pl.multiple_of(24 * (1 - o.c), 8), 24), pl.ds(t * n, n)], out.at[:, mine],
                    last_send.at[k + t], last_recv.at[k + t], o.sibling(),
                )
            )
            copies[-1].start()
        return copies

    last = hand(0, total_i, out_in, fi.total(), 1)
    total_a[...] = fa.total()
    tot.add(1)
    tot.start(2)
    fq.across()
    for copy in dn_copies:
        copy.wait_recv()
    d_normed = d_own + dn[o.x].astype(f32)
    for by in (0, 1, 2):
        d_normed = d_normed + dn_in[by].astype(f32)
    d_resid, _ = rms_backward(x, r_one, gain_one, d_normed)
    d_tokens[...] = (d_after_ref[...] + d_resid).astype(bf16)
    tot.add(2)
    tot.start(3)
    dense = jnp.concatenate([fq.total(), total_a[...]], 1).astype(bf16)
    for j in range(4):
        xs[j] = dense[:, j * 384 : (j + 1) * 384]
    first = [
        remote(xs.at[lax.rem(o.x + by, 4)], xr.at[by - 1], x_send.at[by - 1], x_recv.at[by - 1], o.along_x(by))
        for by in (1, 2, 3)
    ]
    for copy in first:
        copy.start()
    for copy in first:
        copy.wait_recv()
    own = xs[o.x].astype(f32)
    for j in range(3):
        own = own + xr[j].astype(f32)
    xa[o.x] = own.astype(bf16)
    second = [
        remote(xa.at[o.x], xa.at[o.x], x_send.at[by + 2], x_recv.at[by + 2], o.along_x(by)) for by in (1, 2, 3)
    ]
    for copy in second:
        copy.start()
    for copy in second:
        copy.wait_recv()
    whole = jnp.concatenate([xa[0], xa[1], xa[2], xa[3]], 1).astype(f32)
    last += hand(1, total_q, out_qkv, whole[:, :1152], 3)
    last += hand(4, total_a, out_ao, whole[:, 1152:], 1)
    tot.add(3)
    take = lax.broadcasted_iota(jnp.int32, (768, 128), 0) == lax.broadcasted_iota(jnp.int32, (768, 128), 1) + 24 * o.d
    own_small[:, 0:128] = jnp.dot(
        small[4, :, 0:768], jnp.where(take, 1.0, 0.0), precision=highest, preferred_element_type=f32
    )
    heads_of = jnp.concatenate([small[4, :, 768:896], small[4, :, 896:1024]], 0)
    mine = jnp.where(lax.broadcasted_iota(jnp.int32, (16, 128), 1) == o.d, heads_of, 0.0)
    column = jnp.broadcast_to(jnp.sum(mine, -1, keepdims=True), (16, 128))
    same = lax.broadcasted_iota(jnp.int32, (16, 128), 0) == lax.broadcasted_iota(jnp.int32, (16, 128), 1)
    own_small[0:1, 128:256] = jnp.sum(jnp.where(same, column, 0.0), 0, keepdims=True)
    for copy in last:
        copy.wait_recv()
    for copy in results_back + grads_back + dn_copies + tok_copies + first + second + last:
        copy.wait_send()
    tot.drain()
    for f in (fq, fa, fi, fo):
        f.drain([(0, 4)])
    pair_copy.wait_send()
    side.drain()
    for f in flows:
        f.drain()


def layer(*operands):
    vm = pl.BlockSpec(memory_space=pltpu.VMEM)
    dma = pltpu.SemaphoreType.DMA

    def low(*shape):
        return pltpu.VMEM(shape, bf16)

    def full(*shape):
        return pltpu.VMEM(shape, f32)

    sizes = ((48, 1152), (48, 384), (48, 1536), (96, 768))
    weights = (low(2, 4, 4, 48, 1152), low(2, 4, 4, 48, 384), low(2, 4, 4, 48, 1536), low(4, 4, 2, 96, 768))
    return pl.pallas_call(
        layer_kernel,
        in_specs=[vm] * len(operands),
        out_specs=[vm] * 7,
        out_shape=[
            jax.ShapeDtypeStruct((128, 768), bf16),
            jax.ShapeDtypeStruct((128, 768), bf16),
            jax.ShapeDtypeStruct((24, 2304), f32),
            jax.ShapeDtypeStruct((24, 768), f32),
            jax.ShapeDtypeStruct((24, 3072), f32),
            jax.ShapeDtypeStruct((96, 768), f32),
            jax.ShapeDtypeStruct((8, 256), f32),
        ],
        scratch_shapes=[
            full(5, 8, 1024), pltpu.VMEM((1, 1024), jnp.int32), full(48, 3072), full(24, 3072), dma((2,)), dma((4, 17)), dma((4, 11)),
            full(4, 8, 1024), full(7, 8, 1024), dma((7,)), dma((7,)),
            *weights, low(512, 768), dma((3,)), dma((3,)), low(512, 768), low(768, 512), low(128, 768), low(512, 1536), full(16, 640),
            low(12, 128, 512), low(128, 768), full(128, 768), low(128, 768), low(128, 192),
            full(128, 8), full(128, 8), low(2, 4, 48, 768), low(2, 4, 48, 768), dma((2, 3)), dma((2, 3)),
            low(192, 768), low(192, 768), low(4, 192, 768), low(4, 192, 768),
            *weights,
            low(768, 192), full(192, 768), low(2, 4, 48, 768),
            low(512, 1536), low(3, 128, 768), full(16, 640),
            low(4, 48, 384), low(3, 48, 384), low(4, 48, 384),
            *[low(4, 4, *s) for s in sizes[1:]],
            *[low(2, 2, *s) for s in sizes],
            *[low(2, 4, *s) for s in sizes],
            *[low(3, *s) for s in sizes],
            dma((4, 11)), dma((4, 11)), dma((2, 3)), dma((2, 3)), dma((3,)), dma((3,)),
            dma((6,)), dma((6,)), dma((5,)), dma((5,)),
            full(10, 8, 1024), dma((10,)), dma((10,)),
        ],
        compiler_params=pltpu.CompilerParams(
            collective_id=0, has_side_effects=True, vmem_limit_bytes=63 * 2**20
        ),
    )(*operands)


def emit_kernel(
    mixed, d_tokens, qkv, ao, first, second, own,
    o_mixed, o_tokens, o_na, o_qkv, o_ao, o_table, o_nm, o_router, o_first, o_second,
):
    o_mixed[...] = mixed[...]
    o_tokens[...] = d_tokens[...]
    o_qkv[...] = qkv[...]
    o_ao[...] = ao[...]
    o_first[:, 0, :] = first[...]
    o_second[:, 0, :] = second[...]
    o_na[...] = own[0:1, 0:24]
    o_nm[...] = own[1:2, 0:24]
    o_router[...] = own[2:6, 0:24]
    o_table[...] = own[0:1, 128:140]


def emit(*results):
    vm = pl.BlockSpec(memory_space=pltpu.VMEM)
    kinds = (
        ((128, 768), bf16), ((128, 768), bf16), ((1, 24), f32), ((24, 2304), f32), ((24, 768), f32),
        ((1, 12), f32), ((1, 24), f32), ((4, 24), f32), ((24, 1, 3072), f32), ((96, 1, 768), f32),
    )
    return pl.pallas_call(
        emit_kernel,
        in_specs=[vm] * 7,
        out_specs=[vm] * 10,
        out_shape=[jax.ShapeDtypeStruct(shape, kind) for shape, kind in kinds],
    )(*results)


def per_device(
    tokens, norm_attn, w_qkv, w_attn_out, bias_table, norm_moe, router, w_in, w_out, routes, buckets, cotangent
):
    results = layer(
        w_qkv, w_attn_out, w_in[:, 0], w_out[:, 0], norm_attn[None, :], norm_moe[None, :], router.T, bias_table,
        tokens, routes.T, buckets[None, :], cotangent,
    )
    mixed, d_tokens, g_na, g_qkv, g_ao, g_table, g_nm, g_router, g_in, g_out = emit(*results)
    return mixed, d_tokens, g_na[0], g_qkv, g_ao, g_table, g_nm[0], g_router.T, g_in, g_out


def solution(mesh):
    both = ("dp", "expert")
    in_specs = (
        P(both, None), P("dp"), P("dp", None), P("dp", None), P("dp", None), P("dp"), P("dp", None),
        P("dp", "expert", None), P("dp", "expert", None), P(both, None), P(), P(both, None),
    )
    out_specs = (
        P(both, None), P(both, None), P("dp"), P("dp", None), P("dp", None), P("dp", None), P("dp"),
        P("dp", None), P("dp", "expert", None), P("dp", "expert", None),
    )
    return jax.shard_map(
        per_device, mesh=mesh, in_specs=in_specs, out_specs=out_specs, check_vma=False
    )
```

```python
import jax
import jax.numpy as jnp
from jax import lax
from jax.experimental import pallas as pl
from jax.experimental.pallas import tpu as pltpu
from jax.sharding import PartitionSpec as P

epsilon = 1e-06
highest = lax.Precision.HIGHEST
bf16 = jnp.bfloat16
f32 = jnp.float32
NT = (((1,), (1,)), ((), ()))
TN = (((0,), (0,)), ((), ()))


def mm(a, b):
    return jnp.dot(a, b, preferred_element_type=f32)


def mm_nt(a, b):
    return lax.dot_general(a, b, NT, preferred_element_type=f32)


def mm_tn(a, b):
    return lax.dot_general(a, b, TN, preferred_element_type=f32)


def stack_heads(pair):
    left = lax.broadcasted_iota(jnp.int32, pair.shape, 1) < 64
    zero = jnp.zeros_like(pair)
    return jnp.concatenate([jnp.where(left, pair, zero), jnp.where(left, zero, pair)], 0)


def join_pair(stacked):
    rows = stacked.shape[0] // 2
    left = lax.broadcasted_iota(jnp.int32, (rows, 128), 1) < 64
    return jnp.where(left, stacked[:rows], stacked[rows:])


def toeplitz(window_row, rows, keys):
    width = window_row.shape[1]
    wide = jnp.broadcast_to(window_row, (rows, width))
    rolled = pltpu.roll(wide, width - (rows - 1), 1, stride=1, stride_axis=0)
    return rolled[:, :keys]


def diagonal_sums(block, width):
    rows, keys = block.shape
    wide = jnp.concatenate([block, jnp.zeros((rows, width - keys), f32)], 1)
    half = rows // 2
    while half >= 8:
        wide = wide[:half] + pltpu.roll(wide[half:], width - half, 1)
        half //= 2
    row = lax.broadcasted_iota(jnp.int32, wide.shape, 0)
    for bit in (1, 2, 4):
        wide = jnp.where((row & bit) != 0, pltpu.roll(wide, width - bit, 1), wide)
    total = jnp.sum(wide, 0, keepdims=True)
    return pltpu.roll(total, rows - 1, 1)


def rms_forward(values, gain):
    r = lax.rsqrt(jnp.mean(values * values, -1, keepdims=True) + epsilon)
    return r, values * r * gain


def rms_backward(values, r, gain, grad):
    u = grad * gain
    d_values = r * u - values * (r * r * r) * jnp.mean(u * values, -1, keepdims=True)
    return d_values, jnp.sum(grad * values * r, 0)


MESH = pl.DeviceIdType.MESH


class Place:
    def __init__(self):
        d = lax.axis_index("dp")
        self.d = d
        self.x = lax.axis_index("expert")
        self.c = lax.rem(d, 2)
        self.z = lax.rem(lax.div(d, 2), 4)
        self.y = lax.div(d, 8)
        self.p = self.z * (1 - self.c) + self.y * self.c
        self.q = self.y * (1 - self.c) + self.z * self.c

    def at(self, p, q):
        y = q * (1 - self.c) + p * self.c
        z = p * (1 - self.c) + q * self.c
        return ((y * 4 + z) * 2 + self.c, self.x)

    def along_p(self, by):
        return self.at(lax.rem(self.p + by, 4), self.q)

    def along_q(self, by):
        return self.at(self.p, lax.rem(self.q + by, 4))

    def along_x(self, by):
        return (self.d, lax.rem(self.x + by, 4))

    def sibling(self):
        return (self.d + 1 - 2 * self.c, self.x)

    def each_core(self, body):
        pl.when(self.c == 0)(lambda: body(0))
        pl.when(self.c == 1)(lambda: body(1))

    def barrier(self, with_x):
        peers = [self.sibling()] + [self.along_p(i) for i in (1, 2, 3)]
        peers += [self.along_q(i) for i in (1, 2, 3)]
        if with_x:
            peers += [self.along_x(i) for i in (1, 2, 3)]
        sem = pltpu.get_barrier_semaphore()
        for peer in peers:
            pl.semaphore_signal(sem, inc=1, device_id=peer, device_id_type=MESH)
        return lambda: pl.semaphore_wait(sem, len(peers))


def remote(src, dst, send, recv, to):
    return pltpu.make_async_remote_copy(
        src_ref=src, dst_ref=dst, send_sem=send, recv_sem=recv, device_id=to, device_id_type=MESH
    )


def block_of(ref, tall, k, p, q):
    y, z = (q, p) if k == 0 else (p, q)
    return ref.at[y, z, k] if tall else ref.at[k, y, z]


def slab_of(ref, tall, k, q, low=0, count=4):
    y, z = (q, pl.ds(low, count)) if k == 0 else (pl.ds(low, count), q)
    return ref.at[y, z, k] if tall else ref.at[k, y, z]


class Gather:
    sends = 11
    recvs = 11

    def __init__(self, place, ref, tall, send, recv, number):
        self.o, self.ref, self.tall, self.send, self.recv = place, ref, tall, send, recv
        self.number = number

    def block(self, k, by):
        return block_of(self.ref, self.tall, k, lax.rem(self.o.p + by, 4), self.o.q)

    def slab(self, k, by, low=0, count=4):
        return slab_of(self.ref, self.tall, k, lax.rem(self.o.q + by, 4), low, count)

    def go(self, part, s, r, to):
        def body(k):
            src = part(k)
            remote(src, src, self.send.at[s], self.recv.at[r], to).start()

        self.o.each_core(body)

    def arrived(self, r, count):
        if count == 1:
            view = block_of(self.ref, self.tall, 0, 0, 0)
        else:
            view = slab_of(self.ref, self.tall, 0, 0, 0, count)
        remote(view, view, self.send.at[0], self.recv.at[r], self.o.sibling()).wait_recv()

    def sent(self, s, count):
        if count == 1:
            view = block_of(self.ref, self.tall, 0, 0, 0)
        else:
            view = slab_of(self.ref, self.tall, 0, 0, 0, count)
        remote(view, view, self.send.at[s], self.recv.at[0], self.o.sibling()).wait_send()

    def ring_one(self):
        self.go(lambda k: self.block(k, 0), 0, 0, self.o.along_p(1))
        self.go(lambda k: self.block(k, 0), 1, 1, self.o.along_p(3))
        if self.number == 0:
            self.go(lambda k: self.block(k, 0), 2, 2, self.o.along_p(2))

    def ring_one_far(self):
        self.arrived(0, 1)
        self.arrived(1, 1)
        if self.number == 0:
            return
        if self.number % 2 == 0:
            self.go(lambda k: self.block(k, 3), 2, 2, self.o.along_p(1))
        else:
            self.go(lambda k: self.block(k, 1), 2, 2, self.o.along_p(3))

    def ring_two_block(self, by):
        n = 3 if by == 0 else 9 + 2 * by
        self.go(lambda k: self.block(k, by), n, 3, self.o.along_q(1))
        self.go(lambda k: self.block(k, by), 4 if by == 0 else n + 1, 4, self.o.along_q(3))

    def ring_two(self):
        self.arrived(2, 1)
        for by in (1, 2, 3):
            self.ring_two_block(by)
        self.go(lambda k: self.slab(k, 0), 7, 7, self.o.sibling())

    def ring_two_far(self):
        self.arrived(3, 4)
        self.go(lambda k: self.slab(k, 3, 0, 2), 5, 5, self.o.along_q(1))
        self.arrived(4, 4)
        self.go(lambda k: self.slab(k, 1, 2, 2), 6, 6, self.o.along_q(3))
        self.go(lambda k: self.slab(k, 3), 8, 8, self.o.sibling())
        self.go(lambda k: self.slab(k, 1), 9, 9, self.o.sibling())

    def last(self):
        self.arrived(5, 2)
        self.arrived(6, 2)
        self.go(lambda k: self.slab(k, 2), 10, 10, self.o.sibling())

    def finish(self):
        for r in (7, 8, 9, 10):
            self.arrived(r, 4)

    def drain(self):
        for s, count in ((0, 1), (1, 1), (2, 1), (3, 1), (4, 1), (5, 2), (6, 2), (7, 4), (8, 4), (9, 4), (10, 4),
                         *((n, 1) for n in range(11, 17))):
            self.sent(s, count)


class SmallSum:
    def __init__(self, place, value, arrivals, send, recv, with_x):
        self.o, self.value, self.arrivals, self.send, self.recv = place, value, arrivals, send, recv
        o = place
        self.steps = [[o.sibling()], [o.along_p(i) for i in (1, 2, 3)], [o.along_q(i) for i in (1, 2, 3)]]
        if with_x:
            self.steps.append([o.along_x(i) for i in (1, 2, 3)])
        self.copies = []
        n = 0
        for s, peers in enumerate(self.steps):
            row = []
            for peer in peers:
                row.append(
                    remote(value.at[s], arrivals.at[n], send.at[n], recv.at[n], peer)
                )
                n += 1
            self.copies.append(row)

    def start(self, s):
        for copy in self.copies[s]:
            copy.start()

    def add(self, s):
        first = sum(len(row) for row in self.copies[:s])
        total = self.value[s]
        for i, copy in enumerate(self.copies[s]):
            copy.wait_recv()
            total = total + self.arrivals[first + i]
        self.value[s + 1] = total

    def drain(self):
        for row in self.copies:
            for copy in row:
                copy.wait_send()


def place_small(o, out, na, nm, router_t, table):
    row = lax.broadcasted_iota(jnp.int32, (24, 768), 0)
    lane = lax.broadcasted_iota(jnp.int32, (24, 768), 1)
    hit = jnp.where(lane == 24 * o.d + row, 1.0, 0.0)
    out[...] = jnp.zeros((8, 1024), f32)
    out[0:1, 0:768] = mm(na[...].astype(f32), hit)
    out[1:2, 0:768] = mm(nm[...].astype(f32), hit)
    out[2:6, 0:768] = mm(router_t[...].astype(f32), hit)
    head = lax.broadcasted_iota(jnp.int32, (16, 12), 0) == lax.broadcasted_iota(jnp.int32, (16, 12), 1)
    wide = jnp.broadcast_to(table[...].astype(f32), (16, 12))
    column = jnp.sum(jnp.where(head, wide, 0.0), -1, keepdims=True)
    own = lax.broadcasted_iota(jnp.int32, (16, 128), 1) == o.d
    placed = jnp.where(own, jnp.broadcast_to(column, (16, 128)), 0.0)
    out[:, 768:896] = placed[0:8]
    out[:, 896:1024] = placed[8:16]


def meet(o, halves, stage, other, sem):
    at = 0
    for ref, blocks in halves:
        n = ref.shape[1] // (2 * blocks)
        for t in range(blocks):
            own = pl.ds(pl.multiple_of(o.c * n + 2 * t * n, 128), n)
            theirs = pl.ds(pl.multiple_of((1 - o.c) * n + 2 * t * n, 128), n)
            stage[pl.ds(pl.multiple_of(24 * o.c, 8), 24), at : at + n] = ref[:, own].astype(f32)
            other[:, at : at + n] = ref[:, theirs].astype(f32)
            at += n
    return remote(
        other, stage.at[pl.ds(pl.multiple_of(24 * o.c, 8), 24)], sem.at[0], sem.at[1], o.sibling()
    )


class Scatter:
    def __init__(self, place, ref, tall, pair, far, near, side, send, recv):
        self.o, self.ref, self.tall = place, ref, tall
        self.pair, self.far, self.near, self.side = pair, far, near, side
        self.send, self.recv = send, recv

    def where(self, p, q):
        o = self.o
        return q * (1 - o.c) + p * o.c, p * (1 - o.c) + q * o.c

    def q_at(self, by):
        return lax.rem(self.o.q + by, 4)

    def own(self, p, q):
        y, z = self.where(p, q)
        return (y, z, self.o.c) if self.tall else (self.o.c, y, z)

    def to_pair(self, s, low, count):
        rows = pl.ds(low, count)
        theirs = 1 - self.o.c
        src = self.ref.at[rows, :, theirs] if self.tall else self.ref.at[theirs, rows]
        remote(src, self.pair.at[rows], self.send.at[s], self.recv.at[s], self.o.sibling()).start()

    def from_pair(self, s, count):
        view = self.pair.at[pl.ds(0, count)]
        remote(view, view, self.send.at[s], self.recv.at[s], self.o.sibling()).wait_recv()

    def add_pair(self, by):
        q = self.q_at(by)

        def body(p, carry):
            y, z = self.where(p, q)
            at = self.own(p, q)
            self.ref[at] = (self.ref[at].astype(f32) + self.pair[y, z].astype(f32)).astype(bf16)
            return carry

        lax.fori_loop(0, 4, body, 0)

    def go(self, s, by, low, dst, to):
        def body(k):
            src = slab_of(self.ref, self.tall, k, self.q_at(by), low, 2)
            remote(src, dst, self.send.at[s], self.recv.at[s], to).start()

        self.o.each_core(body)

    def ring(self):
        o = self.o
        self.add_pair(2)
        self.go(2, 2, 0, self.far.at[0], o.along_q(1))
        self.go(3, 2, 2, self.far.at[1], o.along_q(3))
        self.add_pair(1)
        self.go(4, 1, 2, self.near.at[0, pl.ds(2, 2)], o.along_q(1))
        self.add_pair(3)
        self.go(5, 3, 0, self.near.at[1, pl.ds(0, 2)], o.along_q(3))
        self.add_pair(0)

    def landed(self, s, view):
        remote(view, view, self.send.at[s], self.recv.at[s], self.o.sibling()).wait_recv()

    def add_far(self, i, by, low):
        q = self.q_at(by)

        def body(j, carry):
            at = self.own(low + j, q)
            self.ref[at] = (self.ref[at].astype(f32) + self.far[i, j].astype(f32)).astype(bf16)
            return carry

        lax.fori_loop(0, 2, body, 0)

    def ring_far(self):
        o = self.o
        self.landed(2, self.far.at[0])
        self.add_far(0, 1, 0)
        self.go(6, 1, 0, self.near.at[0, pl.ds(0, 2)], o.along_q(1))
        self.landed(3, self.far.at[1])
        self.add_far(1, 3, 2)
        self.go(7, 3, 2, self.near.at[1, pl.ds(2, 2)], o.along_q(3))

    def across(self):
        o = self.o
        half = self.near.at[0, pl.ds(0, 2)]
        for s in (4, 5, 6, 7):
            self.landed(s, half)

        def body(p, carry):
            at = self.own(p, o.q)
            total = self.ref[at].astype(f32) + self.near[0, p].astype(f32)
            self.ref[at] = (total + self.near[1, p].astype(f32)).astype(bf16)
            return carry

        lax.fori_loop(0, 4, body, 0)
        for i in (1, 2, 3):
            src = self.ref.at[self.own(lax.rem(o.p + i, 4), o.q)]
            remote(
                src, self.side.at[i - 1], self.send.at[7 + i], self.recv.at[7 + i], o.along_p(i)
            ).start()

    def total(self):
        o = self.o
        for i in (0, 1, 2):
            self.landed(8 + i, self.side.at[i])
        total = self.ref[self.own(o.p, o.q)].astype(f32)
        for i in (0, 1, 2):
            total = total + self.side[i].astype(f32)
        return total

    def sent(self, s, view):
        remote(view, view, self.send.at[s], self.recv.at[s], self.o.sibling()).wait_send()

    def drain(self, pair_parts):
        for s, count in pair_parts:
            self.sent(s, self.pair.at[pl.ds(0, count)])
        for s in range(2, 8):
            self.sent(s, self.far.at[0])
        for s in range(8, 11):
            self.sent(s, self.side.at[0])


SQ = 0.7978845608028654


def gelu_both(h):
    t = jnp.tanh(SQ * (h + 0.044715 * (h * h * h)))
    value = 0.5 * h * (1.0 + t)
    slope = 0.5 * (1.0 + t) + 0.5 * h * (1.0 - t * t) * (SQ * (1.0 + 3 * 0.044715 * (h * h)))
    return value, slope


def hidden_lanes(j):
    return lax.div(j, 2), pl.ds(pl.multiple_of(lax.rem(j, 2) * 768, 128), 768)


def expert_hidden(j, sent, g_in, acts, slopes):
    half, at = hidden_lanes(j)
    value, slope = gelu_both(mm(sent[...], g_in[half, :, :, :, at].reshape(768, 768)))
    acts[j] = value.astype(bf16)
    slopes[j] = slope.astype(bf16)


def expert_second_grad(j, d_result, acts, h_out):
    for r in (0, 1):
        part = acts[j, :, r * 384 : (r + 1) * 384]
        h_out[j, pl.ds(2 * r, 2)] = mm_tn(part, d_result[...]).astype(bf16).reshape(2, 2, 96, 768)


def expert_result(j, acts, g_out, result):
    result[...] += mm(acts[j], g_out[j].reshape(768, 768))


def expert_back(j, sent_t, d_result, slopes, g_in, g_out, h_in, d_incoming):
    half, at = hidden_lanes(j)
    d_act = mm_nt(d_result[...], g_out[j].reshape(768, 768))
    d_hidden = (d_act * slopes[j].astype(f32)).astype(bf16)
    for r in (0, 1):
        part = sent_t[r * 384 : (r + 1) * 384]
        h_in[half, pl.ds(2 * r, 2), :, :, at] = mm(part, d_hidden).astype(bf16).reshape(2, 4, 48, 768)
    d_incoming[...] += mm_nt(d_hidden, g_in[half, :, :, :, at].reshape(768, 768))


def pair_backward(i, query, kv, weights, d_heads, d_query, d_kv, d_window):
    lanes = pl.ds(pl.multiple_of(i * 128, 128), 128)
    value_lanes = pl.ds(pl.multiple_of(i * 128 + 768, 128), 128)
    kept = weights[pl.ds(2 * i, 2)].reshape(256, 512)
    probability = kept.astype(f32)
    d_stack = stack_heads(d_heads[:, lanes])
    d_weights = mm_nt(d_stack, kv[:, value_lanes])
    d_kv[:, value_lanes] = mm_tn(kept, d_stack).astype(bf16)
    d_scores = probability * (d_weights - jnp.sum(probability * d_weights, -1, keepdims=True))
    low = d_scores.astype(bf16)
    d_kv[:, lanes] = mm_tn(low, stack_heads(query[:, lanes])).astype(bf16)
    d_query[:, lanes] = join_pair(mm(low, kv[:, lanes])).astype(bf16)
    for j in (0, 1):
        d_window[pl.ds(2 * i + j, 1), :] = diagonal_sums(d_scores[j * 128 : (j + 1) * 128], 640)


def pair_forward(i, query, kv, window, heads_out, weights):
    lanes = pl.ds(pl.multiple_of(i * 128, 128), 128)
    value_lanes = pl.ds(pl.multiple_of(i * 128 + 768, 128), 128)
    bias = jnp.concatenate([toeplitz(window[pl.ds(2 * i + j, 1), :], 128, 512) for j in (0, 1)], 0)
    scores = mm_nt(stack_heads(query[:, lanes]), kv[:, lanes]) + bias
    top = jnp.max(scores, -1, keepdims=True)
    raised = jnp.exp(scores - top)
    probability = raised / jnp.sum(raised, -1, keepdims=True)
    low = probability.astype(bf16)
    weights[pl.ds(2 * i, 2)] = low.reshape(2, 128, 512)
    heads_out[:, lanes] = join_pair(mm(low, kv[:, value_lanes])).astype(bf16)


def layer_kernel(
    w_qkv, w_ao, w_in, w_out, na, nm, router_t, table, tokens, routes, bucket_list, cotangent,
    mixed, d_tokens, out_qkv, out_ao, out_in, out_out, own_small,
    small, buckets, stage, other, pair_sem, g_sends, g_recvs, side_in, side_arrivals, side_send, side_recv,
    g_qkv, g_ao, g_in, g_out, whole_tokens, tok_send, tok_recv, normed_ref, normed_t, query, kv, window, weights, heads_out,
    after_attn, moe_input, placing, probs, chosen, disp, inc, disp_send, disp_recv, sent, d_result, acts, slopes,
    h_qkv, h_ao, h_in, h_out, sent_t, result, back, d_kv, dn_in, d_window,
    xs, xr, xa,
    pair_a, pair_i, pair_o, far_q, far_a, far_i, far_o, near_q, near_a, near_i, near_o,
    side_q, side_a, side_i, side_o,
    sends, recvs, ret_send, ret_recv, dn_send, dn_recv, x_send, x_recv, last_send, last_recv,
    arrivals, small_send, small_recv,
):
    d_heads_ref, d_after_ref, d_query = heads_out, after_attn, query
    o = Place()
    entered = o.barrier(True)
    flows = [
        Gather(o, ref, tall, g_sends.at[i], g_recvs.at[i], i)
        for i, (ref, tall) in enumerate(((g_qkv, 0), (g_ao, 0), (g_in, 0), (g_out, 1)))
    ]
    qkv, ao, win, wout = flows
    pair_copy = meet(o, ((w_qkv, 3), (w_ao, 1), (w_in, 1)), stage, other, pair_sem)
    side = SmallSum(o, side_in, side_arrivals, side_send, side_recv, False)
    place_small(o, side_in.at[0], na, nm, router_t, table)
    buckets[...] = jnp.zeros_like(buckets)
    buckets[:, 0:1023] = bucket_list[...]
    g_out[o.y, o.z, o.c] = w_out[...]
    own_rows = pl.ds(pl.multiple_of(o.x * 128, 128), 128)
    whole_tokens[own_rows] = tokens[...]
    entered()
    pair_copy.start()
    side.start(0)
    wout.ring_one()
    wout.ring_two_block(0)
    pair_copy.wait_recv()
    at = 0
    for ref in (g_qkv, g_ao, g_in):
        n = ref.shape[-1]
        ref[o.c, o.y, o.z] = stage[:, at : at + n].astype(bf16)
        at += n
    qkv.ring_one()
    qkv.ring_two_block(0)
    side.add(0)
    side.start(1)
    tok_copies = [
        remote(
            whole_tokens.at[own_rows], whole_tokens.at[own_rows], tok_send.at[by - 1], tok_recv.at[by - 1],
            o.along_x(by),
        )
        for by in (1, 2, 3)
    ]
    for copy in tok_copies:
        copy.start()
    win.ring_one()
    ao.ring_one()
    ao.ring_two_block(0)
    win.ring_two_block(0)
    qkv.ring_one_far()
    qkv.ring_two()
    side.add(1)
    side.start(2)
    x = tokens[...].astype(f32)
    bucket_row = buckets[:, pl.ds(pl.multiple_of((3 - o.x) * 128, 128), 640)]
    picks = jnp.where(
        jnp.broadcast_to(bucket_row, (128, 640)) == lax.broadcasted_iota(jnp.int32, (128, 640), 0), 1.0, 0.0
    )
    for f in (wout, win, ao):
        f.ring_one_far()
    ao.ring_two()
    win.ring_two()
    qkv.ring_two_far()
    wout.ring_two()
    for copy in tok_copies:
        copy.wait_recv()
    side.add(2)
    small_in = side_in.at[3]
    gain_row = small_in[0:1, :768]

    def norm_rows(n, carry):
        rows = pl.ds(n * 128, 128)
        _, normed = rms_forward(whole_tokens[rows].astype(f32), gain_row)
        normed_ref[rows] = normed.astype(bf16)
        normed_t[:, rows] = normed.T.astype(bf16)
        return carry

    for n in range(4):
        norm_rows(n, 0)
    table_t = jnp.concatenate([small_in[:, 768:896], small_in[:, 896:1024]], 0)
    window[...] = mm(table_t.astype(bf16), picks.astype(bf16))
    qkv.last()
    ao.ring_two_far()
    qkv.finish()

    for h in (0, 1):
        query[:, 384 * h : 384 * h + 384] = mm(
            normed_ref[own_rows], g_qkv[h, :, :, :, 0:384].reshape(768, 384)
        ).astype(bf16)

    def project_rows(n, carry):
        rows = pl.ds(pl.multiple_of(n * 128, 128), 128)
        for h in (0, 1):
            both = mm(normed_ref[rows], g_qkv[h, :, :, :, 384:1152].reshape(768, 768)).astype(bf16)
            kv[rows, 384 * h : 384 * h + 384] = both[:, :384]
            kv[rows, 768 + 384 * h : 1152 + 384 * h] = both[:, 384:]
        return carry

    lax.fori_loop(0, 4, project_rows, 0)
    ao.last()

    def ahead(i, carry):
        pair_forward(i, query, kv, window, heads_out, weights)
        return carry

    lax.fori_loop(0, 3, ahead, 0)
    win.ring_two_far()
    lax.fori_loop(3, 6, ahead, 0)
    ao.finish()
    mixed_heads = heads_out[...]
    attn = x + jnp.concatenate([mm(mixed_heads, g_ao[h].reshape(768, 384)) for h in (0, 1)], 1)
    after_attn[...] = attn
    small8 = small_in[:, :768]
    r_two = lax.rsqrt(jnp.mean(attn * attn, -1, keepdims=True) + epsilon)
    moe_low = (attn * r_two * small8[1:2]).astype(bf16)
    moe_input[...] = moe_low
    logits = mm_nt(moe_low, small8.astype(bf16))
    lane = lax.broadcasted_iota(jnp.int32, (128, 8), 1)
    logits = jnp.where((lane >= 2) & (lane < 6), logits, -1e30)
    raised = jnp.exp(logits - jnp.max(logits, -1, keepdims=True))
    probability = raised / jnp.sum(raised, -1, keepdims=True)
    probs[...] = probability
    named = jnp.broadcast_to(routes[...], (8, 128)) + 2
    picked = jnp.where(lax.broadcasted_iota(jnp.int32, (8, 128), 0) == named, 1.0, 0.0).T
    chosen[...] = picked
    gate = jnp.sum(probability * picked, -1, keepdims=True)
    before = jnp.where(
        lax.broadcasted_iota(jnp.int32, (128, 128), 1) < lax.broadcasted_iota(jnp.int32, (128, 128), 0), 1.0, 0.0
    )
    slot = jnp.sum(mm(before.astype(bf16), picked.astype(bf16)) * picked, -1, keepdims=True)
    column = jnp.sum(picked * ((lane - 2) * 48).astype(f32), -1, keepdims=True) + slot
    place = jnp.where(
        lax.broadcasted_iota(jnp.int32, (128, 192), 1).astype(f32) == column, 1.0, 0.0
    ).astype(bf16)
    placing[...] = place
    def dispatch(part, value):
        disp[part] = mm_tn(place, value).astype(bf16).reshape(4, 48, 768)
        copies = [
            remote(
                disp.at[part, lax.rem(o.x + by, 4)], inc.at[part, o.x],
                disp_send.at[part, by - 1], disp_recv.at[part, by - 1], o.along_x(by),
            )
            for by in (1, 2, 3)
        ]
        for copy in copies:
            copy.start()
        inc[part, o.x] = disp[part, o.x]
        return copies

    tokens_out = dispatch(0, moe_low)
    grads_out = dispatch(1, (gate * cotangent[...].astype(f32)).astype(bf16))
    win.last()
    wout.ring_two_far()
    for copy in tokens_out:
        copy.wait_recv()
    sent[...] = inc[0].reshape(192, 768)
    sent_t[...] = sent[...].astype(f32).T.astype(bf16)
    win.finish()
    pair_q = pair_i.at[:, :, :, pl.ds(0, 1152)]
    fq = Scatter(o, h_qkv, 0, pair_q, far_q, near_q, side_q, sends.at[0], recvs.at[0])
    fa = Scatter(o, h_ao, 0, pair_a, far_a, near_a, side_a, sends.at[1], recvs.at[1])
    fi = Scatter(o, h_in, 0, pair_i, far_i, near_i, side_i, sends.at[2], recvs.at[2])
    fo = Scatter(o, h_out, 1, pair_o, far_o, near_o, side_o, sends.at[3], recvs.at[3])
    tot = SmallSum(o, small, arrivals, small_send, small_recv, True)

    def times(low, high, body):
        def step(j, carry):
            body(j)
            return carry

        lax.fori_loop(low, high, step, 0)

    times(0, 4, lambda j: expert_hidden(j, sent, g_in, acts, slopes))
    wout.last()
    for copy in grads_out:
        copy.wait_recv()
    d_result[...] = inc[1].reshape(192, 768)
    times(0, 4, lambda j: expert_second_grad(j, d_result, acts, h_out))
    fo.to_pair(0, 0, 4)
    wout.finish()
    result[...] = jnp.zeros_like(result)
    times(0, 4, lambda j: expert_result(j, acts, g_out, result))

    def send_back(part, value):
        for copy in (tokens_out, grads_out)[part]:
            copy.wait_send()
        ret = disp
        ret[part] = value.astype(bf16).reshape(4, 48, 768)
        copies = [
            remote(
                ret.at[part, lax.rem(o.x + by, 4)], back.at[part, o.x],
                ret_send.at[part, by - 1], ret_recv.at[part, by - 1], o.along_x(by),
            )
            for by in (1, 2, 3)
        ]
        for copy in copies:
            copy.start()
        back[part, o.x] = ret[part, o.x]
        return copies

    results_back = send_back(0, result[...])
    d_incoming = result
    d_incoming[...] = jnp.zeros_like(d_incoming)
    start = 2 * (1 - o.c)

    def back_chunk(j):
        expert_back(j, sent_t, d_result, slopes, g_in, g_out, h_in, d_incoming)

    times(start, start + 2, back_chunk)
    fi.to_pair(0, 0, 4)
    fo.from_pair(0, 4)
    fo.ring()
    times(2 - start, 4 - start, back_chunk)
    grads_back = send_back(1, d_incoming[...])
    fi.from_pair(0, 4)
    fi.ring()
    fo.ring_far()
    for copy in results_back + grads_back:
        copy.wait_recv()

    gain_one, gain_two = small8[0:1], small8[1:2]
    returned = mm(placing[...], back[0].reshape(192, 768))
    d_moe = mm(placing[...], back[1].reshape(192, 768))
    attn = after_attn[...]
    r_two = lax.rsqrt(jnp.mean(attn * attn, -1, keepdims=True) + epsilon)
    upstream = cotangent[...].astype(f32)
    gate = jnp.sum(probs[...] * chosen[...], -1, keepdims=True)
    mixed[...] = (attn + gate * returned).astype(bf16)
    d_gate = jnp.sum(upstream * returned, -1, keepdims=True)
    d_logits = probs[...] * (d_gate * chosen[...] - d_gate * gate)
    d_moe = d_moe + jnp.dot(d_logits, small8, precision=highest, preferred_element_type=f32)
    grad_router = lax.dot_general(
        d_logits, moe_input[...].astype(f32), TN, precision=highest, preferred_element_type=f32
    )
    d_after, grad_norm_two = rms_backward(attn, r_two, gain_two, d_moe)
    d_after = d_after + upstream
    d_after_ref[...] = d_after
    d_attn = d_after.astype(bf16)
    d_heads = jnp.zeros((128, 768), f32)
    for h in (0, 1):
        part = d_attn[:, h * 384 : (h + 1) * 384]
        h_ao[h] = mm_tn(heads_out[...], part).astype(bf16).reshape(4, 4, 48, 384)
        d_heads = d_heads + mm_nt(part, g_ao[h].reshape(768, 384))
    fa.to_pair(0, 0, 4)
    d_heads_ref[...] = d_heads.astype(bf16)

    d_window[...] = jnp.zeros_like(d_window)

    def pair(i):
        pair_backward(i, query, kv, weights, d_heads_ref, d_query, d_kv, d_window)

    def lanes_of(h, base):
        return pl.ds(pl.multiple_of(h * 384 + base, 128), 384)

    def dense_grad(h):
        for t, part in enumerate(
            (
                mm(normed_t[:, own_rows], d_query[:, lanes_of(h, 0)]),
                mm(normed_t[...], d_kv[:, lanes_of(h, 0)]),
                mm(normed_t[...], d_kv[:, lanes_of(h, 768)]),
            )
        ):
            h_qkv[h, :, :, :, t * 384 : t * 384 + 384] = part.astype(bf16).reshape(4, 4, 48, 384)

    theirs = 1 - o.c
    times(3 * theirs, 3 * theirs + 3, pair)
    dense_grad(theirs)
    fa.from_pair(0, 4)
    fq.to_pair(0, 0, 4)
    fa.ring()
    fi.ring_far()
    times(3 * o.c, 3 * o.c + 3, pair)
    dense_grad(o.c)
    fo.across()
    fa.ring_far()
    fq.from_pair(0, 4)
    fq.ring()
    fi.across()
    fa.across()
    grad_table = lax.dot_general(
        d_window[...], picks, NT, precision=highest, preferred_element_type=f32
    )
    result[0:8] = jnp.zeros((8, 768), f32)
    dn = acts.at[:, pl.ds(0, 128), :]

    for n in range(4):
        rows = pl.ds(n * 128, 128)
        part = jnp.zeros((128, 768), f32)
        for h in (0, 1):
            part = part + mm_nt(
                d_kv[rows, 384 * h : 384 * h + 384], g_qkv[h, :, :, :, 384:768].reshape(768, 384)
            )
            part = part + mm_nt(
                d_kv[rows, 768 + 384 * h : 1152 + 384 * h], g_qkv[h, :, :, :, 768:1152].reshape(768, 384)
            )
        dn[n] = part.astype(bf16)
        block = whole_tokens[rows].astype(f32)
        r = lax.rsqrt(jnp.mean(block * block, -1, keepdims=True) + epsilon)
        result[0:1] += jnp.sum(part * block * r, 0, keepdims=True)

    dn_copies = [
        remote(dn.at[lax.rem(o.x + by, 4)], dn_in.at[by - 1], dn_send.at[by - 1], dn_recv.at[by - 1], o.along_x(by))
        for by in (1, 2, 3)
    ]
    for copy in dn_copies:
        copy.start()
    d_own = jnp.zeros((128, 768), f32)
    for h in (0, 1):
        d_own = d_own + mm_nt(
            d_query[:, 384 * h : 384 * h + 384], g_qkv[h, :, :, :, 0:384].reshape(768, 384)
        )
    r_one = lax.rsqrt(jnp.mean(x * x, -1, keepdims=True) + epsilon)
    grad_norm_one = result[0:1] + jnp.sum(d_own * x * r_one, 0, keepdims=True)
    row = lax.broadcasted_iota(jnp.int32, (8, 768), 0)
    top = jnp.where(row == 0, grad_norm_one, jnp.where(row == 1, grad_norm_two[None, :], grad_router))
    small[0] = jnp.concatenate([top, grad_table[0:8], grad_table[8:16]], 1)
    tot.start(0)
    fq.ring_far()
    tot.add(0)
    tot.start(1)
    total_q, total_a, total_i = (stage.at[:, pl.ds(a, n)] for a, n in ((0, 1152), (1152, 384), (1536, 1536)))
    out_out[...] = fo.total()

    def hand(k, total, out, value, blocks):
        total[...] = value
        n = value.shape[1] // blocks
        copies = []
        for t in range(blocks):
            mine = pl.ds(pl.multiple_of(o.c * n + 2 * t * n, 128), n)
            out[:, mine] = total[pl.ds(pl.multiple_of(24 * o.c, 8), 24), t * n : t * n + n]
            copies.append(
                remote(
                    total.at[pl.ds(pl.multiple_of(24 * (1 - o.c), 8), 24), pl.ds(t * n, n)], out.at[:, mine],
                    last_send.at[k + t], last_recv.at[k + t], o.sibling(),
                )
            )
            copies[-1].start()
        return copies

    last = hand(0, total_i, out_in, fi.total(), 1)
    total_a[...] = fa.total()
    tot.add(1)
    tot.start(2)
    fq.across()
    for copy in dn_copies:
        copy.wait_recv()
    d_normed = d_own + dn[o.x].astype(f32)
    for by in (0, 1, 2):
        d_normed = d_normed + dn_in[by].astype(f32)
    d_resid, _ = rms_backward(x, r_one, gain_one, d_normed)
    d_tokens[...] = (d_after_ref[...] + d_resid).astype(bf16)
    tot.add(2)
    tot.start(3)
    dense = jnp.concatenate([fq.total(), total_a[...]], 1).astype(bf16)
    for j in range(4):
        xs[j] = dense[:, j * 384 : (j + 1) * 384]
    first = [
        remote(xs.at[lax.rem(o.x + by, 4)], xr.at[by - 1], x_send.at[by - 1], x_recv.at[by - 1], o.along_x(by))
        for by in (1, 2, 3)
    ]
    for copy in first:
        copy.start()
    for copy in first:
        copy.wait_recv()
    own = xs[o.x].astype(f32)
    for j in range(3):
        own = own + xr[j].astype(f32)
    xa[o.x] = own.astype(bf16)
    second = [
        remote(xa.at[o.x], xa.at[o.x], x_send.at[by + 2], x_recv.at[by + 2], o.along_x(by)) for by in (1, 2, 3)
    ]
    for copy in second:
        copy.start()
    for copy in second:
        copy.wait_recv()
    whole = jnp.concatenate([xa[0], xa[1], xa[2], xa[3]], 1).astype(f32)
    last += hand(1, total_q, out_qkv, whole[:, :1152], 3)
    last += hand(4, total_a, out_ao, whole[:, 1152:], 1)
    tot.add(3)
    take = lax.broadcasted_iota(jnp.int32, (768, 128), 0) == lax.broadcasted_iota(jnp.int32, (768, 128), 1) + 24 * o.d
    own_small[:, 0:128] = jnp.dot(
        small[4, :, 0:768], jnp.where(take, 1.0, 0.0), precision=highest, preferred_element_type=f32
    )
    heads_of = jnp.concatenate([small[4, :, 768:896], small[4, :, 896:1024]], 0)
    mine = jnp.where(lax.broadcasted_iota(jnp.int32, (16, 128), 1) == o.d, heads_of, 0.0)
    column = jnp.broadcast_to(jnp.sum(mine, -1, keepdims=True), (16, 128))
    same = lax.broadcasted_iota(jnp.int32, (16, 128), 0) == lax.broadcasted_iota(jnp.int32, (16, 128), 1)
    own_small[0:1, 128:256] = jnp.sum(jnp.where(same, column, 0.0), 0, keepdims=True)
    for copy in last:
        copy.wait_recv()
    for copy in results_back + grads_back + dn_copies + tok_copies + first + second + last:
        copy.wait_send()
    tot.drain()
    for f in (fq, fa, fi, fo):
        f.drain([(0, 4)])
    pair_copy.wait_send()
    side.drain()
    for f in flows:
        f.drain()


def layer(*operands):
    vm = pl.BlockSpec(memory_space=pltpu.VMEM)
    dma = pltpu.SemaphoreType.DMA

    def low(*shape):
        return pltpu.VMEM(shape, bf16)

    def full(*shape):
        return pltpu.VMEM(shape, f32)

    sizes = ((48, 1152), (48, 384), (48, 1536), (96, 768))
    weights = (low(2, 4, 4, 48, 1152), low(2, 4, 4, 48, 384), low(2, 4, 4, 48, 1536), low(4, 4, 2, 96, 768))
    return pl.pallas_call(
        layer_kernel,
        in_specs=[vm] * len(operands),
        out_specs=[vm] * 7,
        out_shape=[
            jax.ShapeDtypeStruct((128, 768), bf16),
            jax.ShapeDtypeStruct((128, 768), bf16),
            jax.ShapeDtypeStruct((24, 2304), f32),
            jax.ShapeDtypeStruct((24, 768), f32),
            jax.ShapeDtypeStruct((24, 3072), f32),
            jax.ShapeDtypeStruct((96, 768), f32),
            jax.ShapeDtypeStruct((8, 256), f32),
        ],
        scratch_shapes=[
            full(5, 8, 1024), pltpu.VMEM((1, 1024), jnp.int32), full(48, 3072), full(24, 3072), dma((2,)), dma((4, 17)), dma((4, 11)),
            full(4, 8, 1024), full(7, 8, 1024), dma((7,)), dma((7,)),
            *weights, low(512, 768), dma((3,)), dma((3,)), low(512, 768), low(768, 512), low(128, 768), low(512, 1536), full(16, 640),
            low(12, 128, 512), low(128, 768), full(128, 768), low(128, 768), low(128, 192),
            full(128, 8), full(128, 8), low(2, 4, 48, 768), low(2, 4, 48, 768), dma((2, 3)), dma((2, 3)),
            low(192, 768), low(192, 768), low(4, 192, 768), low(4, 192, 768),
            *weights,
            low(768, 192), full(192, 768), low(2, 4, 48, 768),
            low(512, 1536), low(3, 128, 768), full(16, 640),
            low(4, 48, 384), low(3, 48, 384), low(4, 48, 384),
            *[low(4, 4, *s) for s in sizes[1:]],
            *[low(2, 2, *s) for s in sizes],
            *[low(2, 4, *s) for s in sizes],
            *[low(3, *s) for s in sizes],
            dma((4, 11)), dma((4, 11)), dma((2, 3)), dma((2, 3)), dma((3,)), dma((3,)),
            dma((6,)), dma((6,)), dma((5,)), dma((5,)),
            full(10, 8, 1024), dma((10,)), dma((10,)),
        ],
        compiler_params=pltpu.CompilerParams(
            collective_id=0, has_side_effects=True, vmem_limit_bytes=63 * 2**20
        ),
    )(*operands)


def emit_kernel(
    mixed, d_tokens, qkv, ao, first, second, own,
    o_mixed, o_tokens, o_na, o_qkv, o_ao, o_table, o_nm, o_router, o_first, o_second,
):
    o_mixed[...] = mixed[...]
    o_tokens[...] = d_tokens[...]
    o_qkv[...] = qkv[...]
    o_ao[...] = ao[...]
    o_first[:, 0, :] = first[...]
    o_second[:, 0, :] = second[...]
    o_na[...] = own[0:1, 0:24]
    o_nm[...] = own[1:2, 0:24]
    o_router[...] = own[2:6, 0:24]
    o_table[...] = own[0:1, 128:140]


def emit(*results):
    vm = pl.BlockSpec(memory_space=pltpu.VMEM)
    kinds = (
        ((128, 768), bf16), ((128, 768), bf16), ((1, 24), f32), ((24, 2304), f32), ((24, 768), f32),
        ((1, 12), f32), ((1, 24), f32), ((4, 24), f32), ((24, 1, 3072), f32), ((96, 1, 768), f32),
    )
    return pl.pallas_call(
        emit_kernel,
        in_specs=[vm] * 7,
        out_specs=[vm] * 10,
        out_shape=[jax.ShapeDtypeStruct(shape, kind) for shape, kind in kinds],
    )(*results)


def per_device(
    tokens, norm_attn, w_qkv, w_attn_out, bias_table, norm_moe, router, w_in, w_out, routes, buckets, cotangent
):
    results = layer(
        w_qkv, w_attn_out, w_in[:, 0], w_out[:, 0], norm_attn[None, :], norm_moe[None, :], router.T, bias_table,
        tokens, routes.T, buckets[None, :], cotangent,
    )
    mixed, d_tokens, g_na, g_qkv, g_ao, g_table, g_nm, g_router, g_in, g_out = emit(*results)
    return mixed, d_tokens, g_na[0], g_qkv, g_ao, g_table, g_nm[0], g_router.T, g_in, g_out


def solution(mesh):
    both = ("dp", "expert")
    in_specs = (
        P(both, None), P("dp"), P("dp", None), P("dp", None), P("dp", None), P("dp"), P("dp", None),
        P("dp", "expert", None), P("dp", "expert", None), P(both, None), P(), P(both, None),
    )
    out_specs = (
        P(both, None), P(both, None), P("dp"), P("dp", None), P("dp", None), P("dp", None), P("dp"),
        P("dp", None), P("dp", "expert", None), P("dp", "expert", None),
    )
    return jax.shard_map(
        per_device, mesh=mesh, in_specs=in_specs, out_specs=out_specs, check_vma=False
    )
```

```python
import jax
import jax.numpy as jnp
from jax import lax
from jax.experimental import pallas as pl
from jax.experimental.pallas import tpu as pltpu
from jax.sharding import PartitionSpec as P

epsilon = 1e-06
highest = lax.Precision.HIGHEST
bf16 = jnp.bfloat16
f32 = jnp.float32
NT = (((1,), (1,)), ((), ()))
TN = (((0,), (0,)), ((), ()))


def mm(a, b):
    return jnp.dot(a, b, preferred_element_type=f32)


def mm_nt(a, b):
    return lax.dot_general(a, b, NT, preferred_element_type=f32)


def mm_tn(a, b):
    return lax.dot_general(a, b, TN, preferred_element_type=f32)


def stack_heads(pair):
    left = lax.broadcasted_iota(jnp.int32, pair.shape, 1) < 64
    zero = jnp.zeros_like(pair)
    return jnp.concatenate([jnp.where(left, pair, zero), jnp.where(left, zero, pair)], 0)


def join_pair(stacked):
    rows = stacked.shape[0] // 2
    left = lax.broadcasted_iota(jnp.int32, (rows, 128), 1) < 64
    return jnp.where(left, stacked[:rows], stacked[rows:])


def toeplitz(window_row, rows, keys):
    width = window_row.shape[1]
    wide = jnp.broadcast_to(window_row, (rows, width))
    rolled = pltpu.roll(wide, width - (rows - 1), 1, stride=1, stride_axis=0)
    return rolled[:, :keys]


def diagonal_sums(block, width):
    rows, keys = block.shape
    wide = jnp.concatenate([block, jnp.zeros((rows, width - keys), f32)], 1)
    half = rows // 2
    while half >= 8:
        wide = wide[:half] + pltpu.roll(wide[half:], width - half, 1)
        half //= 2
    row = lax.broadcasted_iota(jnp.int32, wide.shape, 0)
    for bit in (1, 2, 4):
        wide = jnp.where((row & bit) != 0, pltpu.roll(wide, width - bit, 1), wide)
    total = jnp.sum(wide, 0, keepdims=True)
    return pltpu.roll(total, rows - 1, 1)


def rms_forward(values, gain):
    r = lax.rsqrt(jnp.mean(values * values, -1, keepdims=True) + epsilon)
    return r, values * r * gain


def rms_backward(values, r, gain, grad):
    u = grad * gain
    d_values = r * u - values * (r * r * r) * jnp.mean(u * values, -1, keepdims=True)
    return d_values, jnp.sum(grad * values * r, 0)


MESH = pl.DeviceIdType.MESH


class Place:
    def __init__(self):
        d = lax.axis_index("dp")
        self.d = d
        self.x = lax.axis_index("expert")
        self.c = lax.rem(d, 2)
        self.z = lax.rem(lax.div(d, 2), 4)
        self.y = lax.div(d, 8)
        self.p = self.z * (1 - self.c) + self.y * self.c
        self.q = self.y * (1 - self.c) + self.z * self.c

    def at(self, p, q):
        y = q * (1 - self.c) + p * self.c
        z = p * (1 - self.c) + q * self.c
        return ((y * 4 + z) * 2 + self.c, self.x)

    def along_p(self, by):
        return self.at(lax.rem(self.p + by, 4), self.q)

    def along_q(self, by):
        return self.at(self.p, lax.rem(self.q + by, 4))

    def along_x(self, by):
        return (self.d, lax.rem(self.x + by, 4))

    def sibling(self):
        return (self.d + 1 - 2 * self.c, self.x)

    def each_core(self, body):
        pl.when(self.c == 0)(lambda: body(0))
        pl.when(self.c == 1)(lambda: body(1))

    def barrier(self, with_x):
        peers = [self.sibling()] + [self.along_p(i) for i in (1, 2, 3)]
        peers += [self.along_q(i) for i in (1, 2, 3)]
        if with_x:
            peers += [self.along_x(i) for i in (1, 2, 3)]
        sem = pltpu.get_barrier_semaphore()
        for peer in peers:
            pl.semaphore_signal(sem, inc=1, device_id=peer, device_id_type=MESH)
        return lambda: pl.semaphore_wait(sem, len(peers))


def remote(src, dst, send, recv, to):
    return pltpu.make_async_remote_copy(
        src_ref=src, dst_ref=dst, send_sem=send, recv_sem=recv, device_id=to, device_id_type=MESH
    )


def block_of(ref, tall, k, p, q):
    y, z = (q, p) if k == 0 else (p, q)
    return ref.at[y, z, k] if tall else ref.at[k, y, z]


def slab_of(ref, tall, k, q, low=0, count=4):
    y, z = (q, pl.ds(low, count)) if k == 0 else (pl.ds(low, count), q)
    return ref.at[y, z, k] if tall else ref.at[k, y, z]


class Gather:
    sends = 11
    recvs = 11

    def __init__(self, place, ref, tall, send, recv, number):
        self.o, self.ref, self.tall, self.send, self.recv = place, ref, tall, send, recv
        self.number = number

    def block(self, k, by):
        return block_of(self.ref, self.tall, k, lax.rem(self.o.p + by, 4), self.o.q)

    def slab(self, k, by, low=0, count=4):
        return slab_of(self.ref, self.tall, k, lax.rem(self.o.q + by, 4), low, count)

    def go(self, part, s, r, to):
        def body(k):
            src = part(k)
            remote(src, src, self.send.at[s], self.recv.at[r], to).start()

        self.o.each_core(body)

    def arrived(self, r, count):
        if count == 1:
            view = block_of(self.ref, self.tall, 0, 0, 0)
        else:
            view = slab_of(self.ref, self.tall, 0, 0, 0, count)
        remote(view, view, self.send.at[0], self.recv.at[r], self.o.sibling()).wait_recv()

    def sent(self, s, count):
        if count == 1:
            view = block_of(self.ref, self.tall, 0, 0, 0)
        else:
            view = slab_of(self.ref, self.tall, 0, 0, 0, count)
        remote(view, view, self.send.at[s], self.recv.at[0], self.o.sibling()).wait_send()

    def ring_one(self):
        self.go(lambda k: self.block(k, 0), 0, 0, self.o.along_p(1))
        self.go(lambda k: self.block(k, 0), 1, 1, self.o.along_p(3))
        if self.number == 0:
            self.go(lambda k: self.block(k, 0), 2, 2, self.o.along_p(2))

    def ring_one_far(self):
        self.arrived(0, 1)
        self.arrived(1, 1)
        if self.number == 0:
            return
        if self.number % 2 == 0:
            self.go(lambda k: self.block(k, 3), 2, 2, self.o.along_p(1))
        else:
            self.go(lambda k: self.block(k, 1), 2, 2, self.o.along_p(3))

    def ring_two_block(self, by):
        n = 3 if by == 0 else 9 + 2 * by
        self.go(lambda k: self.block(k, by), n, 3, self.o.along_q(1))
        self.go(lambda k: self.block(k, by), 4 if by == 0 else n + 1, 4, self.o.along_q(3))

    def ring_two(self):
        self.arrived(2, 1)
        for by in (1, 2, 3):
            self.ring_two_block(by)
        self.go(lambda k: self.slab(k, 0), 7, 7, self.o.sibling())

    def ring_two_far(self):
        self.arrived(3, 4)
        self.go(lambda k: self.slab(k, 3, 0, 2), 5, 5, self.o.along_q(1))
        self.arrived(4, 4)
        self.go(lambda k: self.slab(k, 1, 2, 2), 6, 6, self.o.along_q(3))
        self.go(lambda k: self.slab(k, 3), 8, 8, self.o.sibling())
        self.go(lambda k: self.slab(k, 1), 9, 9, self.o.sibling())

    def last(self):
        self.arrived(5, 2)
        self.arrived(6, 2)
        self.go(lambda k: self.slab(k, 2), 10, 10, self.o.sibling())

    def finish(self):
        for r in (7, 8, 9, 10):
            self.arrived(r, 4)

    def drain(self):
        for s, count in ((0, 1), (1, 1), (2, 1), (3, 1), (4, 1), (5, 2), (6, 2), (7, 4), (8, 4), (9, 4), (10, 4),
                         *((n, 1) for n in range(11, 17))):
            self.sent(s, count)


class SmallSum:
    def __init__(self, place, value, arrivals, send, recv, with_x):
        self.o, self.value, self.arrivals, self.send, self.recv = place, value, arrivals, send, recv
        o = place
        self.steps = [[o.sibling()], [o.along_p(i) for i in (1, 2, 3)], [o.along_q(i) for i in (1, 2, 3)]]
        if with_x:
            self.steps.append([o.along_x(i) for i in (1, 2, 3)])
        self.copies = []
        n = 0
        for s, peers in enumerate(self.steps):
            row = []
            for peer in peers:
                row.append(
                    remote(value.at[s], arrivals.at[n], send.at[n], recv.at[n], peer)
                )
                n += 1
            self.copies.append(row)

    def start(self, s):
        for copy in self.copies[s]:
            copy.start()

    def add(self, s):
        first = sum(len(row) for row in self.copies[:s])
        total = self.value[s]
        for i, copy in enumerate(self.copies[s]):
            copy.wait_recv()
            total = total + self.arrivals[first + i]
        self.value[s + 1] = total

    def drain(self):
        for row in self.copies:
            for copy in row:
                copy.wait_send()


def place_small(o, out, na, nm, router_t, table):
    row = lax.broadcasted_iota(jnp.int32, (24, 768), 0)
    lane = lax.broadcasted_iota(jnp.int32, (24, 768), 1)
    hit = jnp.where(lane == 24 * o.d + row, 1.0, 0.0)
    out[...] = jnp.zeros((8, 1024), f32)
    out[0:1, 0:768] = mm(na[...].astype(f32), hit)
    out[1:2, 0:768] = mm(nm[...].astype(f32), hit)
    out[2:6, 0:768] = mm(router_t[...].astype(f32), hit)
    head = lax.broadcasted_iota(jnp.int32, (16, 12), 0) == lax.broadcasted_iota(jnp.int32, (16, 12), 1)
    wide = jnp.broadcast_to(table[...].astype(f32), (16, 12))
    column = jnp.sum(jnp.where(head, wide, 0.0), -1, keepdims=True)
    own = lax.broadcasted_iota(jnp.int32, (16, 128), 1) == o.d
    placed = jnp.where(own, jnp.broadcast_to(column, (16, 128)), 0.0)
    out[:, 768:896] = placed[0:8]
    out[:, 896:1024] = placed[8:16]


def meet(o, halves, stage, other, sem):
    at = 0
    for ref, blocks in halves:
        n = ref.shape[1] // (2 * blocks)
        for t in range(blocks):
            own = pl.ds(pl.multiple_of(o.c * n + 2 * t * n, 128), n)
            theirs = pl.ds(pl.multiple_of((1 - o.c) * n + 2 * t * n, 128), n)
            stage[pl.ds(pl.multiple_of(24 * o.c, 8), 24), at : at + n] = ref[:, own].astype(f32)
            other[:, at : at + n] = ref[:, theirs].astype(f32)
            at += n
    return remote(
        other, stage.at[pl.ds(pl.multiple_of(24 * o.c, 8), 24)], sem.at[0], sem.at[1], o.sibling()
    )


class Scatter:
    def __init__(self, place, ref, tall, pair, far, near, side, send, recv):
        self.o, self.ref, self.tall = place, ref, tall
        self.pair, self.far, self.near, self.side = pair, far, near, side
        self.send, self.recv = send, recv

    def where(self, p, q):
        o = self.o
        return q * (1 - o.c) + p * o.c, p * (1 - o.c) + q * o.c

    def q_at(self, by):
        return lax.rem(self.o.q + by, 4)

    def own(self, p, q):
        y, z = self.where(p, q)
        return (y, z, self.o.c) if self.tall else (self.o.c, y, z)

    def to_pair(self, s, low, count):
        rows = pl.ds(low, count)
        theirs = 1 - self.o.c
        src = self.ref.at[rows, :, theirs] if self.tall else self.ref.at[theirs, rows]
        remote(src, self.pair.at[rows], self.send.at[s], self.recv.at[s], self.o.sibling()).start()

    def from_pair(self, s, count):
        view = self.pair.at[pl.ds(0, count)]
        remote(view, view, self.send.at[s], self.recv.at[s], self.o.sibling()).wait_recv()

    def add_pair(self, by):
        q = self.q_at(by)

        def body(p, carry):
            y, z = self.where(p, q)
            at = self.own(p, q)
            self.ref[at] = (self.ref[at].astype(f32) + self.pair[y, z].astype(f32)).astype(bf16)
            return carry

        lax.fori_loop(0, 4, body, 0)

    def go(self, s, by, low, dst, to):
        def body(k):
            src = slab_of(self.ref, self.tall, k, self.q_at(by), low, 2)
            remote(src, dst, self.send.at[s], self.recv.at[s], to).start()

        self.o.each_core(body)

    def ring(self):
        o = self.o
        self.add_pair(2)
        self.go(2, 2, 0, self.far.at[0], o.along_q(1))
        self.go(3, 2, 2, self.far.at[1], o.along_q(3))
        self.add_pair(1)
        self.go(4, 1, 2, self.near.at[0, pl.ds(2, 2)], o.along_q(1))
        self.add_pair(3)
        self.go(5, 3, 0, self.near.at[1, pl.ds(0, 2)], o.along_q(3))
        self.add_pair(0)

    def landed(self, s, view):
        remote(view, view, self.send.at[s], self.recv.at[s], self.o.sibling()).wait_recv()

    def add_far(self, i, by, low):
        q = self.q_at(by)

        def body(j, carry):
            at = self.own(low + j, q)
            self.ref[at] = (self.ref[at].astype(f32) + self.far[i, j].astype(f32)).astype(bf16)
            return carry

        lax.fori_loop(0, 2, body, 0)

    def ring_far(self):
        o = self.o
        self.landed(2, self.far.at[0])
        self.add_far(0, 1, 0)
        self.go(6, 1, 0, self.near.at[0, pl.ds(0, 2)], o.along_q(1))
        self.landed(3, self.far.at[1])
        self.add_far(1, 3, 2)
        self.go(7, 3, 2, self.near.at[1, pl.ds(2, 2)], o.along_q(3))

    def across(self):
        o = self.o
        half = self.near.at[0, pl.ds(0, 2)]
        for s in (4, 5, 6, 7):
            self.landed(s, half)

        def body(p, carry):
            at = self.own(p, o.q)
            total = self.ref[at].astype(f32) + self.near[0, p].astype(f32)
            self.ref[at] = (total + self.near[1, p].astype(f32)).astype(bf16)
            return carry

        lax.fori_loop(0, 4, body, 0)
        for i in (1, 2, 3):
            src = self.ref.at[self.own(lax.rem(o.p + i, 4), o.q)]
            remote(
                src, self.side.at[i - 1], self.send.at[7 + i], self.recv.at[7 + i], o.along_p(i)
            ).start()

    def total(self):
        o = self.o
        for i in (0, 1, 2):
            self.landed(8 + i, self.side.at[i])
        total = self.ref[self.own(o.p, o.q)].astype(f32)
        for i in (0, 1, 2):
            total = total + self.side[i].astype(f32)
        return total

    def sent(self, s, view):
        remote(view, view, self.send.at[s], self.recv.at[s], self.o.sibling()).wait_send()

    def drain(self, pair_parts):
        for s, count in pair_parts:
            self.sent(s, self.pair.at[pl.ds(0, count)])
        for s in range(2, 8):
            self.sent(s, self.far.at[0])
        for s in range(8, 11):
            self.sent(s, self.side.at[0])


SQ = 0.7978845608028654


def gelu_both(h):
    t = jnp.tanh(SQ * (h + 0.044715 * (h * h * h)))
    value = 0.5 * h * (1.0 + t)
    slope = 0.5 * (1.0 + t) + 0.5 * h * (1.0 - t * t) * (SQ * (1.0 + 3 * 0.044715 * (h * h)))
    return value, slope


def hidden_lanes(j):
    return lax.div(j, 2), pl.ds(pl.multiple_of(lax.rem(j, 2) * 768, 128), 768)


def expert_hidden(j, sent, g_in, acts, slopes):
    half, at = hidden_lanes(j)
    value, slope = gelu_both(mm(sent[...], g_in[half, :, :, :, at].reshape(768, 768)))
    acts[j] = value.astype(bf16)
    slopes[j] = slope.astype(bf16)


def expert_second_grad(j, d_result, acts, h_out):
    for r in (0, 1):
        part = acts[j, :, r * 384 : (r + 1) * 384]
        h_out[j, pl.ds(2 * r, 2)] = mm_tn(part, d_result[...]).astype(bf16).reshape(2, 2, 96, 768)


def expert_result(j, acts, g_out, result):
    result[...] += mm(acts[j], g_out[j].reshape(768, 768))


def expert_back(j, sent_t, d_result, slopes, g_in, g_out, h_in, d_incoming):
    half, at = hidden_lanes(j)
    d_act = mm_nt(d_result[...], g_out[j].reshape(768, 768))
    d_hidden = (d_act * slopes[j].astype(f32)).astype(bf16)
    for r in (0, 1):
        part = sent_t[r * 384 : (r + 1) * 384]
        h_in[half, pl.ds(2 * r, 2), :, :, at] = mm(part, d_hidden).astype(bf16).reshape(2, 4, 48, 768)
    d_incoming[...] += mm_nt(d_hidden, g_in[half, :, :, :, at].reshape(768, 768))


def pair_backward(i, query, kv, weights, d_heads, d_query, d_kv, d_window):
    lanes = pl.ds(pl.multiple_of(i * 128, 128), 128)
    value_lanes = pl.ds(pl.multiple_of(i * 128 + 768, 128), 128)
    kept = weights[pl.ds(2 * i, 2)].reshape(256, 512)
    probability = kept.astype(f32)
    d_stack = stack_heads(d_heads[:, lanes])
    d_weights = mm_nt(d_stack, kv[:, value_lanes])
    d_kv[:, value_lanes] = mm_tn(kept, d_stack).astype(bf16)
    d_scores = probability * (d_weights - jnp.sum(probability * d_weights, -1, keepdims=True))
    low = d_scores.astype(bf16)
    d_kv[:, lanes] = mm_tn(low, stack_heads(query[:, lanes])).astype(bf16)
    d_query[:, lanes] = join_pair(mm(low, kv[:, lanes])).astype(bf16)
    for j in (0, 1):
        d_window[pl.ds(2 * i + j, 1), :] = diagonal_sums(d_scores[j * 128 : (j + 1) * 128], 640)


def pair_forward(i, query, kv, window, heads_out, weights):
    lanes = pl.ds(pl.multiple_of(i * 128, 128), 128)
    value_lanes = pl.ds(pl.multiple_of(i * 128 + 768, 128), 128)
    bias = jnp.concatenate([toeplitz(window[pl.ds(2 * i + j, 1), :], 128, 512) for j in (0, 1)], 0)
    scores = mm_nt(stack_heads(query[:, lanes]), kv[:, lanes]) + bias
    top = jnp.max(scores, -1, keepdims=True)
    raised = jnp.exp(scores - top)
    probability = raised / jnp.sum(raised, -1, keepdims=True)
    low = probability.astype(bf16)
    weights[pl.ds(2 * i, 2)] = low.reshape(2, 128, 512)
    heads_out[:, lanes] = join_pair(mm(low, kv[:, value_lanes])).astype(bf16)


def layer_kernel(
    w_qkv, w_ao, w_in, w_out, na, nm, router_t, table, tokens, routes, bucket_list, cotangent,
    mixed, d_tokens, out_qkv, out_ao, out_in, out_out, own_small,
    small, buckets, stage, other, pair_sem, g_sends, g_recvs, side_in, side_arrivals, side_send, side_recv,
    g_qkv, g_ao, g_in, g_out, whole_tokens, tok_send, tok_recv, normed_ref, normed_t, query, kv, window, weights, heads_out,
    after_attn, moe_input, placing, probs, chosen, disp, inc, disp_send, disp_recv, sent, d_result, acts, slopes,
    h_qkv, h_ao, h_in, h_out, sent_t, result, back, d_kv, dn_in, d_window,
    xs, xr, xa,
    pair_a, pair_i, pair_o, far_q, far_a, far_i, far_o, near_q, near_a, near_i, near_o,
    side_q, side_a, side_i, side_o,
    sends, recvs, ret_send, ret_recv, dn_send, dn_recv, x_send, x_recv, last_send, last_recv,
    arrivals, small_send, small_recv,
):
    d_heads_ref, d_after_ref, d_query = heads_out, after_attn, query
    o = Place()
    entered = o.barrier(True)
    flows = [
        Gather(o, ref, tall, g_sends.at[i], g_recvs.at[i], i)
        for i, (ref, tall) in enumerate(((g_qkv, 0), (g_ao, 0), (g_in, 0), (g_out, 1)))
    ]
    qkv, ao, win, wout = flows
    pair_copy = meet(o, ((w_qkv, 3), (w_ao, 1), (w_in, 1)), stage, other, pair_sem)
    side = SmallSum(o, side_in, side_arrivals, side_send, side_recv, False)
    place_small(o, side_in.at[0], na, nm, router_t, table)
    buckets[...] = jnp.zeros_like(buckets)
    buckets[:, 0:1023] = bucket_list[...]
    g_out[o.y, o.z, o.c] = w_out[...]
    own_rows = pl.ds(pl.multiple_of(o.x * 128, 128), 128)
    whole_tokens[own_rows] = tokens[...]
    entered()
    pair_copy.start()
    side.start(0)
    wout.ring_one()
    wout.ring_two_block(0)
    pair_copy.wait_recv()
    at = 0
    for ref in (g_qkv, g_ao, g_in):
        n = ref.shape[-1]
        ref[o.c, o.y, o.z] = stage[:, at : at + n].astype(bf16)
        at += n
    qkv.ring_one()
    qkv.ring_two_block(0)
    side.add(0)
    side.start(1)
    tok_copies = [
        remote(
            whole_tokens.at[own_rows], whole_tokens.at[own_rows], tok_send.at[by - 1], tok_recv.at[by - 1],
            o.along_x(by),
        )
        for by in (1, 2, 3)
    ]
    for copy in tok_copies:
        copy.start()
    win.ring_one()
    ao.ring_one()
    ao.ring_two_block(0)
    win.ring_two_block(0)
    qkv.ring_one_far()
    qkv.ring_two()
    side.add(1)
    side.start(2)
    x = tokens[...].astype(f32)
    bucket_row = buckets[:, pl.ds(pl.multiple_of((3 - o.x) * 128, 128), 640)]
    picks = jnp.where(
        jnp.broadcast_to(bucket_row, (128, 640)) == lax.broadcasted_iota(jnp.int32, (128, 640), 0), 1.0, 0.0
    )
    for f in (wout, win, ao):
        f.ring_one_far()
    ao.ring_two()
    win.ring_two()
    qkv.ring_two_far()
    wout.ring_two()
    for copy in tok_copies:
        copy.wait_recv()
    side.add(2)
    small_in = side_in.at[3]
    gain_row = small_in[0:1, :768]

    def norm_rows(n, carry):
        rows = pl.ds(n * 128, 128)
        _, normed = rms_forward(whole_tokens[rows].astype(f32), gain_row)
        normed_ref[rows] = normed.astype(bf16)
        normed_t[:, rows] = normed.T.astype(bf16)
        return carry

    for n in range(4):
        norm_rows(n, 0)
    table_t = jnp.concatenate([small_in[:, 768:896], small_in[:, 896:1024]], 0)
    window[...] = mm(table_t.astype(bf16), picks.astype(bf16))
    qkv.last()
    ao.ring_two_far()
    qkv.finish()

    for h in (0, 1):
        query[:, 384 * h : 384 * h + 384] = mm(
            normed_ref[own_rows], g_qkv[h, :, :, :, 0:384].reshape(768, 384)
        ).astype(bf16)

    def project_rows(n, carry):
        rows = pl.ds(pl.multiple_of(n * 128, 128), 128)
        for h in (0, 1):
            both = mm(normed_ref[rows], g_qkv[h, :, :, :, 384:1152].reshape(768, 768)).astype(bf16)
            kv[rows, 384 * h : 384 * h + 384] = both[:, :384]
            kv[rows, 768 + 384 * h : 1152 + 384 * h] = both[:, 384:]
        return carry

    lax.fori_loop(0, 4, project_rows, 0)
    ao.last()

    def ahead(i, carry):
        pair_forward(i, query, kv, window, heads_out, weights)
        return carry

    lax.fori_loop(0, 3, ahead, 0)
    win.ring_two_far()
    lax.fori_loop(3, 6, ahead, 0)
    ao.finish()
    mixed_heads = heads_out[...]
    attn = x + jnp.concatenate([mm(mixed_heads, g_ao[h].reshape(768, 384)) for h in (0, 1)], 1)
    after_attn[...] = attn
    small8 = small_in[:, :768]
    r_two = lax.rsqrt(jnp.mean(attn * attn, -1, keepdims=True) + epsilon)
    moe_low = (attn * r_two * small8[1:2]).astype(bf16)
    moe_input[...] = moe_low
    logits = mm_nt(moe_low, small8.astype(bf16))
    lane = lax.broadcasted_iota(jnp.int32, (128, 8), 1)
    logits = jnp.where((lane >= 2) & (lane < 6), logits, -1e30)
    raised = jnp.exp(logits - jnp.max(logits, -1, keepdims=True))
    probability = raised / jnp.sum(raised, -1, keepdims=True)
    probs[...] = probability
    named = jnp.broadcast_to(routes[...], (8, 128)) + 2
    picked = jnp.where(lax.broadcasted_iota(jnp.int32, (8, 128), 0) == named, 1.0, 0.0).T
    chosen[...] = picked
    gate = jnp.sum(probability * picked, -1, keepdims=True)
    before = jnp.where(
        lax.broadcasted_iota(jnp.int32, (128, 128), 1) < lax.broadcasted_iota(jnp.int32, (128, 128), 0), 1.0, 0.0
    )
    slot = jnp.sum(mm(before.astype(bf16), picked.astype(bf16)) * picked, -1, keepdims=True)
    column = jnp.sum(picked * ((lane - 2) * 48).astype(f32), -1, keepdims=True) + slot
    place = jnp.where(
        lax.broadcasted_iota(jnp.int32, (128, 192), 1).astype(f32) == column, 1.0, 0.0
    ).astype(bf16)
    placing[...] = place
    def dispatch(part, value):
        disp[part] = mm_tn(place, value).astype(bf16).reshape(4, 48, 768)
        copies = [
            remote(
                disp.at[part, lax.rem(o.x + by, 4)], inc.at[part, o.x],
                disp_send.at[part, by - 1], disp_recv.at[part, by - 1], o.along_x(by),
            )
            for by in (1, 2, 3)
        ]
        for copy in copies:
            copy.start()
        inc[part, o.x] = disp[part, o.x]
        return copies

    tokens_out = dispatch(0, moe_low)
    grads_out = dispatch(1, (gate * cotangent[...].astype(f32)).astype(bf16))
    win.last()
    wout.ring_two_far()
    for copy in tokens_out:
        copy.wait_recv()
    sent[...] = inc[0].reshape(192, 768)
    sent_t[...] = sent[...].astype(f32).T.astype(bf16)
    win.finish()
    pair_q = pair_i.at[:, :, :, pl.ds(0, 1152)]
    fq = Scatter(o, h_qkv, 0, pair_q, far_q, near_q, side_q, sends.at[0], recvs.at[0])
    fa = Scatter(o, h_ao, 0, pair_a, far_a, near_a, side_a, sends.at[1], recvs.at[1])
    fi = Scatter(o, h_in, 0, pair_i, far_i, near_i, side_i, sends.at[2], recvs.at[2])
    fo = Scatter(o, h_out, 1, pair_o, far_o, near_o, side_o, sends.at[3], recvs.at[3])
    tot = SmallSum(o, small, arrivals, small_send, small_recv, True)

    def times(low, high, body):
        def step(j, carry):
            body(j)
            return carry

        lax.fori_loop(low, high, step, 0)

    times(0, 4, lambda j: expert_hidden(j, sent, g_in, acts, slopes))
    wout.last()
    for copy in grads_out:
        copy.wait_recv()
    d_result[...] = inc[1].reshape(192, 768)
    times(0, 4, lambda j: expert_second_grad(j, d_result, acts, h_out))
    fo.to_pair(0, 0, 4)
    wout.finish()
    result[...] = jnp.zeros_like(result)
    times(0, 4, lambda j: expert_result(j, acts, g_out, result))

    def send_back(part, value):
        for copy in (tokens_out, grads_out)[part]:
            copy.wait_send()
        ret = disp
        ret[part] = value.astype(bf16).reshape(4, 48, 768)
        copies = [
            remote(
                ret.at[part, lax.rem(o.x + by, 4)], back.at[part, o.x],
                ret_send.at[part, by - 1], ret_recv.at[part, by - 1], o.along_x(by),
            )
            for by in (1, 2, 3)
        ]
        for copy in copies:
            copy.start()
        back[part, o.x] = ret[part, o.x]
        return copies

    results_back = send_back(0, result[...])
    d_incoming = result
    d_incoming[...] = jnp.zeros_like(d_incoming)
    start = 2 * (1 - o.c)

    def back_chunk(j):
        expert_back(j, sent_t, d_result, slopes, g_in, g_out, h_in, d_incoming)

    times(start, start + 2, back_chunk)
    fi.to_pair(0, 0, 4)
    fo.from_pair(0, 4)
    fo.ring()
    times(2 - start, 4 - start, back_chunk)
    grads_back = send_back(1, d_incoming[...])
    fi.from_pair(0, 4)
    fi.ring()
    fo.ring_far()
    for copy in results_back + grads_back:
        copy.wait_recv()

    gain_one, gain_two = small8[0:1], small8[1:2]
    returned = mm(placing[...], back[0].reshape(192, 768))
    d_moe = mm(placing[...], back[1].reshape(192, 768))
    attn = after_attn[...]
    r_two = lax.rsqrt(jnp.mean(attn * attn, -1, keepdims=True) + epsilon)
    upstream = cotangent[...].astype(f32)
    gate = jnp.sum(probs[...] * chosen[...], -1, keepdims=True)
    mixed[...] = (attn + gate * returned).astype(bf16)
    d_gate = jnp.sum(upstream * returned, -1, keepdims=True)
    d_logits = probs[...] * (d_gate * chosen[...] - d_gate * gate)
    d_moe = d_moe + jnp.dot(d_logits, small8, precision=highest, preferred_element_type=f32)
    grad_router = lax.dot_general(
        d_logits, moe_input[...].astype(f32), TN, precision=highest, preferred_element_type=f32
    )
    d_after, grad_norm_two = rms_backward(attn, r_two, gain_two, d_moe)
    d_after = d_after + upstream
    d_after_ref[...] = d_after
    d_attn = d_after.astype(bf16)
    d_heads = jnp.zeros((128, 768), f32)
    for h in (0, 1):
        part = d_attn[:, h * 384 : (h + 1) * 384]
        h_ao[h] = mm_tn(heads_out[...], part).astype(bf16).reshape(4, 4, 48, 384)
        d_heads = d_heads + mm_nt(part, g_ao[h].reshape(768, 384))
    fa.to_pair(0, 0, 4)
    d_heads_ref[...] = d_heads.astype(bf16)

    d_window[...] = jnp.zeros_like(d_window)

    def pair(i):
        pair_backward(i, query, kv, weights, d_heads_ref, d_query, d_kv, d_window)

    def lanes_of(h, base):
        return pl.ds(pl.multiple_of(h * 384 + base, 128), 384)

    def dense_grad(h):
        for t, part in enumerate(
            (
                mm(normed_t[:, own_rows], d_query[:, lanes_of(h, 0)]),
                mm(normed_t[...], d_kv[:, lanes_of(h, 0)]),
                mm(normed_t[...], d_kv[:, lanes_of(h, 768)]),
            )
        ):
            h_qkv[h, :, :, :, t * 384 : t * 384 + 384] = part.astype(bf16).reshape(4, 4, 48, 384)

    theirs = 1 - o.c
    times(3 * theirs, 3 * theirs + 3, pair)
    dense_grad(theirs)
    fa.from_pair(0, 4)
    fq.to_pair(0, 0, 4)
    fa.ring()
    fi.ring_far()
    fo.across()
    times(3 * o.c, 3 * o.c + 3, pair)
    dense_grad(o.c)
    fa.ring_far()
    fq.from_pair(0, 4)
    fq.ring()
    fi.across()
    fa.across()
    grad_table = lax.dot_general(
        d_window[...], picks, NT, precision=highest, preferred_element_type=f32
    )
    result[0:8] = jnp.zeros((8, 768), f32)
    dn = acts.at[:, pl.ds(0, 128), :]

    for n in range(4):
        rows = pl.ds(n * 128, 128)
        part = jnp.zeros((128, 768), f32)
        for h in (0, 1):
            part = part + mm_nt(
                d_kv[rows, 384 * h : 384 * h + 384], g_qkv[h, :, :, :, 384:768].reshape(768, 384)
            )
            part = part + mm_nt(
                d_kv[rows, 768 + 384 * h : 1152 + 384 * h], g_qkv[h, :, :, :, 768:1152].reshape(768, 384)
            )
        dn[n] = part.astype(bf16)
        block = whole_tokens[rows].astype(f32)
        r = lax.rsqrt(jnp.mean(block * block, -1, keepdims=True) + epsilon)
        result[0:1] += jnp.sum(part * block * r, 0, keepdims=True)

    dn_copies = [
        remote(dn.at[lax.rem(o.x + by, 4)], dn_in.at[by - 1], dn_send.at[by - 1], dn_recv.at[by - 1], o.along_x(by))
        for by in (1, 2, 3)
    ]
    for copy in dn_copies:
        copy.start()
    d_own = jnp.zeros((128, 768), f32)
    for h in (0, 1):
        d_own = d_own + mm_nt(
            d_query[:, 384 * h : 384 * h + 384], g_qkv[h, :, :, :, 0:384].reshape(768, 384)
        )
    r_one = lax.rsqrt(jnp.mean(x * x, -1, keepdims=True) + epsilon)
    grad_norm_one = result[0:1] + jnp.sum(d_own * x * r_one, 0, keepdims=True)
    row = lax.broadcasted_iota(jnp.int32, (8, 768), 0)
    top = jnp.where(row == 0, grad_norm_one, jnp.where(row == 1, grad_norm_two[None, :], grad_router))
    small[0] = jnp.concatenate([top, grad_table[0:8], grad_table[8:16]], 1)
    tot.start(0)
    fq.ring_far()
    tot.add(0)
    tot.start(1)
    total_q, total_a, total_i = (stage.at[:, pl.ds(a, n)] for a, n in ((0, 1152), (1152, 384), (1536, 1536)))
    out_out[...] = fo.total()

    def hand(k, total, out, value, blocks):
        total[...] = value
        n = value.shape[1] // blocks
        copies = []
        for t in range(blocks):
            mine = pl.ds(pl.multiple_of(o.c * n + 2 * t * n, 128), n)
            out[:, mine] = total[pl.ds(pl.multiple_of(24 * o.c, 8), 24), t * n : t * n + n]
            copies.append(
                remote(
                    total.at[pl.ds(pl.multiple_of(24 * (1 - o.c), 8), 24), pl.ds(t * n, n)], out.at[:, mine],
                    last_send.at[k + t], last_recv.at[k + t], o.sibling(),
                )
            )
            copies[-1].start()
        return copies

    last = hand(0, total_i, out_in, fi.total(), 1)
    total_a[...] = fa.total()
    tot.add(1)
    tot.start(2)
    fq.across()
    for copy in dn_copies:
        copy.wait_recv()
    d_normed = d_own + dn[o.x].astype(f32)
    for by in (0, 1, 2):
        d_normed = d_normed + dn_in[by].astype(f32)
    d_resid, _ = rms_backward(x, r_one, gain_one, d_normed)
    d_tokens[...] = (d_after_ref[...] + d_resid).astype(bf16)
    tot.add(2)
    tot.start(3)
    dense = jnp.concatenate([fq.total(), total_a[...]], 1).astype(bf16)
    for j in range(4):
        xs[j] = dense[:, j * 384 : (j + 1) * 384]
    first = [
        remote(xs.at[lax.rem(o.x + by, 4)], xr.at[by - 1], x_send.at[by - 1], x_recv.at[by - 1], o.along_x(by))
        for by in (1, 2, 3)
    ]
    for copy in first:
        copy.start()
    for copy in first:
        copy.wait_recv()
    own = xs[o.x].astype(f32)
    for j in range(3):
        own = own + xr[j].astype(f32)
    xa[o.x] = own.astype(bf16)
    second = [
        remote(xa.at[o.x], xa.at[o.x], x_send.at[by + 2], x_recv.at[by + 2], o.along_x(by)) for by in (1, 2, 3)
    ]
    for copy in second:
        copy.start()
    for copy in second:
        copy.wait_recv()
    whole = jnp.concatenate([xa[0], xa[1], xa[2], xa[3]], 1).astype(f32)
    last += hand(1, total_q, out_qkv, whole[:, :1152], 3)
    last += hand(4, total_a, out_ao, whole[:, 1152:], 1)
    tot.add(3)
    take = lax.broadcasted_iota(jnp.int32, (768, 128), 0) == lax.broadcasted_iota(jnp.int32, (768, 128), 1) + 24 * o.d
    own_small[:, 0:128] = jnp.dot(
        small[4, :, 0:768], jnp.where(take, 1.0, 0.0), precision=highest, preferred_element_type=f32
    )
    heads_of = jnp.concatenate([small[4, :, 768:896], small[4, :, 896:1024]], 0)
    mine = jnp.where(lax.broadcasted_iota(jnp.int32, (16, 128), 1) == o.d, heads_of, 0.0)
    column = jnp.broadcast_to(jnp.sum(mine, -1, keepdims=True), (16, 128))
    same = lax.broadcasted_iota(jnp.int32, (16, 128), 0) == lax.broadcasted_iota(jnp.int32, (16, 128), 1)
    own_small[0:1, 128:256] = jnp.sum(jnp.where(same, column, 0.0), 0, keepdims=True)
    for copy in last:
        copy.wait_recv()
    for copy in results_back + grads_back + dn_copies + tok_copies + first + second + last:
        copy.wait_send()
    tot.drain()
    for f in (fq, fa, fi, fo):
        f.drain([(0, 4)])
    pair_copy.wait_send()
    side.drain()
    for f in flows:
        f.drain()


def layer(*operands):
    vm = pl.BlockSpec(memory_space=pltpu.VMEM)
    dma = pltpu.SemaphoreType.DMA

    def low(*shape):
        return pltpu.VMEM(shape, bf16)

    def full(*shape):
        return pltpu.VMEM(shape, f32)

    sizes = ((48, 1152), (48, 384), (48, 1536), (96, 768))
    weights = (low(2, 4, 4, 48, 1152), low(2, 4, 4, 48, 384), low(2, 4, 4, 48, 1536), low(4, 4, 2, 96, 768))
    return pl.pallas_call(
        layer_kernel,
        in_specs=[vm] * len(operands),
        out_specs=[vm] * 7,
        out_shape=[
            jax.ShapeDtypeStruct((128, 768), bf16),
            jax.ShapeDtypeStruct((128, 768), bf16),
            jax.ShapeDtypeStruct((24, 2304), f32),
            jax.ShapeDtypeStruct((24, 768), f32),
            jax.ShapeDtypeStruct((24, 3072), f32),
            jax.ShapeDtypeStruct((96, 768), f32),
            jax.ShapeDtypeStruct((8, 256), f32),
        ],
        scratch_shapes=[
            full(5, 8, 1024), pltpu.VMEM((1, 1024), jnp.int32), full(48, 3072), full(24, 3072), dma((2,)), dma((4, 17)), dma((4, 11)),
            full(4, 8, 1024), full(7, 8, 1024), dma((7,)), dma((7,)),
            *weights, low(512, 768), dma((3,)), dma((3,)), low(512, 768), low(768, 512), low(128, 768), low(512, 1536), full(16, 640),
            low(12, 128, 512), low(128, 768), full(128, 768), low(128, 768), low(128, 192),
            full(128, 8), full(128, 8), low(2, 4, 48, 768), low(2, 4, 48, 768), dma((2, 3)), dma((2, 3)),
            low(192, 768), low(192, 768), low(4, 192, 768), low(4, 192, 768),
            *weights,
            low(768, 192), full(192, 768), low(2, 4, 48, 768),
            low(512, 1536), low(3, 128, 768), full(16, 640),
            low(4, 48, 384), low(3, 48, 384), low(4, 48, 384),
            *[low(4, 4, *s) for s in sizes[1:]],
            *[low(2, 2, *s) for s in sizes],
            *[low(2, 4, *s) for s in sizes],
            *[low(3, *s) for s in sizes],
            dma((4, 11)), dma((4, 11)), dma((2, 3)), dma((2, 3)), dma((3,)), dma((3,)),
            dma((6,)), dma((6,)), dma((5,)), dma((5,)),
            full(10, 8, 1024), dma((10,)), dma((10,)),
        ],
        compiler_params=pltpu.CompilerParams(
            collective_id=0, has_side_effects=True, vmem_limit_bytes=63 * 2**20
        ),
    )(*operands)


def emit_kernel(
    mixed, d_tokens, qkv, ao, first, second, own,
    o_mixed, o_tokens, o_na, o_qkv, o_ao, o_table, o_nm, o_router, o_first, o_second,
):
    o_mixed[...] = mixed[...]
    o_tokens[...] = d_tokens[...]
    o_qkv[...] = qkv[...]
    o_ao[...] = ao[...]
    o_first[:, 0, :] = first[...]
    o_second[:, 0, :] = second[...]
    o_na[...] = own[0:1, 0:24]
    o_nm[...] = own[1:2, 0:24]
    o_router[...] = own[2:6, 0:24]
    o_table[...] = own[0:1, 128:140]


def emit(*results):
    vm = pl.BlockSpec(memory_space=pltpu.VMEM)
    kinds = (
        ((128, 768), bf16), ((128, 768), bf16), ((1, 24), f32), ((24, 2304), f32), ((24, 768), f32),
        ((1, 12), f32), ((1, 24), f32), ((4, 24), f32), ((24, 1, 3072), f32), ((96, 1, 768), f32),
    )
    return pl.pallas_call(
        emit_kernel,
        in_specs=[vm] * 7,
        out_specs=[vm] * 10,
        out_shape=[jax.ShapeDtypeStruct(shape, kind) for shape, kind in kinds],
    )(*results)


def per_device(
    tokens, norm_attn, w_qkv, w_attn_out, bias_table, norm_moe, router, w_in, w_out, routes, buckets, cotangent
):
    results = layer(
        w_qkv, w_attn_out, w_in[:, 0], w_out[:, 0], norm_attn[None, :], norm_moe[None, :], router.T, bias_table,
        tokens, routes.T, buckets[None, :], cotangent,
    )
    mixed, d_tokens, g_na, g_qkv, g_ao, g_table, g_nm, g_router, g_in, g_out = emit(*results)
    return mixed, d_tokens, g_na[0], g_qkv, g_ao, g_table, g_nm[0], g_router.T, g_in, g_out


def solution(mesh):
    both = ("dp", "expert")
    in_specs = (
        P(both, None), P("dp"), P("dp", None), P("dp", None), P("dp", None), P("dp"), P("dp", None),
        P("dp", "expert", None), P("dp", "expert", None), P(both, None), P(), P(both, None),
    )
    out_specs = (
        P(both, None), P(both, None), P("dp"), P("dp", None), P("dp", None), P("dp", None), P("dp"),
        P("dp", None), P("dp", "expert", None), P("dp", "expert", None),
    )
    return jax.shard_map(
        per_device, mesh=mesh, in_specs=in_specs, out_specs=out_specs, check_vma=False
    )
```
